32 devices in a mesh: space: 8 (over z, x), rep: 4 (over y, core).
Axes of the slice: x: 2, y: 2, z: 4, core: 2. Of those that a mesh axis runs over, the one named last changes fastest.
Arguments:
- feats: bfloat16 [4, 32, 64, 512], P('rep', 'space'), may hold values from -6 to 6
- cotangent: bfloat16 [4, 32, 64, 512], P('rep', 'space'), may hold values from -6 to 6
- weight: bfloat16 [27, 64, 64], replicated, may hold values from -0.15625 to 0.15625
- bias: float32 [64], replicated, may hold values from -3 to 3
- neighbours: int32 [4, 32, 26], P('rep', 'space'), may hold values from -1 to 31, as said below
- occupancy: int32 [4, 32, 512], P('rep', 'space'), may hold values from 0 to 1, as said below
Outputs:
- out_feats: bfloat16 [4, 32, 64, 512], P('rep', 'space')
- in_grad: bfloat16 [4, 32, 64, 512], P('rep', 'space')
- weight_grad: float32 [27, 64, 64], replicated
- bias_grad: float32 [64], replicated
The draws below stay inside these ranges and needn't reach their ends.
Inputs may be any that keep to these rules, and one draw needn't show every extreme that they name: Slot s of a district lies on space index s // 4. On each space index the live bricks fill the first slots; a live brick has at least one occupied voxel and a dead slot none. A brick of a district lies in the slab of its space index at one of 8 x 8 positions; neighbours[s, j] is the slot of the live brick adjacent in direction j, which lies on space index s // 4 + dx; dead slots list only -1, and the lists are symmetric. In every district some space index holds 4 live bricks. `occupancy`: dead slots are all zero.
All inputs are finite; a program needn't handle non-finite values.
Results may differ from the reference program's by a relative error of at most 0.0085.
Values may be sent and summed in bfloat16 or wider, within the bound.
No kernel may reach another device: no remote copies, remote signals or barrier semaphores. Data moves between devices by JAX's collectives and lax.ppermute only.
A program may use at most 128 MiB of HBM per device.

```python
import math
import jax
import jax.numpy as jnp
from jax import lax

C = 64
B_DEV = 4
GRID = 8
BRICKS = 32
DISTRICTS = 4


DIRECTIONS = [(a, b, c) for a in (-1, 0, 1) for b in (-1, 0, 1) for c in (-1, 0, 1) if (a, b, c) != (0, 0, 0)]


def layout(key):
    base = jax.random.fold_in(key, 11)
    subkeys = jax.random.split(base, 4)
    devices = BRICKS // B_DEV
    places = GRID * GRID
    live_count = jax.random.randint(subkeys[0], (DISTRICTS, devices), 1, B_DEV + 1)
    fullest = jax.random.randint(subkeys[1], (DISTRICTS, 1), 0, devices)
    live_count = jnp.where(jnp.arange(devices)[None, :] == fullest, B_DEV, live_count).astype(jnp.int32)
    scores = jax.random.randint(subkeys[2], (DISTRICTS, devices, places), 0, 1 << 20) * places + jnp.arange(places)[None, None, :]
    slot_places = jnp.argsort(scores, axis=-1).astype(jnp.int32)
    place_slots = jnp.argsort(slot_places, axis=-1).astype(jnp.int32)
    return (live_count, slot_places, place_slots, subkeys[3])


def draw_neighbours(key, part):
    live_count, slot_places, place_slots, leftover = layout(key)
    devices = BRICKS // B_DEV
    places = GRID * GRID
    shape3 = (DISTRICTS, devices, B_DEV)
    position = slot_places[:, :, :B_DEV]
    row_index = position // GRID
    col_index = position % GRID
    own_live = jnp.arange(B_DEV)[None, None, :] < live_count[:, :, None]
    device = jnp.broadcast_to(jnp.arange(devices)[None, :, None], shape3)
    flat_slots = place_slots.reshape(DISTRICTS, devices * places)
    columns = []
    for a, b, c in DIRECTIONS:
        there_dev = device + a
        new_row = row_index + b
        new_col = col_index + c
        inside = (there_dev >= 0) & (there_dev < devices) & (new_row >= 0) & (new_row < GRID) & (new_col >= 0) & (new_col < GRID)
        there_clip = jnp.clip(there_dev, 0, devices - 1)
        place_clip = jnp.clip(new_row, 0, GRID - 1) * GRID + jnp.clip(new_col, 0, GRID - 1)
        flat_index = (there_clip * places + place_clip).reshape(DISTRICTS, -1)
        target_slot = jnp.take_along_axis(flat_slots, flat_index, axis=1).reshape(shape3)
        live_there = jnp.take_along_axis(live_count, there_clip.reshape(DISTRICTS, -1), axis=1).reshape(shape3)
        usable = inside & own_live & (target_slot < live_there)
        columns.append(jnp.where(usable, there_clip * B_DEV + target_slot, -1))
    return jnp.stack(columns, axis=-1).reshape(DISTRICTS, BRICKS, 26).astype(jnp.int32)


def draw_occupancy(key, part):
    live_count, slot_places, place_slots, leftover = layout(key)
    subkeys = jax.random.split(leftover, 3)
    percent = jax.random.randint(subkeys[0], (DISTRICTS, BRICKS, 1), 20, 91)
    rolled = jax.random.randint(subkeys[1], (DISTRICTS, BRICKS, 512), 0, 100)
    forced = jax.random.randint(subkeys[2], (DISTRICTS, BRICKS, 1), 0, 512)
    own_live = (jnp.arange(B_DEV)[None, None, :] < live_count[:, :, None]).reshape(DISTRICTS, BRICKS, 1)
    filled = ((rolled < percent) | (jnp.arange(512)[None, None, :] == forced)) & own_live
    return filled.astype(jnp.int32)


def steps_of(stream_key, dims, shards, least, top_value):
    factor_of, own = 1.0, jax.random.fold_in(stream_key, 6)
    for axis_at, blocks in shards:
        draws = jnp.exp(jax.random.uniform(jax.random.fold_in(own, axis_at), (blocks,), jnp.float32, least / len(shards), top_value / len(shards)))
        factor_of = factor_of * jnp.repeat(draws, dims[axis_at] // blocks).reshape([-1 if axis == axis_at else 1 for axis in range(len(dims))])
    return factor_of


def noise(stream_key, shape, deviation, reach, pieces=(), held_as=jnp.bfloat16):
    entries = jax.random.normal(stream_key, shape, jnp.float32) * deviation
    if len(pieces) > 0:
        entries = steps_of(stream_key, shape, pieces, -0.22, 0.18) * entries
    return jnp.clip(entries, min=-reach, max=reach).astype(held_as)


def setup_inputs(seed: int = 0) -> dict:
    seeds = jax.random.split(jax.random.key(seed), 7)
    return {
        "feats": noise(seeds[0], (DISTRICTS, BRICKS, C, 512), 1.0, 6.0, ((0, 4), (1, 8))),
        "cotangent": noise(seeds[1], (DISTRICTS, BRICKS, C, 512), 1.0, 6.0, ((0, 4), (1, 8))),
        "weight": noise(seeds[2], (27, C, C), (27 * C) ** -0.5, 0.15625),
        "bias": noise(seeds[3], (C,), 0.5, 3.0, (), jnp.float32),
        "neighbours": draw_neighbours(jax.random.fold_in(seeds[6], 71), 0),
        "occupancy": draw_occupancy(jax.random.fold_in(seeds[6], 71), 0),
    }


DIRECTIONS = [(a, b, c) for a in (-1, 0, 1) for b in (-1, 0, 1) for c in (-1, 0, 1) if (a, b, c) != (0, 0, 0)]

def extent(shift_step):
    if shift_step < 0:
        return (slice(7, 8), slice(0, 1))
    if shift_step == 0:
        return (slice(0, 8), slice(1, 9))
    return (slice(0, 1), slice(9, 10))

def surround(bricks_cube, targets):
    slot_count = bricks_cube.shape[0]
    padded = jnp.zeros(bricks_cube.shape[:2] + (10, 10, 10), bricks_cube.dtype)
    padded = padded.at[:, :, 1:9, 1:9, 1:9].set(bricks_cube)
    for direction, (a, b, c) in enumerate(DIRECTIONS):
        take_x, put_x = extent(a)
        take_y, put_y = extent(b)
        take_z, put_z = extent(c)
        chosen = targets[:, direction]
        source = jnp.take(bricks_cube[:, :, take_x, take_y, take_z], jnp.clip(chosen, 0, slot_count - 1).astype(jnp.int32), axis=0)
        source = jnp.where((chosen >= 0)[:, None, None, None, None], source, jnp.zeros((), bricks_cube.dtype))
        padded = padded.at[:, :, put_x, put_y, put_z].set(source)
    return padded

def convolve(padded, weight, bias):
    slot_count, channels = (padded.shape[0], padded.shape[1])
    summed = jnp.zeros((slot_count, channels, 512), jnp.float32) + bias[None, :, None]
    for a in range(3):
        for b in range(3):
            for c in range(3):
                shifted = padded[:, :, a:a + 8, b:b + 8, c:c + 8].reshape(slot_count, channels, 512).astype(jnp.float32)
                summed = summed + jnp.einsum('oi,niv->nov', weight[9 * a + 3 * b + c].astype(jnp.float32), shifted)
    return summed

def back_convolve(padded_grad, weight):
    slot_count, channels = (padded_grad.shape[0], padded_grad.shape[1])
    summed = jnp.zeros((slot_count, channels, 512), jnp.float32)
    for a in range(3):
        for b in range(3):
            for c in range(3):
                shifted = padded_grad[:, :, 2 - a:10 - a, 2 - b:10 - b, 2 - c:10 - c].reshape(slot_count, channels, 512).astype(jnp.float32)
                summed = summed + jnp.einsum('oi,nov->niv', weight[9 * a + 3 * b + c].astype(jnp.float32), shifted)
    return summed

def weight_products(grad_pre, padded):
    slot_count, channels = (padded.shape[0], padded.shape[1])
    grad_float = grad_pre.astype(jnp.float32)
    terms_list = []
    for a in range(3):
        for b in range(3):
            for c in range(3):
                shifted = padded[:, :, a:a + 8, b:b + 8, c:c + 8].reshape(slot_count, channels, 512).astype(jnp.float32)
                terms_list.append(jnp.einsum('nov,niv->oi', grad_float, shifted))
    return jnp.stack(terms_list)

def reference(feats, cotangent, weight, bias, neighbours, occupancy):

    def district(inputs):
        features, incoming, targets, filled = inputs
        slot_count, channels = (features.shape[0], features.shape[1])
        masked = features * filled.astype(jnp.bfloat16)[:, None, :]
        keep_float = filled.astype(jnp.float32)[:, None, :]
        padded = surround(masked.reshape(slot_count, channels, 8, 8, 8), targets)
        preact = convolve(padded, weight, bias)
        sigmoid_pre = jax.nn.sigmoid(preact)
        result = (masked.astype(jnp.float32) + keep_float * preact * sigmoid_pre).astype(jnp.bfloat16)
        grad_pre = (incoming.astype(jnp.float32) * keep_float * sigmoid_pre * (1.0 + preact * (1.0 - sigmoid_pre))).astype(jnp.bfloat16)
        padded_grad = surround(grad_pre.reshape(slot_count, channels, 8, 8, 8), targets)
        returned = back_convolve(padded_grad, weight)
        in_grad = (keep_float * (incoming.astype(jnp.float32) + returned)).astype(jnp.bfloat16)
        weight_terms = weight_products(grad_pre, padded)
        bias_terms = lax.optimization_barrier(jnp.sum(grad_pre.astype(jnp.float32), axis=(0, 2)))
        return (result, in_grad, weight_terms, bias_terms)
    result, in_grad, weight_terms, bias_terms = lax.map(district, (feats, cotangent, neighbours, occupancy))
    normaliser = 1.0 / math.sqrt(DISTRICTS * BRICKS * 512)
    return (result, in_grad, lax.optimization_barrier(jnp.sum(weight_terms, axis=0)) * normaliser, lax.optimization_barrier(jnp.sum(bias_terms, axis=0)) * normaliser)
```

```python
import math

import jax
import jax.numpy as jnp
from jax import lax
from jax.experimental import pallas as pl
from jax.experimental.pallas import tpu as pltpu
from jax.sharding import PartitionSpec as P

BF, F32 = jnp.bfloat16, jnp.float32
DIRECTIONS = [
    (a, b, c) for a in (-1, 0, 1) for b in (-1, 0, 1) for c in (-1, 0, 1) if (a, b, c) != (0, 0, 0)
]
PLANE = 64
VMEM = pl.BlockSpec(memory_space=pltpu.VMEM)
SMEM = pl.BlockSpec(memory_space=pltpu.SMEM)


def to_planes(tiles, t):
    low = lax.broadcasted_iota(jnp.int32, tiles[0].shape, 1) < PLANE
    turned = [pltpu.roll(tile, PLANE, 1) for tile in tiles]
    first, second = [], []
    for m in range(0, len(tiles), 2):
        first.append(jnp.where(low, tiles[m], turned[m + 1]))
        second.append(jnp.where(low, turned[m], tiles[m + 1]))
    return jnp.concatenate(first, axis=1), jnp.concatenate(second, axis=1)


def from_planes(first, second):
    low = lax.broadcasted_iota(jnp.int32, (first.shape[0], 128), 1) < PLANE
    tiles = []
    for g in range(first.shape[1] // 128):
        one = first[:, 128 * g : 128 * g + 128]
        two = second[:, 128 * g : 128 * g + 128]
        tiles.append(jnp.where(low, one, pltpu.roll(two, PLANE, 1)))
        tiles.append(jnp.where(low, pltpu.roll(one, PLANE, 1), two))
    return tiles


def slot_rows(near_ref, dx, bricks):
    lane = lax.broadcasted_iota(jnp.int32, (1, bricks * PLANE), 1)
    brick = lane // PLANE
    rows = {}
    for dy in (-1, 0, 1):
        for dz in (-1, 0, 1):
            if (dx, dy, dz) == (0, 0, 0):
                rows[dy, dz] = brick * PLANE
                continue
            j = DIRECTIONS.index((dx, dy, dz))
            found = jnp.full(lane.shape, -(1 << 20), jnp.int32)
            for n in range(bricks):
                chosen = near_ref[n, j]
                row = jnp.where(chosen >= 0, lax.rem(chosen, bricks) * PLANE, -(1 << 20))
                found = jnp.where(brick == n, row, found)
            rows[dy, dz] = found
    return rows


def selection(rows, b, c, bricks):
    size = bricks * PLANE
    lane = lax.broadcasted_iota(jnp.int32, (1, size), 1)
    y = ((lane >> 3) & 7) + (b - 1)
    z = (lane & 7) + (c - 1)
    out_y = (y < 0) | (y > 7)
    out_z = (z < 0) | (z > 7)
    base = rows[0, 0]
    if b != 1:
        base = jnp.where(out_y, rows[b - 1, 0], base)
    if c != 1:
        base = jnp.where(out_z, rows[0, c - 1], base)
    if b != 1 and c != 1:
        base = jnp.where(out_y & out_z, rows[b - 1, c - 1], base)
    source = base + (y & 7) * 8 + (z & 7)
    row = lax.broadcasted_iota(jnp.int32, (size, size), 0)
    return jnp.where(row == source, 1.0, 0.0).astype(BF)


def dot(x, y):
    return lax.dot_general(x, y, (((1,), (0,)), ((), ())), preferred_element_type=F32)


def dot_t(x, y):
    return lax.dot_general(x, y, (((1,), (1,)), ((), ())), preferred_element_type=F32)


def faces_kernel(feats_ref, occ_ref, low_ref, high_ref):
    bricks, _, voxels = feats_ref.shape
    keep = occ_ref[...].astype(F32)
    for ref, t, which in ((low_ref, 0, 0), (high_ref, voxels // 128 - 1, 1)):
        at = slice(128 * t, 128 * t + 128)
        tiles = [feats_ref[m, :, at].astype(F32) * keep[m : m + 1, at] for m in range(bricks)]
        ref[...] = to_planes(tiles, t)[which].astype(BF)


def shifted(planes_ref, moved_ref, near_ref, bricks, channels):
    rows = slot_rows(near_ref, 0, bricks)
    count = planes_ref.shape[0]
    flat = planes_ref[...].reshape(count * channels, bricks * PLANE)
    for b in range(3):
        for c in range(3):
            k = 3 * b + c
            if k == 4:
                part = flat
            else:
                part = dot(flat, selection(rows, b, c, bricks)).astype(BF)
            moved_ref[:, channels * k : channels * (k + 1), :] = part.reshape(
                count, channels, bricks * PLANE
            )


def shifted_face(face, near_ref, dx, bricks):
    rows = slot_rows(near_ref, dx, bricks)
    parts = []
    for b in range(3):
        for c in range(3):
            parts.append(dot(face, selection(rows, b, c, bricks)).astype(BF))
    return jnp.concatenate(parts, axis=0)


def inner_kernel(
    near_ref, feats_ref, cot_ref, occ_ref, weight_ref, bias_ref,
    moved_ref, pre_ref, cot2_ref, occ2_ref, planes_ref, total_ref,
):
    bricks, channels, voxels = feats_ref.shape
    keep = occ_ref[...].astype(F32)
    for t in range(voxels // 128):
        at = slice(128 * t, 128 * t + 128)
        kept = [jnp.broadcast_to(keep[m : m + 1, at], (channels, 128)) for m in range(bricks)]
        first, second = to_planes([feats_ref[m, :, at].astype(F32) * kept[m] for m in range(bricks)], t)
        planes_ref[2 * t] = first.astype(BF)
        planes_ref[2 * t + 1] = second.astype(BF)
        first, second = to_planes([cot_ref[m, :, at].astype(F32) * kept[m] for m in range(bricks)], t)
        cot2_ref[2 * t] = first.astype(BF)
        cot2_ref[2 * t + 1] = second.astype(BF)
        first, second = to_planes([kept[m][:8] for m in range(bricks)], t)
        occ2_ref[2 * t] = first
        occ2_ref[2 * t + 1] = second
    shifted(planes_ref, moved_ref, near_ref, bricks, channels)
    count = planes_ref.shape[0]
    start = jnp.broadcast_to(bias_ref[...], (channels, bricks * PLANE))
    for x in range(count + 2):
        total_ref[channels * x : channels * (x + 1), :] = start
    for x in range(count):
        at = slice(channels * x, channels * (x + 3))
        total_ref[at, :] += dot(weight_ref[...], moved_ref[x])
    pre_ref[...] = total_ref[channels : channels * (count + 1), :].reshape(pre_ref.shape)


def outer_kernel(
    near_ref, low_ref, high_ref, moved_ref, pre_ref, cot2_ref, occ2_ref, weight_ref,
    result_ref, grad_ref, terms_ref, padded_ref,
):
    count, channels, lanes = pre_ref.shape
    bricks = lanes // PLANE
    moved_low = shifted_face(low_ref[...], near_ref, -1, bricks)
    moved_high = shifted_face(high_ref[...], near_ref, 1, bricks)
    add_low = dot(weight_ref[2 * channels : 3 * channels, :], moved_low)
    add_high = dot(weight_ref[0:channels, :], moved_high)
    padded_ref[0:channels, :] = jnp.zeros((channels, lanes), BF)
    padded_ref[channels * (count + 1) :, :] = jnp.zeros((channels, lanes), BF)
    bias = jnp.zeros((channels, lanes), F32)
    for x in range(count):
        pre = pre_ref[x]
        if x == 0:
            pre = pre + add_low
        if x == count - 1:
            pre = pre + add_high
        keep = jnp.broadcast_to(occ2_ref[x][0:1], (channels, lanes))
        sig = jax.nn.sigmoid(pre)
        masked = moved_ref[x, 4 * channels : 5 * channels, :].astype(F32)
        result_ref[x] = (masked + keep * pre * sig).astype(BF)
        grad = (cot2_ref[x].astype(F32) * sig * (1.0 + pre * (1.0 - sig))).astype(BF)
        grad_ref[x] = grad
        padded_ref[channels * (x + 1) : channels * (x + 2), :] = grad
        bias = bias + grad.astype(F32)
    terms = dot_t(padded_ref[0 : 3 * channels, :], moved_ref[0])
    for x in range(1, count):
        terms = terms + dot_t(padded_ref[channels * x : channels * (x + 3), :], moved_ref[x])
    width = 9 * channels
    terms_ref[:, 0:width] = terms
    terms_ref[2 * channels : 3 * channels, 0:width] += dot_t(grad_ref[0], moved_low)
    terms_ref[0:channels, 0:width] += dot_t(grad_ref[count - 1], moved_high)
    terms_ref[:, width:] = jnp.zeros((3 * channels, terms_ref.shape[1] - width), F32)
    terms_ref[0:channels, width:] = jnp.broadcast_to(
        jnp.sum(bias, axis=1, keepdims=True), (channels, terms_ref.shape[1] - width)
    )


def back_kernel(
    near_ref, low_ref, high_ref, grad_ref, result2_ref, cot_ref, occ_ref, weight_ref,
    result_ref, in_grad_ref, moved_ref, total_ref,
):
    count, channels, lanes = grad_ref.shape
    bricks = lanes // PLANE
    shifted(grad_ref, moved_ref, near_ref, bricks, channels)
    total_ref[...] = jnp.zeros(total_ref.shape, F32)
    for x in range(count):
        at = slice(channels * x, channels * (x + 3))
        total_ref[at, :] += dot(weight_ref[...], moved_ref[x])
    moved_low = shifted_face(low_ref[...], near_ref, -1, bricks)
    moved_high = shifted_face(high_ref[...], near_ref, 1, bricks)
    total_ref[channels : 2 * channels, :] += dot(
        weight_ref[2 * channels : 3 * channels, :], moved_low
    )
    total_ref[channels * count : channels * (count + 1), :] += dot(
        weight_ref[0:channels, :], moved_high
    )
    keep = occ_ref[...].astype(F32)
    for t in range(count // 2):
        at = slice(128 * t, 128 * t + 128)
        first = total_ref[channels * (2 * t + 1) : channels * (2 * t + 2), :]
        second = total_ref[channels * (2 * t + 2) : channels * (2 * t + 3), :]
        back = from_planes(first, second)
        out = from_planes(result2_ref[2 * t].astype(F32), result2_ref[2 * t + 1].astype(F32))
        for m in range(bricks):
            in_grad_ref[m, :, at] = (
                keep[m : m + 1, at] * (cot_ref[m, :, at].astype(F32) + back[m])
            ).astype(BF)
            result_ref[m, :, at] = out[m].astype(BF)


def call(body, outs, ins, scratch=(), flops=0):
    shapes = [jax.ShapeDtypeStruct(shape, dtype) for shape, dtype in outs]
    moved = sum(math.prod(s.shape) * s.dtype.itemsize for s in shapes)
    moved += sum(math.prod(x.shape) * x.dtype.itemsize for _, x in ins)
    return pl.pallas_call(
        body,
        out_shape=shapes,
        in_specs=[spec for spec, _ in ins],
        out_specs=[VMEM] * len(shapes),
        scratch_shapes=list(scratch),
        compiler_params=pltpu.CompilerParams(vmem_limit_bytes=32 << 20),
        cost_estimate=pl.CostEstimate(flops=flops, bytes_accessed=moved, transcendentals=0),
    )(*[x for _, x in ins])


def exchange_faces(low, high):
    size = lax.axis_size("space")
    up = [(i, i + 1) for i in range(size - 1)]
    down = [(j, i) for i, j in up]
    return lax.ppermute(high, "space", up), lax.ppermute(low, "space", down)


def total_over_devices(terms):
    axes = ("space", "rep")
    spaces, reps = lax.axis_size("space"), lax.axis_size("rep")
    me = lax.axis_index("rep")
    core = me % 2
    half = terms.shape[0] // 2
    partner = [(i, i ^ 1) for i in range(spaces * reps)]
    theirs = lax.dynamic_slice_in_dim(terms, (1 - core) * half, half, 0).astype(BF)
    mine = lax.dynamic_slice_in_dim(terms, core * half, half, 0)
    mine = mine + lax.ppermute(theirs, axes, partner).astype(F32)
    bits = [1 << i for i in range(1, (spaces * reps).bit_length() - 1)]
    orders = (bits, bits[2:] + bits[:2]) if len(bits) == 4 else (bits, bits)
    for steps in zip(*orders):
        sent = mine.astype(BF)
        pairs = [(i, i ^ steps[i % 2]) for i in range(spaces * reps)]
        mine = sent.astype(F32) + lax.ppermute(sent, axes, pairs).astype(F32)
    other = lax.ppermute(mine, axes, partner)
    first = jnp.where(core == 0, mine, other)
    second = jnp.where(core == 0, other, mine)
    return jnp.concatenate([first, second], axis=0)


def on_device(feats, cotangent, weight, bias, neighbours, occupancy):
    x, cot, near, occ = feats[0], cotangent[0], neighbours[0], occupancy[0]
    bricks, channels, voxels = x.shape
    count, lanes = voxels // PLANE, bricks * PLANE
    width = 9 * channels
    low, high = call(
        faces_kernel, [((channels, lanes), BF)] * 2, [(VMEM, x), (VMEM, occ)]
    )
    from_low, from_high = exchange_faces(low, high)
    by_step = weight.reshape(3, 9, channels, channels)
    ahead = by_step[::-1].transpose(0, 2, 1, 3).reshape(3 * channels, width)
    back = by_step[:, ::-1].transpose(0, 3, 1, 2).reshape(3 * channels, width)
    moved, pre, cot2, occ2 = call(
        inner_kernel,
        [
            ((count, width, lanes), BF),
            ((count, channels, lanes), F32),
            ((count, channels, lanes), BF),
            ((count, 8, lanes), F32),
        ],
        [(SMEM, near), (VMEM, x), (VMEM, cot), (VMEM, occ), (VMEM, ahead), (VMEM, bias[:, None])],
        [
            pltpu.VMEM((count, channels, lanes), BF),
            pltpu.VMEM((channels * (count + 2), lanes), F32),
        ],
        flops=2 * 27 * channels * channels * bricks * voxels,
    )
    result2, grad, terms = call(
        outer_kernel,
        [
            ((count, channels, lanes), BF),
            ((count, channels, lanes), BF),
            ((3 * channels, width + 64), F32),
        ],
        [
            (SMEM, near), (VMEM, from_low), (VMEM, from_high), (VMEM, moved), (VMEM, pre),
            (VMEM, cot2), (VMEM, occ2), (VMEM, ahead),
        ],
        [pltpu.VMEM((channels * (count + 2), lanes), BF)],
        flops=2 * 27 * channels * channels * bricks * voxels,
    )
    grad_low, grad_high = exchange_faces(grad[0], grad[count - 1])
    total = total_over_devices(terms)
    result, in_grad = call(
        back_kernel,
        [((bricks, channels, voxels), BF)] * 2,
        [
            (SMEM, near), (VMEM, grad_low), (VMEM, grad_high), (VMEM, grad), (VMEM, result2),
            (VMEM, cot), (VMEM, occ), (VMEM, back),
        ],
        [
            pltpu.VMEM((count, width, lanes), BF),
            pltpu.VMEM((channels * (count + 2), lanes), F32),
        ],
        flops=2 * 27 * channels * channels * bricks * voxels,
    )
    normaliser = 1.0 / math.sqrt(
        feats.shape[0] * lax.axis_size("rep") * bricks * lax.axis_size("space") * voxels
    )
    total = total * normaliser
    weight_grad = total[:, :width].reshape(3, channels, 9, channels)[::-1].transpose(0, 2, 1, 3)
    return (
        result[None],
        in_grad[None],
        weight_grad.reshape(weight.shape),
        total[:channels, width],
    )


def solution(mesh):
    placed = (
        P("rep", "space", None, None),
        P("rep", "space", None, None),
        P(),
        P(),
        P("rep", "space", None),
        P("rep", "space", None),
    )
    return jax.shard_map(
        on_device,
        mesh=mesh,
        in_specs=placed,
        out_specs=(P("rep", "space", None, None), P("rep", "space", None, None), P(), P()),
        check_vma=False,
    )
```

```python
import functools
import math

import jax
import jax.numpy as jnp
from jax import lax
from jax.experimental import pallas as pl
from jax.experimental.pallas import tpu as pltpu
from jax.sharding import PartitionSpec as P

BF, F32 = jnp.bfloat16, jnp.float32
DIRECTIONS = [
    (a, b, c) for a in (-1, 0, 1) for b in (-1, 0, 1) for c in (-1, 0, 1) if (a, b, c) != (0, 0, 0)
]
PLANE = 64
VMEM = pl.BlockSpec(memory_space=pltpu.VMEM)
ANY = pl.BlockSpec(memory_space=pl.ANY)
SMEM = pl.BlockSpec(memory_space=pltpu.SMEM)


def to_planes(tiles):
    low = lax.broadcasted_iota(jnp.int32, tiles[0].shape, 1) < PLANE
    turned = [pltpu.roll(tile, PLANE, 1) for tile in tiles]
    first, second = [], []
    for m in range(0, len(tiles), 2):
        first.append(jnp.where(low, tiles[m], turned[m + 1]))
        second.append(jnp.where(low, turned[m], tiles[m + 1]))
    return jnp.concatenate(first, axis=1), jnp.concatenate(second, axis=1)


def from_planes(first, second):
    low = lax.broadcasted_iota(jnp.int32, (first.shape[0], 128), 1) < PLANE
    tiles = []
    for g in range(first.shape[1] // 128):
        one = first[:, 128 * g : 128 * g + 128]
        two = second[:, 128 * g : 128 * g + 128]
        tiles.append(jnp.where(low, one, pltpu.roll(two, PLANE, 1)))
        tiles.append(jnp.where(low, pltpu.roll(one, PLANE, 1), two))
    return tiles


def slot_rows(near_ref, dx, bricks):
    lane = lax.broadcasted_iota(jnp.int32, (1, bricks * PLANE), 1)
    brick = lane // PLANE
    rows = {}
    for dy in (-1, 0, 1):
        for dz in (-1, 0, 1):
            if (dx, dy, dz) == (0, 0, 0):
                rows[dy, dz] = brick * PLANE
                continue
            j = DIRECTIONS.index((dx, dy, dz))
            found = jnp.full(lane.shape, -(1 << 20), jnp.int32)
            for n in range(bricks):
                chosen = near_ref[n, j]
                row = jnp.where(chosen >= 0, lax.rem(chosen, bricks) * PLANE, -(1 << 20))
                found = jnp.where(brick == n, row, found)
            rows[dy, dz] = found
    return rows


def selection(rows, b, c, bricks):
    size = bricks * PLANE
    lane = lax.broadcasted_iota(jnp.int32, (1, size), 1)
    y = ((lane >> 3) & 7) + (b - 1)
    z = (lane & 7) + (c - 1)
    out_y = (y < 0) | (y > 7)
    out_z = (z < 0) | (z > 7)
    base = rows[0, 0]
    if b != 1:
        base = jnp.where(out_y, rows[b - 1, 0], base)
    if c != 1:
        base = jnp.where(out_z, rows[0, c - 1], base)
    if b != 1 and c != 1:
        base = jnp.where(out_y & out_z, rows[b - 1, c - 1], base)
    source = base + (y & 7) * 8 + (z & 7)
    row = lax.broadcasted_iota(jnp.int32, (size, size), 0)
    return jnp.where(row == source, 1.0, 0.0).astype(BF)


def dot(x, y):
    return lax.dot_general(x, y, (((1,), (0,)), ((), ())), preferred_element_type=F32)


def dot_t(x, y):
    return lax.dot_general(x, y, (((1,), (1,)), ((), ())), preferred_element_type=F32)


def faces_kernel(feats_ref, occ_ref, low_ref, high_ref, held_ref, keep_ref, sems):
    bricks, _, voxels = feats_ref.shape
    copies = [pltpu.make_async_copy(occ_ref, keep_ref, sems.at[0])]
    for i, start in enumerate((0, voxels - 128)):
        copies.append(
            pltpu.make_async_copy(
                feats_ref.at[:, :, pl.ds(start, 128)], held_ref.at[i], sems.at[i + 1]
            )
        )
    for copy in copies:
        copy.start()
    for copy in copies:
        copy.wait()
    keep = keep_ref[...].astype(F32)
    for i, (ref, start) in enumerate(((low_ref, 0), (high_ref, voxels - 128))):
        at = slice(start, start + 128)
        tiles = [held_ref[i, m].astype(F32) * keep[m : m + 1, at] for m in range(bricks)]
        ref[...] = to_planes(tiles)[i].astype(BF)


def weights_kernel(weight_ref, ahead_ref, back_ref):
    channels = weight_ref.shape[1]
    for r in range(3):
        blocks = [weight_ref[9 * (2 - r) + k].astype(F32) for k in range(9)]
        ahead_ref[channels * r : channels * (r + 1), :] = jnp.concatenate(blocks, axis=1).astype(BF)
        blocks = [weight_ref[9 * r + 8 - k].astype(F32).T for k in range(9)]
        back_ref[channels * r : channels * (r + 1), :] = jnp.concatenate(blocks, axis=1).astype(BF)


def shifted(planes_ref, moved_ref, near_ref, bricks, channels):
    rows = slot_rows(near_ref, 0, bricks)
    count = planes_ref.shape[0]
    flat = planes_ref[...].reshape(count * channels, bricks * PLANE)
    for b in range(3):
        for c in range(3):
            k = 3 * b + c
            if k == 4:
                part = flat
            else:
                part = dot(flat, selection(rows, b, c, bricks)).astype(BF)
            moved_ref[:, channels * k : channels * (k + 1), :] = part.reshape(
                count, channels, bricks * PLANE
            )


def shifted_face(face, near_ref, dx, bricks):
    rows = slot_rows(near_ref, dx, bricks)
    parts = []
    for b in range(3):
        for c in range(3):
            parts.append(dot(face, selection(rows, b, c, bricks)).astype(BF))
    return jnp.concatenate(parts, axis=0)


def inner_kernel(
    near_ref, feats_ref, cot_ref, occ_ref, weight_ref, bias_ref,
    moved_ref, pre_ref, cot2_ref, occ2_ref, planes_ref, total_ref,
):
    bricks, channels, voxels = feats_ref.shape
    keep = occ_ref[...].astype(F32)
    for t in range(voxels // 128):
        at = slice(128 * t, 128 * t + 128)
        kept = [jnp.broadcast_to(keep[m : m + 1, at], (channels, 128)) for m in range(bricks)]
        first, second = to_planes([feats_ref[m, :, at].astype(F32) * kept[m] for m in range(bricks)])
        planes_ref[2 * t] = first.astype(BF)
        planes_ref[2 * t + 1] = second.astype(BF)
        first, second = to_planes([cot_ref[m, :, at].astype(F32) * kept[m] for m in range(bricks)])
        cot2_ref[2 * t] = first.astype(BF)
        cot2_ref[2 * t + 1] = second.astype(BF)
        first, second = to_planes([kept[m][:8] for m in range(bricks)])
        occ2_ref[2 * t] = first
        occ2_ref[2 * t + 1] = second
    shifted(planes_ref, moved_ref, near_ref, bricks, channels)
    count = planes_ref.shape[0]
    start = jnp.broadcast_to(bias_ref[...], (channels, bricks * PLANE))
    for x in range(count + 2):
        total_ref[channels * x : channels * (x + 1), :] = start
    for x in range(count):
        at = slice(channels * x, channels * (x + 3))
        total_ref[at, :] += dot(weight_ref[...], moved_ref[x])
    pre_ref[...] = total_ref[channels : channels * (count + 1), :].reshape(pre_ref.shape)


def outer_kernel(
    near_ref, low_ref, high_ref, moved_ref, pre_ref, cot2_ref, occ2_ref, weight_ref,
    result_ref, grad_ref, terms_ref, padded_ref,
):
    count, channels, lanes = pre_ref.shape
    bricks = lanes // PLANE
    moved_low = shifted_face(low_ref[...], near_ref, -1, bricks)
    moved_high = shifted_face(high_ref[...], near_ref, 1, bricks)
    add_low = dot(weight_ref[2 * channels : 3 * channels, :], moved_low)
    add_high = dot(weight_ref[0:channels, :], moved_high)
    padded_ref[0:channels, :] = jnp.zeros((channels, lanes), BF)
    padded_ref[channels * (count + 1) :, :] = jnp.zeros((channels, lanes), BF)
    bias = jnp.zeros((channels, lanes), F32)
    for x in range(count):
        pre = pre_ref[x]
        if x == 0:
            pre = pre + add_low
        if x == count - 1:
            pre = pre + add_high
        keep = jnp.broadcast_to(occ2_ref[x][0:1], (channels, lanes))
        sig = jax.nn.sigmoid(pre)
        masked = moved_ref[x, 4 * channels : 5 * channels, :].astype(F32)
        result_ref[x] = (masked + keep * pre * sig).astype(BF)
        grad = (cot2_ref[x].astype(F32) * sig * (1.0 + pre * (1.0 - sig))).astype(BF)
        grad_ref[x] = grad
        padded_ref[channels * (x + 1) : channels * (x + 2), :] = grad
        bias = bias + grad.astype(F32)
    terms = dot_t(padded_ref[0 : 3 * channels, :], moved_ref[0])
    for x in range(1, count):
        terms = terms + dot_t(padded_ref[channels * x : channels * (x + 3), :], moved_ref[x])
    width = 9 * channels
    terms_ref[:, 0:width] = terms
    terms_ref[2 * channels : 3 * channels, 0:width] += dot_t(grad_ref[0], moved_low)
    terms_ref[0:channels, 0:width] += dot_t(grad_ref[count - 1], moved_high)
    spare = terms_ref.shape[1] - width
    terms_ref[channels:, width:] = jnp.zeros((2 * channels, spare), F32)
    terms_ref[0:channels, width:] = jnp.sum(bias, axis=1, keepdims=True) * spread(spare)


def spread(count):
    return 1.0 + lax.broadcasted_iota(jnp.int32, (1, count), 1).astype(F32) * (1.0 / count)


def first_sum_kernel(mine_ref, other_ref, grad_ref, out_ref, low_ref, high_ref):
    out_ref[...] = (mine_ref[...] + other_ref[...].astype(F32)).astype(BF)
    low_ref[...] = grad_ref[0]
    high_ref[...] = grad_ref[grad_ref.shape[0] - 1]


def sum_kernel(mine_ref, other_ref, *refs):
    out_ref = refs[-1]
    out_ref[...] = (mine_ref[...].astype(F32) + other_ref[...].astype(F32)).astype(out_ref.dtype)


def back_inner_kernel(
    near_ref, grad_ref, result2_ref, weight_ref, after_ref, result_ref, total_ref, moved_ref
):
    count, channels, lanes = grad_ref.shape
    bricks = lanes // PLANE
    shifted(grad_ref, moved_ref, near_ref, bricks, channels)
    total_ref[...] = jnp.zeros(total_ref.shape, F32)
    for x in range(count):
        at = slice(channels * x, channels * (x + 3))
        total_ref[at, :] += dot(weight_ref[...], moved_ref[x])
    for t in range(count // 2):
        out = from_planes(result2_ref[2 * t].astype(F32), result2_ref[2 * t + 1].astype(F32))
        for m in range(bricks):
            result_ref[m, :, 128 * t : 128 * t + 128] = out[m].astype(BF)


def back_outer_kernel(
    near_ref, low_ref, high_ref, total_ref, cot_ref, occ_ref, weight_ref, after_ref, in_grad_ref
):
    bricks, channels, voxels = cot_ref.shape
    count = voxels // PLANE
    moved_low = shifted_face(low_ref[...], near_ref, -1, bricks)
    moved_high = shifted_face(high_ref[...], near_ref, 1, bricks)
    add_low = dot(weight_ref[2 * channels : 3 * channels, :], moved_low)
    add_high = dot(weight_ref[0:channels, :], moved_high)
    keep = occ_ref[...].astype(F32)
    for t in range(count // 2):
        at = slice(128 * t, 128 * t + 128)
        first = total_ref[channels * (2 * t + 1) : channels * (2 * t + 2), :]
        second = total_ref[channels * (2 * t + 2) : channels * (2 * t + 3), :]
        if t == 0:
            first = first + add_low
        if t == count // 2 - 1:
            second = second + add_high
        back = from_planes(first, second)
        for m in range(bricks):
            in_grad_ref[m, :, at] = (
                keep[m : m + 1, at] * (cot_ref[m, :, at].astype(F32) + back[m])
            ).astype(BF)


def final_kernel(normaliser, core_ref, mine_ref, other_ref, weight_ref, bias_ref, whole_ref):
    half, columns = mine_ref.shape
    channels = weight_ref.shape[1]
    core = core_ref[0]
    whole_ref[pl.ds(core * half, half), :] = mine_ref[...]
    whole_ref[pl.ds((1 - core) * half, half), :] = other_ref[...]
    for r in range(3):
        rows = slice(channels * r, channels * (r + 1))
        for t in range(columns // 128):
            tile = whole_ref[rows, 128 * t : 128 * t + 128] * normaliser
            weight_ref[9 * (2 - r) + 2 * t] = tile[:, :channels]
            if 2 * t + 1 < 9:
                weight_ref[9 * (2 - r) + 2 * t + 1] = pltpu.roll(tile, 128 - channels, 1)[:, :channels]
            elif r == 0:
                copies = pltpu.roll(tile, 128 - channels, 1)[:, :channels]
                copies = copies / (spread(channels) * channels)
                column = jnp.sum(copies, axis=1, keepdims=True)
                at = (channels, channels)
                same = lax.broadcasted_iota(jnp.int32, at, 0) == lax.broadcasted_iota(jnp.int32, at, 1)
                bias_ref[...] = jnp.sum(jnp.where(same, column, 0.0), axis=0, keepdims=True)


def call(body, outs, ins, scratch=(), flops=0):
    shapes = [jax.ShapeDtypeStruct(shape, dtype) for shape, dtype in outs]
    moved = sum(math.prod(s.shape) * s.dtype.itemsize for s in shapes)
    moved += sum(math.prod(x.shape) * x.dtype.itemsize for _, x in ins)
    return pl.pallas_call(
        body,
        out_shape=shapes,
        in_specs=[spec for spec, _ in ins],
        out_specs=[VMEM] * len(shapes),
        scratch_shapes=list(scratch),
        compiler_params=pltpu.CompilerParams(vmem_limit_bytes=32 << 20),
        cost_estimate=pl.CostEstimate(flops=flops, bytes_accessed=moved, transcendentals=0),
    )(*[x for _, x in ins])


def exchange_faces(low, high):
    size = lax.axis_size("space")
    up = [(i, i + 1) for i in range(size - 1)]
    down = [(j, i) for i, j in up]
    return lax.ppermute(high, "space", up), lax.ppermute(low, "space", down)


def on_device(feats, cotangent, weight, bias, neighbours, occupancy):
    x, cot, near, occ = feats[0], cotangent[0], neighbours[0], occupancy[0]
    bricks, channels, voxels = x.shape
    count, lanes = voxels // PLANE, bricks * PLANE
    width = 9 * channels
    low, high = call(
        faces_kernel,
        [((channels, lanes), BF)] * 2,
        [(ANY, x), (ANY, occ)],
        [
            pltpu.VMEM((2, bricks, channels, 128), BF),
            pltpu.VMEM((bricks, voxels), jnp.int32),
            pltpu.SemaphoreType.DMA((3,)),
        ],
    )
    from_low, from_high = exchange_faces(low, high)
    ahead, back = call(weights_kernel, [((3 * channels, width), BF)] * 2, [(VMEM, weight)])
    moved, pre, cot2, occ2 = call(
        inner_kernel,
        [
            ((count, width, lanes), BF),
            ((count, channels, lanes), F32),
            ((count, channels, lanes), BF),
            ((count, 8, lanes), F32),
        ],
        [(SMEM, near), (VMEM, x), (VMEM, cot), (VMEM, occ), (VMEM, ahead), (VMEM, bias[:, None])],
        [
            pltpu.VMEM((count, channels, lanes), BF),
            pltpu.VMEM((channels * (count + 2), lanes), F32),
        ],
        flops=2 * 27 * channels * channels * bricks * voxels,
    )
    result2, grad, terms = call(
        outer_kernel,
        [
            ((count, channels, lanes), BF),
            ((count, channels, lanes), BF),
            ((3 * channels, width + 64), F32),
        ],
        [
            (SMEM, near), (VMEM, from_low), (VMEM, from_high), (VMEM, moved), (VMEM, pre),
            (VMEM, cot2), (VMEM, occ2), (VMEM, ahead),
        ],
        [pltpu.VMEM((channels * (count + 2), lanes), BF)],
        flops=2 * 27 * channels * channels * bricks * voxels,
    )
    axes = ("space", "rep")
    devices = lax.axis_size("space") * lax.axis_size("rep")
    core = lax.axis_index("rep") % 2
    half = 3 * channels // 2
    partner = [(i, i ^ 1) for i in range(devices)]
    theirs = lax.dynamic_slice_in_dim(terms, (1 - core) * half, half, 0).astype(BF)
    mine = lax.dynamic_slice_in_dim(terms, core * half, half, 0)
    other = lax.ppermute(theirs, axes, partner)
    plane = ((channels, lanes), BF)
    sent = ((half, terms.shape[1]), BF)
    mine, low, high = call(
        first_sum_kernel, [sent, plane, plane], [(VMEM, mine), (VMEM, other), (VMEM, grad)]
    )
    bits = [1 << i for i in range(1, (devices).bit_length() - 1)]
    turn = len(bits) // 2
    grad_low = grad_high = total = in_grad = result = None
    rounds = list(zip(bits, bits[turn:] + bits[:turn]))
    for i, steps in enumerate(rounds):
        other = lax.ppermute(mine, axes, [(j, j ^ steps[j % 2]) for j in range(devices)])
        held = []
        if i == 0:
            grad_low, grad_high = exchange_faces(low, high)
            held = [grad_low, grad_high]
        if i == 1:
            result, total = call(
                back_inner_kernel,
                [((bricks, channels, voxels), BF), ((channels * (count + 2), lanes), F32)],
                [(SMEM, near), (VMEM, grad), (VMEM, result2), (VMEM, back), (ANY, mine)],
                [pltpu.VMEM((count, width, lanes), BF)],
                flops=2 * 27 * channels * channels * bricks * voxels,
            )
            held = [total]
        if i == 2:
            (in_grad,) = call(
                back_outer_kernel,
                [((bricks, channels, voxels), BF)],
                [
                    (SMEM, near), (VMEM, grad_low), (VMEM, grad_high), (VMEM, total), (VMEM, cot),
                    (VMEM, occ), (VMEM, back), (ANY, mine),
                ],
                flops=2 * 6 * channels * channels * bricks * voxels,
            )
            held = [in_grad]
        last = i == len(rounds) - 1
        (mine,) = call(
            sum_kernel,
            [(sent[0], F32 if last else BF)],
            [(VMEM, mine), (VMEM, other)] + [(ANY, h) for h in held],
        )
    other = lax.ppermute(mine, axes, partner)
    normaliser = 1.0 / math.sqrt(
        feats.shape[0] * lax.axis_size("rep") * bricks * lax.axis_size("space") * voxels
    )
    weight_grad, bias_grad = call(
        functools.partial(final_kernel, normaliser),
        [(weight.shape, F32), ((1, channels), F32)],
        [(SMEM, core.astype(jnp.int32)[None]), (VMEM, mine), (VMEM, other)],
        [pltpu.VMEM(terms.shape, F32)],
    )
    return result[None], in_grad[None], weight_grad, bias_grad[0]


def solution(mesh):
    placed = (
        P("rep", "space", None, None),
        P("rep", "space", None, None),
        P(),
        P(),
        P("rep", "space", None),
        P("rep", "space", None),
    )
    return jax.shard_map(
        on_device,
        mesh=mesh,
        in_specs=placed,
        out_specs=(P("rep", "space", None, None), P("rep", "space", None, None), P(), P()),
        check_vma=False,
    )
```

```python
import functools
import math

import jax
import jax.numpy as jnp
from jax import lax
from jax.experimental import pallas as pl
from jax.experimental.pallas import tpu as pltpu
from jax.sharding import PartitionSpec as P

BF, F32 = jnp.bfloat16, jnp.float32
DIRECTIONS = [
    (a, b, c) for a in (-1, 0, 1) for b in (-1, 0, 1) for c in (-1, 0, 1) if (a, b, c) != (0, 0, 0)
]
PLANE = 64
VMEM = pl.BlockSpec(memory_space=pltpu.VMEM)
ANY = pl.BlockSpec(memory_space=pl.ANY)
HBM = pl.BlockSpec(memory_space=pltpu.HBM)
SMEM = pl.BlockSpec(memory_space=pltpu.SMEM)


def to_planes(tiles):
    low = lax.broadcasted_iota(jnp.int32, tiles[0].shape, 1) < PLANE
    turned = [pltpu.roll(tile, PLANE, 1) for tile in tiles]
    first, second = [], []
    for m in range(0, len(tiles), 2):
        first.append(jnp.where(low, tiles[m], turned[m + 1]))
        second.append(jnp.where(low, turned[m], tiles[m + 1]))
    return jnp.concatenate(first, axis=1), jnp.concatenate(second, axis=1)


def from_planes(first, second):
    low = lax.broadcasted_iota(jnp.int32, (first.shape[0], 128), 1) < PLANE
    tiles = []
    for g in range(first.shape[1] // 128):
        one = first[:, 128 * g : 128 * g + 128]
        two = second[:, 128 * g : 128 * g + 128]
        tiles.append(jnp.where(low, one, pltpu.roll(two, PLANE, 1)))
        tiles.append(jnp.where(low, pltpu.roll(one, PLANE, 1), two))
    return tiles


SHIFTS = [(a, b, c) for a in (-1, 0, 1) for b in (-1, 0, 1) for c in (-1, 0, 1)]


def fill_slot_rows(near_ref, rows_ref, bricks):
    lane = lax.broadcasted_iota(jnp.int32, (1, bricks * PLANE), 1)
    brick = lane // PLANE
    for d, shift in enumerate(SHIFTS):
        if shift == (0, 0, 0):
            rows_ref[d : d + 1, :] = brick * PLANE
            continue
        j = DIRECTIONS.index(shift)
        found = jnp.full(lane.shape, -(1 << 20), jnp.int32)
        for n in range(bricks):
            chosen = near_ref[n, j]
            row = jnp.where(chosen >= 0, lax.rem(chosen, bricks) * PLANE, -(1 << 20))
            found = jnp.where(brick == n, row, found)
        rows_ref[d : d + 1, :] = found


def slot_rows(rows_ref, dx):
    rows = {}
    for d, (a, b, c) in enumerate(SHIFTS):
        if a == dx:
            rows[b, c] = rows_ref[d : d + 1, :]
    return rows


def selection(rows, b, c, bricks):
    size = bricks * PLANE
    lane = lax.broadcasted_iota(jnp.int32, (1, size), 1)
    y = ((lane >> 3) & 7) + (b - 1)
    z = (lane & 7) + (c - 1)
    out_y = (y < 0) | (y > 7)
    out_z = (z < 0) | (z > 7)
    base = rows[0, 0]
    if b != 1:
        base = jnp.where(out_y, rows[b - 1, 0], base)
    if c != 1:
        base = jnp.where(out_z, rows[0, c - 1], base)
    if b != 1 and c != 1:
        base = jnp.where(out_y & out_z, rows[b - 1, c - 1], base)
    source = base + (y & 7) * 8 + (z & 7)
    row = lax.broadcasted_iota(jnp.int32, (size, size), 0)
    return jnp.where(row == source, 1.0, 0.0).astype(BF)


def dot(x, y):
    return lax.dot_general(x, y, (((1,), (0,)), ((), ())), preferred_element_type=F32)


def dot_t(x, y):
    return lax.dot_general(x, y, (((1,), (1,)), ((), ())), preferred_element_type=F32)


def stage_kernel(
    feats_ref, occ_ref, near_ref, cot_ref, weight_ref, bias_ref,
    low_ref, high_ref, rows_ref, x_ref, keep_ref, cot_out_ref, weight_out_ref, bias_out_ref,
    near_held_ref, sems,
):
    pairs = (
        (near_ref, near_held_ref), (occ_ref, keep_ref), (feats_ref, x_ref), (cot_ref, cot_out_ref),
        (weight_ref, weight_out_ref), (bias_ref, bias_out_ref),
    )
    copies = [pltpu.make_async_copy(a, b, sems.at[i]) for i, (a, b) in enumerate(pairs)]
    for copy in copies:
        copy.start()
    bricks, _, voxels = x_ref.shape
    copies[0].wait()
    fill_slot_rows(near_held_ref, rows_ref, bricks)
    copies[1].wait()
    copies[2].wait()
    keep = keep_ref[...].astype(F32)
    for i, (ref, start) in enumerate(((low_ref, 0), (high_ref, voxels - 128))):
        at = slice(start, start + 128)
        tiles = [x_ref[m, :, at].astype(F32) * keep[m : m + 1, at] for m in range(bricks)]
        ref[...] = to_planes(tiles)[i].astype(BF)
    for copy in copies[3:]:
        copy.wait()


def ahead_weights(weight_ref, ahead_ref):
    channels = weight_ref.shape[1]
    for r in range(3):
        blocks = [weight_ref[9 * (2 - r) + k].astype(F32) for k in range(9)]
        ahead_ref[channels * r : channels * (r + 1), :] = jnp.concatenate(blocks, axis=1).astype(BF)


def back_weights(weight_ref, back_ref):
    channels = weight_ref.shape[1]
    for r in range(3):
        blocks = [weight_ref[9 * r + 8 - k].astype(F32).T for k in range(9)]
        back_ref[channels * r : channels * (r + 1), :] = jnp.concatenate(blocks, axis=1).astype(BF)


def shifted(planes_ref, moved_ref, rows_ref, bricks, channels):
    rows = slot_rows(rows_ref, 0)
    count = planes_ref.shape[0]
    flat = planes_ref[...].reshape(count * channels, bricks * PLANE)
    for b in range(3):
        for c in range(3):
            k = 3 * b + c
            if k == 4:
                part = flat
            else:
                part = dot(flat, selection(rows, b, c, bricks)).astype(BF)
            moved_ref[:, channels * k : channels * (k + 1), :] = part.reshape(
                count, channels, bricks * PLANE
            )


def shifted_face(face, rows_ref, dx, bricks):
    rows = slot_rows(rows_ref, dx)
    parts = []
    for b in range(3):
        for c in range(3):
            parts.append(dot(face, selection(rows, b, c, bricks)).astype(BF))
    return jnp.concatenate(parts, axis=0)


def inner_kernel(
    rows_ref, feats_ref, cot_ref, occ_ref, weight_ref, bias_ref,
    moved_ref, pre_ref, cot2_ref, occ2_ref, ahead_ref, planes_ref, total_ref,
):
    bricks, channels, voxels = feats_ref.shape
    keep = occ_ref[...].astype(F32)
    for t in range(voxels // 128):
        at = slice(128 * t, 128 * t + 128)
        kept = [jnp.broadcast_to(keep[m : m + 1, at], (channels, 128)) for m in range(bricks)]
        first, second = to_planes([feats_ref[m, :, at].astype(F32) * kept[m] for m in range(bricks)])
        planes_ref[2 * t] = first.astype(BF)
        planes_ref[2 * t + 1] = second.astype(BF)
        first, second = to_planes([cot_ref[m, :, at].astype(F32) * kept[m] for m in range(bricks)])
        cot2_ref[2 * t] = first.astype(BF)
        cot2_ref[2 * t + 1] = second.astype(BF)
        first, second = to_planes([kept[m][:8] for m in range(bricks)])
        occ2_ref[2 * t] = first
        occ2_ref[2 * t + 1] = second
    shifted(planes_ref, moved_ref, rows_ref, bricks, channels)
    ahead_weights(weight_ref, ahead_ref)
    count = planes_ref.shape[0]
    at = (channels, channels)
    same = lax.broadcasted_iota(jnp.int32, at, 0) == lax.broadcasted_iota(jnp.int32, at, 1)
    column = jnp.sum(jnp.where(same, bias_ref[...], 0.0), axis=1, keepdims=True)
    start = jnp.broadcast_to(column, (channels, bricks * PLANE))
    for x in range(count + 2):
        total_ref[channels * x : channels * (x + 1), :] = start
    for x in range(count):
        at = slice(channels * x, channels * (x + 3))
        total_ref[at, :] += dot(ahead_ref[...], moved_ref[x])
    pre_ref[...] = total_ref[channels : channels * (count + 1), :].reshape(pre_ref.shape)


def outer_kernel(
    rows_ref, low_ref, high_ref, moved_ref, pre_ref, cot2_ref, occ2_ref, weight_ref,
    result_ref, grad_ref, terms_ref, padded_ref,
):
    count, channels, lanes = pre_ref.shape
    bricks = lanes // PLANE
    moved_low = shifted_face(low_ref[...], rows_ref, -1, bricks)
    moved_high = shifted_face(high_ref[...], rows_ref, 1, bricks)
    add_low = dot(weight_ref[2 * channels : 3 * channels, :], moved_low)
    add_high = dot(weight_ref[0:channels, :], moved_high)
    padded_ref[0:channels, :] = jnp.zeros((channels, lanes), BF)
    padded_ref[channels * (count + 1) :, :] = jnp.zeros((channels, lanes), BF)
    bias = jnp.zeros((channels, lanes), F32)
    for x in range(count):
        pre = pre_ref[x]
        if x == 0:
            pre = pre + add_low
        if x == count - 1:
            pre = pre + add_high
        keep = jnp.broadcast_to(occ2_ref[x][0:1], (channels, lanes))
        sig = jax.nn.sigmoid(pre)
        masked = moved_ref[x, 4 * channels : 5 * channels, :].astype(F32)
        result_ref[x] = (masked + keep * pre * sig).astype(BF)
        grad = (cot2_ref[x].astype(F32) * sig * (1.0 + pre * (1.0 - sig))).astype(BF)
        grad_ref[x] = grad
        padded_ref[channels * (x + 1) : channels * (x + 2), :] = grad
        bias = bias + grad.astype(F32)
    terms = dot_t(padded_ref[0 : 3 * channels, :], moved_ref[0])
    for x in range(1, count):
        terms = terms + dot_t(padded_ref[channels * x : channels * (x + 3), :], moved_ref[x])
    width = 9 * channels
    terms_ref[:, 0:width] = terms
    terms_ref[2 * channels : 3 * channels, 0:width] += dot_t(grad_ref[0], moved_low)
    terms_ref[0:channels, 0:width] += dot_t(grad_ref[count - 1], moved_high)
    spare = terms_ref.shape[1] - width
    terms_ref[channels:, width:] = jnp.zeros((2 * channels, spare), F32)
    terms_ref[0:channels, width:] = jnp.sum(bias, axis=1, keepdims=True) * spread(spare)


def spread(count):
    return 1.0 + lax.broadcasted_iota(jnp.int32, (1, count), 1).astype(F32) * (1.0 / count)


def first_sum_kernel(mine_ref, other_ref, grad_ref, out_ref, low_ref, high_ref):
    out_ref[...] = (mine_ref[...] + other_ref[...].astype(F32)).astype(BF)
    low_ref[...] = grad_ref[0]
    high_ref[...] = grad_ref[grad_ref.shape[0] - 1]


def sum_kernel(mine_ref, other_ref, *refs):
    out_ref = refs[-1]
    out_ref[...] = (mine_ref[...].astype(F32) + other_ref[...].astype(F32)).astype(out_ref.dtype)


def back_inner_kernel(
    rows_ref, grad_ref, result2_ref, weight_ref, after_ref,
    result_ref, total_ref, back_ref, moved_ref,
):
    count, channels, lanes = grad_ref.shape
    bricks = lanes // PLANE
    back_weights(weight_ref, back_ref)
    shifted(grad_ref, moved_ref, rows_ref, bricks, channels)
    total_ref[...] = jnp.zeros(total_ref.shape, F32)
    for x in range(count):
        at = slice(channels * x, channels * (x + 3))
        total_ref[at, :] += dot(back_ref[...], moved_ref[x])
    for t in range(count // 2):
        out = from_planes(result2_ref[2 * t].astype(F32), result2_ref[2 * t + 1].astype(F32))
        for m in range(bricks):
            result_ref[m, :, 128 * t : 128 * t + 128] = out[m].astype(BF)


def back_outer_kernel(
    rows_ref, low_ref, high_ref, total_ref, cot_ref, occ_ref, weight_ref, after_ref,
    in_grad_ref, done_ref,
):
    bricks, channels, voxels = cot_ref.shape
    count = voxels // PLANE
    done_ref[...] = jnp.zeros(done_ref.shape, F32)
    moved_low = shifted_face(low_ref[...], rows_ref, -1, bricks)
    moved_high = shifted_face(high_ref[...], rows_ref, 1, bricks)
    add_low = dot(weight_ref[2 * channels : 3 * channels, :], moved_low)
    add_high = dot(weight_ref[0:channels, :], moved_high)
    keep = occ_ref[...].astype(F32)
    for t in range(count // 2):
        at = slice(128 * t, 128 * t + 128)
        first = total_ref[channels * (2 * t + 1) : channels * (2 * t + 2), :]
        second = total_ref[channels * (2 * t + 2) : channels * (2 * t + 3), :]
        if t == 0:
            first = first + add_low
        if t == count // 2 - 1:
            second = second + add_high
        back = from_planes(first, second)
        for m in range(bricks):
            in_grad_ref[m, :, at] = (
                keep[m : m + 1, at] * (cot_ref[m, :, at].astype(F32) + back[m])
            ).astype(BF)


def final_kernel(normaliser, core_ref, mine_ref, other_ref, weight_ref, bias_ref, whole_ref):
    half, columns = mine_ref.shape
    channels = weight_ref.shape[1]
    core = core_ref[0]
    whole_ref[pl.ds(core * half, half), :] = mine_ref[...]
    whole_ref[pl.ds((1 - core) * half, half), :] = other_ref[...]
    for r in range(3):
        rows = slice(channels * r, channels * (r + 1))
        for t in range(columns // 128):
            tile = whole_ref[rows, 128 * t : 128 * t + 128] * normaliser
            weight_ref[9 * (2 - r) + 2 * t] = tile[:, :channels]
            if 2 * t + 1 < 9:
                weight_ref[9 * (2 - r) + 2 * t + 1] = pltpu.roll(tile, 128 - channels, 1)[:, :channels]
            elif r == 0:
                copies = pltpu.roll(tile, 128 - channels, 1)[:, :channels]
                copies = copies / (spread(channels) * channels)
                column = jnp.sum(copies, axis=1, keepdims=True)
                at = (channels, channels)
                same = lax.broadcasted_iota(jnp.int32, at, 0) == lax.broadcasted_iota(jnp.int32, at, 1)
                bias_ref[...] = jnp.sum(jnp.where(same, column, 0.0), axis=0, keepdims=True)


def call(body, outs, ins, scratch=(), flops=0):
    shapes = [jax.ShapeDtypeStruct(shape, dtype) for shape, dtype in outs]
    moved = sum(math.prod(s.shape) * s.dtype.itemsize for s in shapes)
    moved += sum(math.prod(x.shape) * x.dtype.itemsize for _, x in ins)
    return pl.pallas_call(
        body,
        out_shape=shapes,
        in_specs=[spec for spec, _ in ins],
        out_specs=[VMEM] * len(shapes),
        scratch_shapes=list(scratch),
        compiler_params=pltpu.CompilerParams(vmem_limit_bytes=32 << 20),
        cost_estimate=pl.CostEstimate(flops=flops, bytes_accessed=moved, transcendentals=0),
    )(*[pltpu.with_memory_space_constraint(x, pltpu.HBM) if s is HBM else x for s, x in ins])


def exchange_faces(low, high):
    size = lax.axis_size("space")
    up = [(i, (i + 1) % size) for i in range(size)]
    down = [(j, i) for i, j in up]
    return lax.ppermute(high, "space", up), lax.ppermute(low, "space", down)


def on_device(feats, cotangent, weight, bias, neighbours, occupancy):
    x, cot, near, occ = feats[0], cotangent[0], neighbours[0], occupancy[0]
    bricks, channels, voxels = x.shape
    count, lanes = voxels // PLANE, bricks * PLANE
    width = 9 * channels
    plane = ((channels, lanes), BF)
    low, high, rows, x, occ, cot, weight, bias = call(
        stage_kernel,
        [
            plane, plane, ((32, lanes), jnp.int32), (x.shape, BF), (occ.shape, jnp.int32), (x.shape, BF),
            (weight.shape, BF), ((1, channels), F32),
        ],
        [(HBM, x), (HBM, occ), (HBM, near), (HBM, cot), (HBM, weight), (HBM, bias[None])],
        [pltpu.SMEM(near.shape, jnp.int32), pltpu.SemaphoreType.DMA((6,))],
    )
    from_low, from_high = exchange_faces(low, high)
    moved, pre, cot2, occ2, ahead = call(
        inner_kernel,
        [
            ((count, width, lanes), BF),
            ((count, channels, lanes), F32),
            ((count, channels, lanes), BF),
            ((count, 8, lanes), F32),
            ((3 * channels, width), BF),
        ],
        [(VMEM, rows), (VMEM, x), (VMEM, cot), (VMEM, occ), (VMEM, weight), (VMEM, bias)],
        [
            pltpu.VMEM((count, channels, lanes), BF),
            pltpu.VMEM((channels * (count + 2), lanes), F32),
        ],
        flops=2 * 27 * channels * channels * bricks * voxels,
    )
    result2, grad, terms = call(
        outer_kernel,
        [
            ((count, channels, lanes), BF),
            ((count, channels, lanes), BF),
            ((3 * channels, width + 64), F32),
        ],
        [
            (VMEM, rows), (VMEM, from_low), (VMEM, from_high), (VMEM, moved), (VMEM, pre),
            (VMEM, cot2), (VMEM, occ2), (VMEM, ahead),
        ],
        [pltpu.VMEM((channels * (count + 2), lanes), BF)],
        flops=2 * 27 * channels * channels * bricks * voxels,
    )
    axes = ("space", "rep")
    devices = lax.axis_size("space") * lax.axis_size("rep")
    core = lax.axis_index("rep") % 2
    half = 3 * channels // 2
    partner = [(i, i ^ 1) for i in range(devices)]
    theirs = lax.dynamic_slice_in_dim(terms, (1 - core) * half, half, 0).astype(BF)
    mine = lax.dynamic_slice_in_dim(terms, core * half, half, 0)
    other = lax.ppermute(theirs, axes, partner)
    sent = ((half, terms.shape[1]), BF)
    mine, low, high = call(
        first_sum_kernel, [sent, plane, plane], [(VMEM, mine), (VMEM, other), (VMEM, grad)]
    )
    bits = [1 << i for i in range(1, (devices).bit_length() - 1)]
    turn = len(bits) // 2
    grad_low = grad_high = total = in_grad = result = None
    rounds = list(zip(bits, bits[turn:] + bits[:turn]))
    for i, steps in enumerate(rounds):
        other = lax.ppermute(mine, axes, [(j, j ^ steps[j % 2]) for j in range(devices)])
        held = []
        if i == 0:
            grad_low, grad_high = exchange_faces(low, high)
            held = [grad_low, grad_high]
        if i == 1:
            result, total, back = call(
                back_inner_kernel,
                [
                    ((bricks, channels, voxels), BF),
                    ((channels * (count + 2), lanes), F32),
                    ((3 * channels, width), BF),
                ],
                [(VMEM, rows), (VMEM, grad), (VMEM, result2), (VMEM, weight), (ANY, mine)],
                [pltpu.VMEM((count, width, lanes), BF)],
                flops=2 * 27 * channels * channels * bricks * voxels,
            )
            held = [total]
        if i == 2:
            in_grad, done = call(
                back_outer_kernel,
                [((bricks, channels, voxels), BF), ((8, 128), F32)],
                [
                    (VMEM, rows), (VMEM, grad_low), (VMEM, grad_high), (VMEM, total), (VMEM, cot),
                    (VMEM, occ), (VMEM, back), (ANY, mine),
                ],
                flops=2 * 6 * channels * channels * bricks * voxels,
            )
            held = [done]
        last = i == len(rounds) - 1
        (mine,) = call(
            sum_kernel,
            [(sent[0], F32 if last else BF)],
            [(VMEM, mine), (VMEM, other)] + [(ANY, h) for h in held],
        )
    other = lax.ppermute(mine, axes, partner)
    normaliser = 1.0 / math.sqrt(
        feats.shape[0] * lax.axis_size("rep") * bricks * lax.axis_size("space") * voxels
    )
    weight_grad, bias_grad = call(
        functools.partial(final_kernel, normaliser),
        [(weight.shape, F32), ((1, channels), F32)],
        [(SMEM, core.astype(jnp.int32)[None]), (VMEM, mine), (VMEM, other)],
        [pltpu.VMEM(terms.shape, F32)],
    )
    return result[None], in_grad[None], weight_grad, bias_grad[0]


def solution(mesh):
    placed = (
        P("rep", "space", None, None),
        P("rep", "space", None, None),
        P(),
        P(),
        P("rep", "space", None),
        P("rep", "space", None),
    )
    return jax.shard_map(
        on_device,
        mesh=mesh,
        in_specs=placed,
        out_specs=(P("rep", "space", None, None), P("rep", "space", None, None), P(), P()),
        check_vma=False,
    )
```

```python
import functools
import math

import jax
import jax.numpy as jnp
from jax import lax
from jax.experimental import pallas as pl
from jax.experimental.pallas import tpu as pltpu
from jax.sharding import PartitionSpec as P

BF, F32 = jnp.bfloat16, jnp.float32
DIRECTIONS = [
    (a, b, c) for a in (-1, 0, 1) for b in (-1, 0, 1) for c in (-1, 0, 1) if (a, b, c) != (0, 0, 0)
]
PLANE = 64
VMEM = pl.BlockSpec(memory_space=pltpu.VMEM)
ANY = pl.BlockSpec(memory_space=pl.ANY)
HBM = pl.BlockSpec(memory_space=pltpu.HBM)
SMEM = pl.BlockSpec(memory_space=pltpu.SMEM)


def to_planes(tiles):
    low = lax.broadcasted_iota(jnp.int32, tiles[0].shape, 1) < PLANE
    turned = [pltpu.roll(tile, PLANE, 1) for tile in tiles]
    first, second = [], []
    for m in range(0, len(tiles), 2):
        first.append(jnp.where(low, tiles[m], turned[m + 1]))
        second.append(jnp.where(low, turned[m], tiles[m + 1]))
    return jnp.concatenate(first, axis=1), jnp.concatenate(second, axis=1)


def from_planes(first, second):
    low = lax.broadcasted_iota(jnp.int32, (first.shape[0], 128), 1) < PLANE
    tiles = []
    for g in range(first.shape[1] // 128):
        one = first[:, 128 * g : 128 * g + 128]
        two = second[:, 128 * g : 128 * g + 128]
        tiles.append(jnp.where(low, one, pltpu.roll(two, PLANE, 1)))
        tiles.append(jnp.where(low, pltpu.roll(one, PLANE, 1), two))
    return tiles


SHIFTS = [(a, b, c) for a in (-1, 0, 1) for b in (-1, 0, 1) for c in (-1, 0, 1)]


def fill_slot_rows(near_ref, rows_ref, bricks):
    lane = lax.broadcasted_iota(jnp.int32, (1, bricks * PLANE), 1)
    brick = lane // PLANE
    for d, shift in enumerate(SHIFTS):
        if shift == (0, 0, 0):
            rows_ref[d : d + 1, :] = brick * PLANE
            continue
        j = DIRECTIONS.index(shift)
        found = jnp.full(lane.shape, -(1 << 20), jnp.int32)
        for n in range(bricks):
            chosen = near_ref[n, j]
            row = jnp.where(chosen >= 0, lax.rem(chosen, bricks) * PLANE, -(1 << 20))
            found = jnp.where(brick == n, row, found)
        rows_ref[d : d + 1, :] = found


def slot_rows(rows_ref, dx):
    rows = {}
    for d, (a, b, c) in enumerate(SHIFTS):
        if a == dx:
            rows[b, c] = rows_ref[d : d + 1, :]
    return rows


def selection(rows, b, c, bricks):
    size = bricks * PLANE
    lane = lax.broadcasted_iota(jnp.int32, (1, size), 1)
    y = ((lane >> 3) & 7) + (b - 1)
    z = (lane & 7) + (c - 1)
    out_y = (y < 0) | (y > 7)
    out_z = (z < 0) | (z > 7)
    base = rows[0, 0]
    if b != 1:
        base = jnp.where(out_y, rows[b - 1, 0], base)
    if c != 1:
        base = jnp.where(out_z, rows[0, c - 1], base)
    if b != 1 and c != 1:
        base = jnp.where(out_y & out_z, rows[b - 1, c - 1], base)
    source = base + (y & 7) * 8 + (z & 7)
    row = lax.broadcasted_iota(jnp.int32, (size, size), 0)
    return jnp.where(row == source, 1.0, 0.0).astype(BF)


def dot(x, y):
    return lax.dot_general(x, y, (((1,), (0,)), ((), ())), preferred_element_type=F32)


def dot_t(x, y):
    return lax.dot_general(x, y, (((1,), (1,)), ((), ())), preferred_element_type=F32)


def store_faces(core_ref, low, high, first_ref, second_ref):
    even = core_ref[0] == 0

    @pl.when(even)
    def _():
        first_ref[...] = high
        second_ref[...] = low

    @pl.when(jnp.logical_not(even))
    def _():
        first_ref[...] = low
        second_ref[...] = high


def load_faces(core_ref, first_ref, second_ref):
    even = core_ref[0] == 0
    first, second = first_ref[...].astype(F32), second_ref[...].astype(F32)
    return jnp.where(even, first, second).astype(BF), jnp.where(even, second, first).astype(BF)


def stage_kernel(
    core_ref, feats_ref, occ_ref, near_ref, cot_ref, weight_ref, bias_ref,
    first_ref, second_ref, rows_ref, x_ref, keep_ref, cot_out_ref, weight_out_ref, bias_out_ref,
    near_held_ref, sems,
):
    pairs = (
        (near_ref, near_held_ref), (occ_ref, keep_ref), (feats_ref, x_ref), (cot_ref, cot_out_ref),
        (weight_ref, weight_out_ref), (bias_ref, bias_out_ref),
    )
    copies = [pltpu.make_async_copy(a, b, sems.at[i]) for i, (a, b) in enumerate(pairs)]
    for copy in copies:
        copy.start()
    bricks, _, voxels = x_ref.shape
    copies[0].wait()
    fill_slot_rows(near_held_ref, rows_ref, bricks)
    copies[1].wait()
    copies[2].wait()
    keep = keep_ref[...].astype(F32)
    faces = []
    for i, start in enumerate((0, voxels - 128)):
        at = slice(start, start + 128)
        tiles = [x_ref[m, :, at].astype(F32) * keep[m : m + 1, at] for m in range(bricks)]
        faces.append(to_planes(tiles)[i].astype(BF))
    store_faces(core_ref, faces[0], faces[1], first_ref, second_ref)
    for copy in copies[3:]:
        copy.wait()


def ahead_weights(weight_ref, ahead_ref):
    channels = weight_ref.shape[1]
    for r in range(3):
        blocks = [weight_ref[9 * (2 - r) + k].astype(F32) for k in range(9)]
        ahead_ref[channels * r : channels * (r + 1), :] = jnp.concatenate(blocks, axis=1).astype(BF)


def back_weights(weight_ref, back_ref):
    channels = weight_ref.shape[1]
    for r in range(3):
        blocks = [weight_ref[9 * r + 8 - k].astype(F32).T for k in range(9)]
        back_ref[channels * r : channels * (r + 1), :] = jnp.concatenate(blocks, axis=1).astype(BF)


def shifted(planes_ref, moved_ref, rows_ref, bricks, channels):
    rows = slot_rows(rows_ref, 0)
    count = planes_ref.shape[0]
    flat = planes_ref[...].reshape(count * channels, bricks * PLANE)
    for b in range(3):
        for c in range(3):
            k = 3 * b + c
            if k == 4:
                part = flat
            else:
                part = dot(flat, selection(rows, b, c, bricks)).astype(BF)
            moved_ref[:, channels * k : channels * (k + 1), :] = part.reshape(
                count, channels, bricks * PLANE
            )


def shifted_face(face, rows_ref, dx, bricks):
    rows = slot_rows(rows_ref, dx)
    parts = []
    for b in range(3):
        for c in range(3):
            parts.append(dot(face, selection(rows, b, c, bricks)).astype(BF))
    return jnp.concatenate(parts, axis=0)


def inner_kernel(
    rows_ref, feats_ref, cot_ref, occ_ref, weight_ref, bias_ref,
    moved_ref, pre_ref, cot2_ref, occ2_ref, ahead_ref, planes_ref, total_ref,
):
    bricks, channels, voxels = feats_ref.shape
    keep = occ_ref[...].astype(F32)
    for t in range(voxels // 128):
        at = slice(128 * t, 128 * t + 128)
        kept = [jnp.broadcast_to(keep[m : m + 1, at], (channels, 128)) for m in range(bricks)]
        first, second = to_planes([feats_ref[m, :, at].astype(F32) * kept[m] for m in range(bricks)])
        planes_ref[2 * t] = first.astype(BF)
        planes_ref[2 * t + 1] = second.astype(BF)
        first, second = to_planes([cot_ref[m, :, at].astype(F32) * kept[m] for m in range(bricks)])
        cot2_ref[2 * t] = first.astype(BF)
        cot2_ref[2 * t + 1] = second.astype(BF)
        first, second = to_planes([kept[m][:8] for m in range(bricks)])
        occ2_ref[2 * t] = first
        occ2_ref[2 * t + 1] = second
    shifted(planes_ref, moved_ref, rows_ref, bricks, channels)
    ahead_weights(weight_ref, ahead_ref)
    count = planes_ref.shape[0]
    at = (channels, channels)
    same = lax.broadcasted_iota(jnp.int32, at, 0) == lax.broadcasted_iota(jnp.int32, at, 1)
    column = jnp.sum(jnp.where(same, bias_ref[...], 0.0), axis=1, keepdims=True)
    start = jnp.broadcast_to(column, (channels, bricks * PLANE))
    for x in range(count + 2):
        total_ref[channels * x : channels * (x + 1), :] = start
    for x in range(count):
        at = slice(channels * x, channels * (x + 3))
        total_ref[at, :] += dot(ahead_ref[...], moved_ref[x])
    pre_ref[...] = total_ref[channels : channels * (count + 1), :].reshape(pre_ref.shape)


def outer_kernel(
    core_ref, rows_ref, first_ref, second_ref, moved_ref, pre_ref, cot2_ref, occ2_ref, weight_ref,
    result_ref, grad_ref, terms_ref, padded_ref,
):
    count, channels, lanes = pre_ref.shape
    bricks = lanes // PLANE
    low, high = load_faces(core_ref, first_ref, second_ref)
    moved_low = shifted_face(low, rows_ref, -1, bricks)
    moved_high = shifted_face(high, rows_ref, 1, bricks)
    add_low = dot(weight_ref[2 * channels : 3 * channels, :], moved_low)
    add_high = dot(weight_ref[0:channels, :], moved_high)
    padded_ref[0:channels, :] = jnp.zeros((channels, lanes), BF)
    padded_ref[channels * (count + 1) :, :] = jnp.zeros((channels, lanes), BF)
    bias = jnp.zeros((channels, lanes), F32)
    for x in range(count):
        pre = pre_ref[x]
        if x == 0:
            pre = pre + add_low
        if x == count - 1:
            pre = pre + add_high
        keep = jnp.broadcast_to(occ2_ref[x][0:1], (channels, lanes))
        sig = jax.nn.sigmoid(pre)
        masked = moved_ref[x, 4 * channels : 5 * channels, :].astype(F32)
        result_ref[x] = (masked + keep * pre * sig).astype(BF)
        grad = (cot2_ref[x].astype(F32) * sig * (1.0 + pre * (1.0 - sig))).astype(BF)
        grad_ref[x] = grad
        padded_ref[channels * (x + 1) : channels * (x + 2), :] = grad
        bias = bias + grad.astype(F32)
    terms = dot_t(padded_ref[0 : 3 * channels, :], moved_ref[0])
    for x in range(1, count):
        terms = terms + dot_t(padded_ref[channels * x : channels * (x + 3), :], moved_ref[x])
    width = 9 * channels
    terms_ref[:, 0:width] = terms
    terms_ref[2 * channels : 3 * channels, 0:width] += dot_t(grad_ref[0], moved_low)
    terms_ref[0:channels, 0:width] += dot_t(grad_ref[count - 1], moved_high)
    spare = terms_ref.shape[1] - width
    terms_ref[channels:, width:] = jnp.zeros((2 * channels, spare), F32)
    terms_ref[0:channels, width:] = jnp.sum(bias, axis=1, keepdims=True) * spread(spare)


def spread(count):
    return 1.0 + lax.broadcasted_iota(jnp.int32, (1, count), 1).astype(F32) * (1.0 / count)


def first_sum_kernel(core_ref, mine_ref, other_ref, grad_ref, out_ref, first_ref, second_ref):
    out_ref[...] = (mine_ref[...] + other_ref[...].astype(F32)).astype(BF)
    last = grad_ref.shape[0] - 1
    store_faces(core_ref, grad_ref[0], grad_ref[last], first_ref, second_ref)


def sum_kernel(mine_ref, other_ref, *refs):
    out_ref = refs[-1]
    out_ref[...] = (mine_ref[...].astype(F32) + other_ref[...].astype(F32)).astype(out_ref.dtype)


def back_inner_kernel(
    rows_ref, grad_ref, result2_ref, weight_ref, after_ref,
    result_ref, total_ref, back_ref, moved_ref,
):
    count, channels, lanes = grad_ref.shape
    bricks = lanes // PLANE
    back_weights(weight_ref, back_ref)
    shifted(grad_ref, moved_ref, rows_ref, bricks, channels)
    total_ref[...] = jnp.zeros(total_ref.shape, F32)
    for x in range(count):
        at = slice(channels * x, channels * (x + 3))
        total_ref[at, :] += dot(back_ref[...], moved_ref[x])
    for t in range(count // 2):
        out = from_planes(result2_ref[2 * t].astype(F32), result2_ref[2 * t + 1].astype(F32))
        for m in range(bricks):
            result_ref[m, :, 128 * t : 128 * t + 128] = out[m].astype(BF)


def back_outer_kernel(
    core_ref, rows_ref, first_ref, second_ref, total_ref, cot_ref, occ_ref, weight_ref, after_ref,
    in_grad_ref, done_ref,
):
    bricks, channels, voxels = cot_ref.shape
    count = voxels // PLANE
    done_ref[...] = jnp.zeros(done_ref.shape, F32)
    low, high = load_faces(core_ref, first_ref, second_ref)
    moved_low = shifted_face(low, rows_ref, -1, bricks)
    moved_high = shifted_face(high, rows_ref, 1, bricks)
    add_low = dot(weight_ref[2 * channels : 3 * channels, :], moved_low)
    add_high = dot(weight_ref[0:channels, :], moved_high)
    keep = occ_ref[...].astype(F32)
    for t in range(count // 2):
        at = slice(128 * t, 128 * t + 128)
        first = total_ref[channels * (2 * t + 1) : channels * (2 * t + 2), :]
        second = total_ref[channels * (2 * t + 2) : channels * (2 * t + 3), :]
        if t == 0:
            first = first + add_low
        if t == count // 2 - 1:
            second = second + add_high
        back = from_planes(first, second)
        for m in range(bricks):
            in_grad_ref[m, :, at] = (
                keep[m : m + 1, at] * (cot_ref[m, :, at].astype(F32) + back[m])
            ).astype(BF)


def final_kernel(normaliser, core_ref, mine_ref, other_ref, weight_ref, bias_ref, whole_ref):
    half, columns = mine_ref.shape
    channels = weight_ref.shape[1]
    core = core_ref[0]
    whole_ref[pl.ds(core * half, half), :] = mine_ref[...]
    whole_ref[pl.ds((1 - core) * half, half), :] = other_ref[...]
    for r in range(3):
        rows = slice(channels * r, channels * (r + 1))
        for t in range(columns // 128):
            tile = whole_ref[rows, 128 * t : 128 * t + 128] * normaliser
            weight_ref[9 * (2 - r) + 2 * t] = tile[:, :channels]
            if 2 * t + 1 < 9:
                weight_ref[9 * (2 - r) + 2 * t + 1] = pltpu.roll(tile, 128 - channels, 1)[:, :channels]
            elif r == 0:
                copies = pltpu.roll(tile, 128 - channels, 1)[:, :channels]
                copies = copies / (spread(channels) * channels)
                column = jnp.sum(copies, axis=1, keepdims=True)
                at = (channels, channels)
                same = lax.broadcasted_iota(jnp.int32, at, 0) == lax.broadcasted_iota(jnp.int32, at, 1)
                bias_ref[...] = jnp.sum(jnp.where(same, column, 0.0), axis=0, keepdims=True)


def call(body, outs, ins, scratch=(), flops=0):
    shapes = [jax.ShapeDtypeStruct(shape, dtype) for shape, dtype in outs]
    moved = sum(math.prod(s.shape) * s.dtype.itemsize for s in shapes)
    moved += sum(math.prod(x.shape) * x.dtype.itemsize for _, x in ins)
    return pl.pallas_call(
        body,
        out_shape=shapes,
        in_specs=[spec for spec, _ in ins],
        out_specs=[VMEM] * len(shapes),
        scratch_shapes=list(scratch),
        compiler_params=pltpu.CompilerParams(vmem_limit_bytes=32 << 20),
        cost_estimate=pl.CostEstimate(flops=flops, bytes_accessed=moved, transcendentals=0),
    )(*[pltpu.with_memory_space_constraint(x, pltpu.HBM) if s is HBM else x for s, x in ins])


def exchange_faces(first, second):
    spaces, reps = lax.axis_size("space"), lax.axis_size("rep")
    pairs = []
    for space in range(spaces):
        for rep in range(reps):
            step = 1 if rep % 2 == 0 else -1
            there, to = space + step, rep
            if not 0 <= there < spaces:
                there, to = space, rep ^ 1
            pairs.append((space * reps + rep, there * reps + to))
    back = [(j, i) for i, j in pairs]
    axes = ("space", "rep")
    return lax.ppermute(first, axes, pairs), lax.ppermute(second, axes, back)


def on_device(feats, cotangent, weight, bias, neighbours, occupancy):
    x, cot, near, occ = feats[0], cotangent[0], neighbours[0], occupancy[0]
    bricks, channels, voxels = x.shape
    count, lanes = voxels // PLANE, bricks * PLANE
    width = 9 * channels
    plane = ((channels, lanes), BF)
    core = (lax.axis_index("rep") % 2).astype(jnp.int32)
    cores = core[None]
    first, second, rows, x, occ, cot, weight, bias = call(
        stage_kernel,
        [
            plane, plane, ((32, lanes), jnp.int32), (x.shape, BF), (occ.shape, jnp.int32), (x.shape, BF),
            (weight.shape, BF), ((1, channels), F32),
        ],
        [(SMEM, cores), (HBM, x), (HBM, occ), (HBM, near), (HBM, cot), (HBM, weight), (HBM, bias[None])],
        [pltpu.SMEM(near.shape, jnp.int32), pltpu.SemaphoreType.DMA((6,))],
    )
    first, second = exchange_faces(first, second)
    moved, pre, cot2, occ2, ahead = call(
        inner_kernel,
        [
            ((count, width, lanes), BF),
            ((count, channels, lanes), F32),
            ((count, channels, lanes), BF),
            ((count, 8, lanes), F32),
            ((3 * channels, width), BF),
        ],
        [(VMEM, rows), (VMEM, x), (VMEM, cot), (VMEM, occ), (VMEM, weight), (VMEM, bias)],
        [
            pltpu.VMEM((count, channels, lanes), BF),
            pltpu.VMEM((channels * (count + 2), lanes), F32),
        ],
        flops=2 * 27 * channels * channels * bricks * voxels,
    )
    result2, grad, terms = call(
        outer_kernel,
        [
            ((count, channels, lanes), BF),
            ((count, channels, lanes), BF),
            ((3 * channels, width + 64), F32),
        ],
        [
            (SMEM, cores), (VMEM, rows), (VMEM, first), (VMEM, second), (VMEM, moved), (VMEM, pre),
            (VMEM, cot2), (VMEM, occ2), (VMEM, ahead),
        ],
        [pltpu.VMEM((channels * (count + 2), lanes), BF)],
        flops=2 * 27 * channels * channels * bricks * voxels,
    )
    axes = ("space", "rep")
    devices = lax.axis_size("space") * lax.axis_size("rep")
    half = 3 * channels // 2
    partner = [(i, i ^ 1) for i in range(devices)]
    theirs = lax.dynamic_slice_in_dim(terms, (1 - core) * half, half, 0).astype(BF)
    mine = lax.dynamic_slice_in_dim(terms, core * half, half, 0)
    other = lax.ppermute(theirs, axes, partner)
    sent = ((half, terms.shape[1]), BF)
    mine, first, second = call(
        first_sum_kernel,
        [sent, plane, plane],
        [(SMEM, cores), (VMEM, mine), (VMEM, other), (VMEM, grad)],
    )
    bits = [1 << i for i in range(1, (devices).bit_length() - 1)]
    turn = len(bits) // 2
    total = in_grad = result = None
    rounds = list(zip(bits, bits[turn:] + bits[:turn]))
    for i, steps in enumerate(rounds):
        other = lax.ppermute(mine, axes, [(j, j ^ steps[j % 2]) for j in range(devices)])
        held = []
        if i == 0:
            first, second = exchange_faces(first, second)
            held = [first, second]
        if i == 1:
            result, total, back = call(
                back_inner_kernel,
                [
                    ((bricks, channels, voxels), BF),
                    ((channels * (count + 2), lanes), F32),
                    ((3 * channels, width), BF),
                ],
                [(VMEM, rows), (VMEM, grad), (VMEM, result2), (VMEM, weight), (ANY, mine)],
                [pltpu.VMEM((count, width, lanes), BF)],
                flops=2 * 27 * channels * channels * bricks * voxels,
            )
            held = [total]
        if i == 2:
            in_grad, done = call(
                back_outer_kernel,
                [((bricks, channels, voxels), BF), ((8, 128), F32)],
                [
                    (SMEM, cores), (VMEM, rows), (VMEM, first), (VMEM, second), (VMEM, total), (VMEM, cot),
                    (VMEM, occ), (VMEM, back), (ANY, mine),
                ],
                flops=2 * 6 * channels * channels * bricks * voxels,
            )
            held = [done]
        last = i == len(rounds) - 1
        (mine,) = call(
            sum_kernel,
            [(sent[0], F32 if last else BF)],
            [(VMEM, mine), (VMEM, other)] + [(ANY, h) for h in held],
        )
    other = lax.ppermute(mine, axes, partner)
    normaliser = 1.0 / math.sqrt(
        feats.shape[0] * lax.axis_size("rep") * bricks * lax.axis_size("space") * voxels
    )
    weight_grad, bias_grad = call(
        functools.partial(final_kernel, normaliser),
        [(weight.shape, F32), ((1, channels), F32)],
        [(SMEM, cores), (VMEM, mine), (VMEM, other)],
        [pltpu.VMEM(terms.shape, F32)],
    )
    return result[None], in_grad[None], weight_grad, bias_grad[0]


def solution(mesh):
    placed = (
        P("rep", "space", None, None),
        P("rep", "space", None, None),
        P(),
        P(),
        P("rep", "space", None),
        P("rep", "space", None),
    )
    return jax.shard_map(
        on_device,
        mesh=mesh,
        in_specs=placed,
        out_specs=(P("rep", "space", None, None), P("rep", "space", None, None), P(), P()),
        check_vma=False,
    )
```

```python
import functools
import math

import jax
import jax.numpy as jnp
from jax import lax
from jax.experimental import pallas as pl
from jax.experimental.pallas import tpu as pltpu
from jax.sharding import PartitionSpec as P

BF, F32 = jnp.bfloat16, jnp.float32
DIRECTIONS = [
    (a, b, c) for a in (-1, 0, 1) for b in (-1, 0, 1) for c in (-1, 0, 1) if (a, b, c) != (0, 0, 0)
]
PLANE = 64
VMEM = pl.BlockSpec(memory_space=pltpu.VMEM)
ANY = pl.BlockSpec(memory_space=pl.ANY)
HBM = pl.BlockSpec(memory_space=pltpu.HBM)
SMEM = pl.BlockSpec(memory_space=pltpu.SMEM)


def to_planes(tiles):
    low = lax.broadcasted_iota(jnp.int32, tiles[0].shape, 1) < PLANE
    turned = [pltpu.roll(tile, PLANE, 1) for tile in tiles]
    first, second = [], []
    for m in range(0, len(tiles), 2):
        first.append(jnp.where(low, tiles[m], turned[m + 1]))
        second.append(jnp.where(low, turned[m], tiles[m + 1]))
    return jnp.concatenate(first, axis=1), jnp.concatenate(second, axis=1)


def from_planes(first, second):
    low = lax.broadcasted_iota(jnp.int32, (first.shape[0], 128), 1) < PLANE
    tiles = []
    for g in range(first.shape[1] // 128):
        one = first[:, 128 * g : 128 * g + 128]
        two = second[:, 128 * g : 128 * g + 128]
        tiles.append(jnp.where(low, one, pltpu.roll(two, PLANE, 1)))
        tiles.append(jnp.where(low, pltpu.roll(one, PLANE, 1), two))
    return tiles


SHIFTS = [(a, b, c) for a in (-1, 0, 1) for b in (-1, 0, 1) for c in (-1, 0, 1)]


def fill_slot_rows(near_ref, rows_ref, bricks):
    lane = lax.broadcasted_iota(jnp.int32, (1, bricks * PLANE), 1)
    brick = lane // PLANE
    for d, shift in enumerate(SHIFTS):
        if shift == (0, 0, 0):
            rows_ref[d : d + 1, :] = brick * PLANE
            continue
        j = DIRECTIONS.index(shift)
        found = jnp.full(lane.shape, -(1 << 20), jnp.int32)
        for n in range(bricks):
            chosen = near_ref[n, j]
            row = jnp.where(chosen >= 0, lax.rem(chosen, bricks) * PLANE, -(1 << 20))
            found = jnp.where(brick == n, row, found)
        rows_ref[d : d + 1, :] = found


def slot_rows(rows_ref, dx):
    rows = {}
    for d, (a, b, c) in enumerate(SHIFTS):
        if a == dx:
            rows[b, c] = rows_ref[d : d + 1, :]
    return rows


def selection(rows, b, c, bricks):
    size = bricks * PLANE
    lane = lax.broadcasted_iota(jnp.int32, (1, size), 1)
    y = ((lane >> 3) & 7) + (b - 1)
    z = (lane & 7) + (c - 1)
    out_y = (y < 0) | (y > 7)
    out_z = (z < 0) | (z > 7)
    base = rows[0, 0]
    if b != 1:
        base = jnp.where(out_y, rows[b - 1, 0], base)
    if c != 1:
        base = jnp.where(out_z, rows[0, c - 1], base)
    if b != 1 and c != 1:
        base = jnp.where(out_y & out_z, rows[b - 1, c - 1], base)
    source = base + (y & 7) * 8 + (z & 7)
    row = lax.broadcasted_iota(jnp.int32, (size, size), 0)
    return jnp.where(row == source, 1.0, 0.0).astype(BF)


def dot(x, y):
    return lax.dot_general(x, y, (((1,), (0,)), ((), ())), preferred_element_type=F32)


def dot_t(x, y):
    return lax.dot_general(x, y, (((1,), (1,)), ((), ())), preferred_element_type=F32)


def store_faces(core_ref, low, high, first_ref, second_ref):
    even = core_ref[0] == 0

    @pl.when(even)
    def _():
        first_ref[...] = high
        second_ref[...] = low

    @pl.when(jnp.logical_not(even))
    def _():
        first_ref[...] = low
        second_ref[...] = high


def load_faces(core_ref, first_ref, second_ref):
    even = core_ref[0] == 0
    first, second = first_ref[...].astype(F32), second_ref[...].astype(F32)
    return jnp.where(even, first, second).astype(BF), jnp.where(even, second, first).astype(BF)


def stage_kernel(
    core_ref, feats_ref, occ_ref, near_ref, cot_ref, weight_ref, bias_ref,
    first_ref, second_ref, rows_ref, x_ref, keep_ref, cot_out_ref, weight_out_ref, bias_out_ref,
    near_held_ref, sems,
):
    pairs = (
        (near_ref, near_held_ref), (occ_ref, keep_ref), (feats_ref, x_ref), (cot_ref, cot_out_ref),
        (weight_ref, weight_out_ref), (bias_ref, bias_out_ref),
    )
    copies = [pltpu.make_async_copy(a, b, sems.at[i]) for i, (a, b) in enumerate(pairs)]
    for copy in copies:
        copy.start()
    bricks, _, voxels = x_ref.shape
    copies[0].wait()
    fill_slot_rows(near_held_ref, rows_ref, bricks)
    copies[1].wait()
    copies[2].wait()
    keep = keep_ref[...].astype(F32)
    faces = []
    for i, start in enumerate((0, voxels - 128)):
        at = slice(start, start + 128)
        tiles = [x_ref[m, :, at].astype(F32) * keep[m : m + 1, at] for m in range(bricks)]
        faces.append(to_planes(tiles)[i].astype(BF))
    store_faces(core_ref, faces[0], faces[1], first_ref, second_ref)
    for copy in copies[3:]:
        copy.wait()


def ahead_weights(weight_ref, ahead_ref):
    channels = weight_ref.shape[1]
    for r in range(3):
        blocks = [weight_ref[9 * (2 - r) + k].astype(F32) for k in range(9)]
        ahead_ref[channels * r : channels * (r + 1), :] = jnp.concatenate(blocks, axis=1).astype(BF)


def back_weights(weight_ref, back_ref):
    channels = weight_ref.shape[1]
    for r in range(3):
        blocks = [weight_ref[9 * r + 8 - k].astype(F32).T for k in range(9)]
        back_ref[channels * r : channels * (r + 1), :] = jnp.concatenate(blocks, axis=1).astype(BF)


def shifted(planes_ref, moved_ref, rows_ref, bricks, channels):
    rows = slot_rows(rows_ref, 0)
    count = planes_ref.shape[0]
    flat = planes_ref[...].reshape(count * channels, bricks * PLANE)
    for b in range(3):
        for c in range(3):
            k = 3 * b + c
            if k == 4:
                part = flat
            else:
                part = dot(flat, selection(rows, b, c, bricks)).astype(BF)
            moved_ref[:, channels * k : channels * (k + 1), :] = part.reshape(
                count, channels, bricks * PLANE
            )


def shifted_face(face, rows_ref, dx, bricks):
    rows = slot_rows(rows_ref, dx)
    parts = []
    for b in range(3):
        for c in range(3):
            parts.append(dot(face, selection(rows, b, c, bricks)).astype(BF))
    return jnp.concatenate(parts, axis=0)


def inner_kernel(
    rows_ref, feats_ref, cot_ref, occ_ref, weight_ref, bias_ref,
    moved_ref, pre_ref, cot2_ref, occ2_ref, ahead_ref, planes_ref, total_ref,
):
    bricks, channels, voxels = feats_ref.shape
    keep = occ_ref[...].astype(F32)
    for t in range(voxels // 128):
        at = slice(128 * t, 128 * t + 128)
        kept = [jnp.broadcast_to(keep[m : m + 1, at], (channels, 128)) for m in range(bricks)]
        first, second = to_planes([feats_ref[m, :, at].astype(F32) * kept[m] for m in range(bricks)])
        planes_ref[2 * t] = first.astype(BF)
        planes_ref[2 * t + 1] = second.astype(BF)
        first, second = to_planes([cot_ref[m, :, at].astype(F32) * kept[m] for m in range(bricks)])
        cot2_ref[2 * t] = first.astype(BF)
        cot2_ref[2 * t + 1] = second.astype(BF)
        first, second = to_planes([kept[m][:8] for m in range(bricks)])
        occ2_ref[2 * t] = first
        occ2_ref[2 * t + 1] = second
    shifted(planes_ref, moved_ref, rows_ref, bricks, channels)
    ahead_weights(weight_ref, ahead_ref)
    count = planes_ref.shape[0]
    at = (channels, channels)
    same = lax.broadcasted_iota(jnp.int32, at, 0) == lax.broadcasted_iota(jnp.int32, at, 1)
    column = jnp.sum(jnp.where(same, bias_ref[...], 0.0), axis=1, keepdims=True)
    start = jnp.broadcast_to(column, (channels, bricks * PLANE))
    for x in range(count + 2):
        total_ref[channels * x : channels * (x + 1), :] = start
    for x in range(count):
        at = slice(channels * x, channels * (x + 3))
        total_ref[at, :] += dot(ahead_ref[...], moved_ref[x])
    pre_ref[...] = total_ref[channels : channels * (count + 1), :].reshape(pre_ref.shape)


def outer_kernel(
    core_ref, rows_ref, first_ref, second_ref, moved_ref, pre_ref, cot2_ref, occ2_ref, weight_ref,
    result_ref, grad_ref, terms_ref, padded_ref,
):
    count, channels, lanes = pre_ref.shape
    bricks = lanes // PLANE
    low, high = load_faces(core_ref, first_ref, second_ref)
    moved_low = shifted_face(low, rows_ref, -1, bricks)
    moved_high = shifted_face(high, rows_ref, 1, bricks)
    add_low = dot(weight_ref[2 * channels : 3 * channels, :], moved_low)
    add_high = dot(weight_ref[0:channels, :], moved_high)
    padded_ref[0:channels, :] = jnp.zeros((channels, lanes), BF)
    padded_ref[channels * (count + 1) :, :] = jnp.zeros((channels, lanes), BF)
    bias = jnp.zeros((channels, lanes), F32)
    for x in range(count):
        pre = pre_ref[x]
        if x == 0:
            pre = pre + add_low
        if x == count - 1:
            pre = pre + add_high
        keep = jnp.broadcast_to(occ2_ref[x][0:1], (channels, lanes))
        sig = jax.nn.sigmoid(pre)
        masked = moved_ref[x, 4 * channels : 5 * channels, :].astype(F32)
        result_ref[x] = (masked + keep * pre * sig).astype(BF)
        grad = (cot2_ref[x].astype(F32) * sig * (1.0 + pre * (1.0 - sig))).astype(BF)
        grad_ref[x] = grad
        padded_ref[channels * (x + 1) : channels * (x + 2), :] = grad
        bias = bias + grad.astype(F32)
    terms = dot_t(padded_ref[0 : 3 * channels, :], moved_ref[0])
    for x in range(1, count):
        terms = terms + dot_t(padded_ref[channels * x : channels * (x + 3), :], moved_ref[x])
    width = 9 * channels
    terms_ref[:, 0:width] = terms
    terms_ref[2 * channels : 3 * channels, 0:width] += dot_t(grad_ref[0], moved_low)
    terms_ref[0:channels, 0:width] += dot_t(grad_ref[count - 1], moved_high)
    spare = terms_ref.shape[1] - width
    terms_ref[channels:, width:] = jnp.zeros((2 * channels, spare), F32)
    terms_ref[0:channels, width:] = jnp.sum(bias, axis=1, keepdims=True) * spread(spare)


def spread(count):
    return 1.0 + lax.broadcasted_iota(jnp.int32, (1, count), 1).astype(F32) * (1.0 / count)


def first_sum_kernel(core_ref, mine_ref, other_ref, grad_ref, out_ref, first_ref, second_ref):
    out_ref[...] = (mine_ref[...] + other_ref[...].astype(F32)).astype(BF)
    last = grad_ref.shape[0] - 1
    store_faces(core_ref, grad_ref[0], grad_ref[last], first_ref, second_ref)


def sum_kernel(mine_ref, other_ref, *refs):
    out_ref = refs[-1]
    out_ref[...] = (mine_ref[...].astype(F32) + other_ref[...].astype(F32)).astype(out_ref.dtype)


def back_inner_kernel(
    rows_ref, grad_ref, result2_ref, weight_ref, after_ref,
    result_ref, total_ref, back_ref, moved_ref,
):
    count, channels, lanes = grad_ref.shape
    bricks = lanes // PLANE
    back_weights(weight_ref, back_ref)
    shifted(grad_ref, moved_ref, rows_ref, bricks, channels)
    total_ref[...] = jnp.zeros(total_ref.shape, F32)
    for x in range(count):
        at = slice(channels * x, channels * (x + 3))
        total_ref[at, :] += dot(back_ref[...], moved_ref[x])
    for t in range(count // 2):
        out = from_planes(result2_ref[2 * t].astype(F32), result2_ref[2 * t + 1].astype(F32))
        for m in range(bricks):
            result_ref[m, :, 128 * t : 128 * t + 128] = out[m].astype(BF)


def back_outer_kernel(
    core_ref, rows_ref, first_ref, second_ref, total_ref, cot_ref, occ_ref, weight_ref, after_ref,
    in_grad_ref, done_ref,
):
    bricks, channels, voxels = cot_ref.shape
    count = voxels // PLANE
    done_ref[...] = jnp.zeros(done_ref.shape, F32)
    low, high = load_faces(core_ref, first_ref, second_ref)
    moved_low = shifted_face(low, rows_ref, -1, bricks)
    moved_high = shifted_face(high, rows_ref, 1, bricks)
    add_low = dot(weight_ref[2 * channels : 3 * channels, :], moved_low)
    add_high = dot(weight_ref[0:channels, :], moved_high)
    keep = occ_ref[...].astype(F32)
    for t in range(count // 2):
        at = slice(128 * t, 128 * t + 128)
        first = total_ref[channels * (2 * t + 1) : channels * (2 * t + 2), :]
        second = total_ref[channels * (2 * t + 2) : channels * (2 * t + 3), :]
        if t == 0:
            first = first + add_low
        if t == count // 2 - 1:
            second = second + add_high
        back = from_planes(first, second)
        for m in range(bricks):
            in_grad_ref[m, :, at] = (
                keep[m : m + 1, at] * (cot_ref[m, :, at].astype(F32) + back[m])
            ).astype(BF)


def final_kernel(normaliser, own_ref, mine_ref, other_ref, weight_ref, bias_ref, whole_ref):
    half, columns = mine_ref.shape
    channels = weight_ref.shape[1]
    own = own_ref[0]
    whole_ref[pl.ds(own * half, half), :] = mine_ref[...]
    whole_ref[pl.ds((1 - own) * half, half), :] = other_ref[...]
    for r in range(3):
        rows = slice(channels * r, channels * (r + 1))
        for t in range(columns // 128):
            tile = whole_ref[rows, 128 * t : 128 * t + 128] * normaliser
            weight_ref[9 * (2 - r) + 2 * t] = tile[:, :channels]
            if 2 * t + 1 < 9:
                weight_ref[9 * (2 - r) + 2 * t + 1] = pltpu.roll(tile, 128 - channels, 1)[:, :channels]
            elif r == 0:
                copies = pltpu.roll(tile, 128 - channels, 1)[:, :channels]
                copies = copies / (spread(channels) * channels)
                column = jnp.sum(copies, axis=1, keepdims=True)
                at = (channels, channels)
                same = lax.broadcasted_iota(jnp.int32, at, 0) == lax.broadcasted_iota(jnp.int32, at, 1)
                bias_ref[...] = jnp.sum(jnp.where(same, column, 0.0), axis=0, keepdims=True)


def call(body, outs, ins, scratch=(), flops=0):
    shapes = [jax.ShapeDtypeStruct(shape, dtype) for shape, dtype in outs]
    moved = sum(math.prod(s.shape) * s.dtype.itemsize for s in shapes)
    moved += sum(math.prod(x.shape) * x.dtype.itemsize for _, x in ins)
    return pl.pallas_call(
        body,
        out_shape=shapes,
        in_specs=[spec for spec, _ in ins],
        out_specs=[VMEM] * len(shapes),
        scratch_shapes=list(scratch),
        compiler_params=pltpu.CompilerParams(vmem_limit_bytes=32 << 20),
        cost_estimate=pl.CostEstimate(flops=flops, bytes_accessed=moved, transcendentals=0),
    )(*[pltpu.with_memory_space_constraint(x, pltpu.HBM) if s is HBM else x for s, x in ins])


def exchange_faces(first, second):
    spaces, reps = lax.axis_size("space"), lax.axis_size("rep")
    pairs = []
    for space in range(spaces):
        for rep in range(reps):
            step = 1 if rep % 2 == 0 else -1
            there, to = space + step, rep
            if not 0 <= there < spaces:
                there, to = space, rep ^ 1
            pairs.append((space * reps + rep, there * reps + to))
    back = [(j, i) for i, j in pairs]
    axes = ("space", "rep")
    return lax.ppermute(first, axes, pairs), lax.ppermute(second, axes, back)


def on_device(feats, cotangent, weight, bias, neighbours, occupancy):
    x, cot, near, occ = feats[0], cotangent[0], neighbours[0], occupancy[0]
    bricks, channels, voxels = x.shape
    count, lanes = voxels // PLANE, bricks * PLANE
    width = 9 * channels
    plane = ((channels, lanes), BF)
    core = (lax.axis_index("rep") % 2).astype(jnp.int32)
    cores = core[None]
    first, second, rows, x, occ, cot, weight, bias = call(
        stage_kernel,
        [
            plane, plane, ((32, lanes), jnp.int32), (x.shape, BF), (occ.shape, jnp.int32), (x.shape, BF),
            (weight.shape, BF), ((1, channels), F32),
        ],
        [(SMEM, cores), (HBM, x), (HBM, occ), (HBM, near), (HBM, cot), (HBM, weight), (HBM, bias[None])],
        [pltpu.SMEM(near.shape, jnp.int32), pltpu.SemaphoreType.DMA((6,))],
    )
    first, second = exchange_faces(first, second)
    moved, pre, cot2, occ2, ahead = call(
        inner_kernel,
        [
            ((count, width, lanes), BF),
            ((count, channels, lanes), F32),
            ((count, channels, lanes), BF),
            ((count, 8, lanes), F32),
            ((3 * channels, width), BF),
        ],
        [(VMEM, rows), (VMEM, x), (VMEM, cot), (VMEM, occ), (VMEM, weight), (VMEM, bias)],
        [
            pltpu.VMEM((count, channels, lanes), BF),
            pltpu.VMEM((channels * (count + 2), lanes), F32),
        ],
        flops=2 * 27 * channels * channels * bricks * voxels,
    )
    result2, grad, terms = call(
        outer_kernel,
        [
            ((count, channels, lanes), BF),
            ((count, channels, lanes), BF),
            ((3 * channels, width + 64), F32),
        ],
        [
            (SMEM, cores), (VMEM, rows), (VMEM, first), (VMEM, second), (VMEM, moved), (VMEM, pre),
            (VMEM, cot2), (VMEM, occ2), (VMEM, ahead),
        ],
        [pltpu.VMEM((channels * (count + 2), lanes), BF)],
        flops=2 * 27 * channels * channels * bricks * voxels,
    )
    axes = ("space", "rep")
    devices = lax.axis_size("space") * lax.axis_size("rep")
    half = 3 * channels // 2
    partner = [(i, i ^ 1) for i in range(devices)]
    me = lax.axis_index("space") * lax.axis_size("rep") + lax.axis_index("rep")
    own = lax.population_count(me.astype(jnp.int32)) & 1
    theirs = lax.dynamic_slice_in_dim(terms, (1 - own) * half, half, 0).astype(BF)
    mine = lax.dynamic_slice_in_dim(terms, own * half, half, 0)
    other = lax.ppermute(theirs, axes, partner)
    sent = ((half, terms.shape[1]), BF)
    mine, first, second = call(
        first_sum_kernel,
        [sent, plane, plane],
        [(SMEM, cores), (VMEM, mine), (VMEM, other), (VMEM, grad)],
    )
    bits = [1 << i for i in range(1, (devices).bit_length() - 1)]
    turn = len(bits) // 2
    total = in_grad = result = None
    rounds = list(zip(bits, bits[turn:] + bits[:turn]))
    for i, steps in enumerate(rounds):
        pairs = [(j, j ^ 1 ^ steps[j.bit_count() % 2]) for j in range(devices)]
        other = lax.ppermute(mine, axes, pairs)
        held = []
        if i == 0:
            first, second = exchange_faces(first, second)
        if i == 1:
            result, total, back = call(
                back_inner_kernel,
                [
                    ((bricks, channels, voxels), BF),
                    ((channels * (count + 2), lanes), F32),
                    ((3 * channels, width), BF),
                ],
                [(VMEM, rows), (VMEM, grad), (VMEM, result2), (VMEM, weight), (ANY, mine)],
                [pltpu.VMEM((count, width, lanes), BF)],
                flops=2 * 27 * channels * channels * bricks * voxels,
            )
            held = [total, first, second]
        if i == 2:
            in_grad, done = call(
                back_outer_kernel,
                [((bricks, channels, voxels), BF), ((8, 128), F32)],
                [
                    (SMEM, cores), (VMEM, rows), (VMEM, first), (VMEM, second), (VMEM, total), (VMEM, cot),
                    (VMEM, occ), (VMEM, back), (ANY, mine),
                ],
                flops=2 * 6 * channels * channels * bricks * voxels,
            )
            held = [done]
        last = i == len(rounds) - 1
        (mine,) = call(
            sum_kernel,
            [(sent[0], F32 if last else BF)],
            [(VMEM, mine), (VMEM, other)] + [(ANY, h) for h in held],
        )
    other = lax.ppermute(mine, axes, partner)
    normaliser = 1.0 / math.sqrt(
        feats.shape[0] * lax.axis_size("rep") * bricks * lax.axis_size("space") * voxels
    )
    weight_grad, bias_grad = call(
        functools.partial(final_kernel, normaliser),
        [(weight.shape, F32), ((1, channels), F32)],
        [(SMEM, own[None]), (VMEM, mine), (VMEM, other)],
        [pltpu.VMEM(terms.shape, F32)],
    )
    return result[None], in_grad[None], weight_grad, bias_grad[0]


def solution(mesh):
    placed = (
        P("rep", "space", None, None),
        P("rep", "space", None, None),
        P(),
        P(),
        P("rep", "space", None),
        P("rep", "space", None),
    )
    return jax.shard_map(
        on_device,
        mesh=mesh,
        in_specs=placed,
        out_specs=(P("rep", "space", None, None), P("rep", "space", None, None), P(), P()),
        check_vma=False,
    )
```

```python
import functools
import math

import jax
import jax.numpy as jnp
from jax import lax
from jax.experimental import pallas as pl
from jax.experimental.pallas import tpu as pltpu
from jax.sharding import PartitionSpec as P

BF, F32 = jnp.bfloat16, jnp.float32
DIRECTIONS = [
    (a, b, c) for a in (-1, 0, 1) for b in (-1, 0, 1) for c in (-1, 0, 1) if (a, b, c) != (0, 0, 0)
]
PLANE = 64
VMEM = pl.BlockSpec(memory_space=pltpu.VMEM)
ANY = pl.BlockSpec(memory_space=pl.ANY)
HBM = pl.BlockSpec(memory_space=pltpu.HBM)
SMEM = pl.BlockSpec(memory_space=pltpu.SMEM)


def to_planes(tiles):
    low = lax.broadcasted_iota(jnp.int32, tiles[0].shape, 1) < PLANE
    turned = [pltpu.roll(tile, PLANE, 1) for tile in tiles]
    first, second = [], []
    for m in range(0, len(tiles), 2):
        first.append(jnp.where(low, tiles[m], turned[m + 1]))
        second.append(jnp.where(low, turned[m], tiles[m + 1]))
    return jnp.concatenate(first, axis=1), jnp.concatenate(second, axis=1)


def from_planes(first, second):
    low = lax.broadcasted_iota(jnp.int32, (first.shape[0], 128), 1) < PLANE
    tiles = []
    for g in range(first.shape[1] // 128):
        one = first[:, 128 * g : 128 * g + 128]
        two = second[:, 128 * g : 128 * g + 128]
        tiles.append(jnp.where(low, one, pltpu.roll(two, PLANE, 1)))
        tiles.append(jnp.where(low, pltpu.roll(one, PLANE, 1), two))
    return tiles


SHIFTS = [(a, b, c) for a in (-1, 0, 1) for b in (-1, 0, 1) for c in (-1, 0, 1)]


def fill_slot_rows(near_ref, rows_ref, bricks):
    lane = lax.broadcasted_iota(jnp.int32, (1, bricks * PLANE), 1)
    brick = lane // PLANE
    for d, shift in enumerate(SHIFTS):
        if shift == (0, 0, 0):
            rows_ref[d : d + 1, :] = brick * PLANE
            continue
        j = DIRECTIONS.index(shift)
        found = jnp.full(lane.shape, -(1 << 20), jnp.int32)
        for n in range(bricks):
            chosen = near_ref[n, j]
            row = jnp.where(chosen >= 0, lax.rem(chosen, bricks) * PLANE, -(1 << 20))
            found = jnp.where(brick == n, row, found)
        rows_ref[d : d + 1, :] = found


def slot_rows(rows_ref, dx):
    rows = {}
    for d, (a, b, c) in enumerate(SHIFTS):
        if a == dx:
            rows[b, c] = rows_ref[d : d + 1, :]
    return rows


def selection(rows, b, c, bricks):
    size = bricks * PLANE
    lane = lax.broadcasted_iota(jnp.int32, (1, size), 1)
    y = ((lane >> 3) & 7) + (b - 1)
    z = (lane & 7) + (c - 1)
    out_y = (y < 0) | (y > 7)
    out_z = (z < 0) | (z > 7)
    base = rows[0, 0]
    if b != 1:
        base = jnp.where(out_y, rows[b - 1, 0], base)
    if c != 1:
        base = jnp.where(out_z, rows[0, c - 1], base)
    if b != 1 and c != 1:
        base = jnp.where(out_y & out_z, rows[b - 1, c - 1], base)
    source = base + (y & 7) * 8 + (z & 7)
    row = lax.broadcasted_iota(jnp.int32, (size, size), 0)
    return jnp.where(row == source, 1.0, 0.0).astype(BF)


def dot(x, y):
    return lax.dot_general(x, y, (((1,), (0,)), ((), ())), preferred_element_type=F32)


def dot_t(x, y):
    return lax.dot_general(x, y, (((1,), (1,)), ((), ())), preferred_element_type=F32)


def store_faces(core_ref, low, high, first_ref, second_ref):
    even = core_ref[0] == 0

    @pl.when(even)
    def _():
        first_ref[...] = high
        second_ref[...] = low

    @pl.when(jnp.logical_not(even))
    def _():
        first_ref[...] = low
        second_ref[...] = high


def load_faces(core_ref, first_ref, second_ref):
    even = core_ref[0] == 0
    first, second = first_ref[...].astype(F32), second_ref[...].astype(F32)
    return jnp.where(even, first, second).astype(BF), jnp.where(even, second, first).astype(BF)


def stage_kernel(
    core_ref, feats_ref, occ_ref, near_ref, cot_ref, weight_ref, bias_ref,
    first_ref, second_ref, rows_ref, x_ref, keep_ref, cot_out_ref, weight_out_ref, bias_out_ref,
    near_held_ref, sems,
):
    pairs = (
        (near_ref, near_held_ref), (occ_ref, keep_ref), (feats_ref, x_ref), (cot_ref, cot_out_ref),
        (weight_ref, weight_out_ref), (bias_ref, bias_out_ref),
    )
    copies = [pltpu.make_async_copy(a, b, sems.at[i]) for i, (a, b) in enumerate(pairs)]
    for copy in copies:
        copy.start()
    bricks, _, voxels = x_ref.shape
    copies[0].wait()
    fill_slot_rows(near_held_ref, rows_ref, bricks)
    copies[1].wait()
    copies[2].wait()
    keep = keep_ref[...].astype(F32)
    faces = []
    for i, start in enumerate((0, voxels - 128)):
        at = slice(start, start + 128)
        tiles = [x_ref[m, :, at].astype(F32) * keep[m : m + 1, at] for m in range(bricks)]
        faces.append(to_planes(tiles)[i].astype(BF))
    store_faces(core_ref, faces[0], faces[1], first_ref, second_ref)
    for copy in copies[3:]:
        copy.wait()


def ahead_weights(weight_ref, ahead_ref):
    channels = weight_ref.shape[1]
    for r in range(3):
        blocks = [weight_ref[9 * (2 - r) + k].astype(F32) for k in range(9)]
        ahead_ref[channels * r : channels * (r + 1), :] = jnp.concatenate(blocks, axis=1).astype(BF)


def back_weights(weight_ref, back_ref):
    channels = weight_ref.shape[1]
    for r in range(3):
        blocks = [weight_ref[9 * r + 8 - k].astype(F32).T for k in range(9)]
        back_ref[channels * r : channels * (r + 1), :] = jnp.concatenate(blocks, axis=1).astype(BF)


def shifted(planes_ref, moved_ref, rows_ref, bricks, channels):
    rows = slot_rows(rows_ref, 0)
    count = planes_ref.shape[0]
    flat = planes_ref[...].reshape(count * channels, bricks * PLANE)
    for b in range(3):
        for c in range(3):
            k = 3 * b + c
            if k == 4:
                part = flat
            else:
                part = dot(flat, selection(rows, b, c, bricks)).astype(BF)
            moved_ref[:, channels * k : channels * (k + 1), :] = part.reshape(
                count, channels, bricks * PLANE
            )


def shifted_face(face, rows_ref, dx, bricks):
    rows = slot_rows(rows_ref, dx)
    parts = []
    for b in range(3):
        for c in range(3):
            parts.append(dot(face, selection(rows, b, c, bricks)).astype(BF))
    return jnp.concatenate(parts, axis=0)


def inner_kernel(
    rows_ref, feats_ref, cot_ref, occ_ref, weight_ref, bias_ref,
    moved_ref, pre_ref, cot2_ref, occ2_ref, ahead_ref, planes_ref, total_ref,
):
    bricks, channels, voxels = feats_ref.shape
    keep = occ_ref[...].astype(F32)
    for t in range(voxels // 128):
        at = slice(128 * t, 128 * t + 128)
        kept = [jnp.broadcast_to(keep[m : m + 1, at], (channels, 128)) for m in range(bricks)]
        first, second = to_planes([feats_ref[m, :, at].astype(F32) * kept[m] for m in range(bricks)])
        planes_ref[2 * t] = first.astype(BF)
        planes_ref[2 * t + 1] = second.astype(BF)
        first, second = to_planes([cot_ref[m, :, at].astype(F32) * kept[m] for m in range(bricks)])
        cot2_ref[2 * t] = first.astype(BF)
        cot2_ref[2 * t + 1] = second.astype(BF)
        first, second = to_planes([kept[m][:8] for m in range(bricks)])
        occ2_ref[2 * t] = first
        occ2_ref[2 * t + 1] = second
    shifted(planes_ref, moved_ref, rows_ref, bricks, channels)
    ahead_weights(weight_ref, ahead_ref)
    count = planes_ref.shape[0]
    at = (channels, channels)
    same = lax.broadcasted_iota(jnp.int32, at, 0) == lax.broadcasted_iota(jnp.int32, at, 1)
    column = jnp.sum(jnp.where(same, bias_ref[...], 0.0), axis=1, keepdims=True)
    start = jnp.broadcast_to(column, (channels, bricks * PLANE))
    for x in range(count + 2):
        total_ref[channels * x : channels * (x + 1), :] = start
    for x in range(count):
        at = slice(channels * x, channels * (x + 3))
        total_ref[at, :] += dot(ahead_ref[...], moved_ref[x])
    pre_ref[...] = total_ref[channels : channels * (count + 1), :].reshape(pre_ref.shape)


def outer_kernel(
    core_ref, own_ref, rows_ref, first_ref, second_ref, moved_ref, pre_ref, cot2_ref, occ2_ref,
    weight_ref, result_ref, grad_ref, mine_ref, theirs_ref, padded_ref, terms_ref,
):
    count, channels, lanes = pre_ref.shape
    bricks = lanes // PLANE
    low, high = load_faces(core_ref, first_ref, second_ref)
    moved_low = shifted_face(low, rows_ref, -1, bricks)
    moved_high = shifted_face(high, rows_ref, 1, bricks)
    add_low = dot(weight_ref[2 * channels : 3 * channels, :], moved_low)
    add_high = dot(weight_ref[0:channels, :], moved_high)
    padded_ref[0:channels, :] = jnp.zeros((channels, lanes), BF)
    padded_ref[channels * (count + 1) :, :] = jnp.zeros((channels, lanes), BF)
    bias = jnp.zeros((channels, lanes), F32)
    for x in range(count):
        pre = pre_ref[x]
        if x == 0:
            pre = pre + add_low
        if x == count - 1:
            pre = pre + add_high
        keep = jnp.broadcast_to(occ2_ref[x][0:1], (channels, lanes))
        sig = jax.nn.sigmoid(pre)
        masked = moved_ref[x, 4 * channels : 5 * channels, :].astype(F32)
        result_ref[x] = (masked + keep * pre * sig).astype(BF)
        grad = (cot2_ref[x].astype(F32) * sig * (1.0 + pre * (1.0 - sig))).astype(BF)
        grad_ref[x] = grad
        padded_ref[channels * (x + 1) : channels * (x + 2), :] = grad
        bias = bias + grad.astype(F32)
    terms = dot_t(padded_ref[0 : 3 * channels, :], moved_ref[0])
    for x in range(1, count):
        terms = terms + dot_t(padded_ref[channels * x : channels * (x + 3), :], moved_ref[x])
    width = 9 * channels
    terms_ref[:, 0:width] = terms
    terms_ref[2 * channels : 3 * channels, 0:width] += dot_t(grad_ref[0], moved_low)
    terms_ref[0:channels, 0:width] += dot_t(grad_ref[count - 1], moved_high)
    spare = terms_ref.shape[1] - width
    terms_ref[channels:, width:] = jnp.zeros((2 * channels, spare), F32)
    terms_ref[0:channels, width:] = jnp.sum(bias, axis=1, keepdims=True) * spread(spare)
    half = mine_ref.shape[0]
    own = own_ref[0]
    mine_ref[...] = terms_ref[pl.ds(own * half, half), :]
    theirs_ref[0:half, :] = terms_ref[pl.ds((1 - own) * half, half), :].astype(BF)
    even = core_ref[0] == 0
    part = channels // 2
    low, high = grad_ref[0].astype(F32), grad_ref[count - 1].astype(F32)
    face = jnp.where(even, low, high).astype(BF)
    theirs_ref[half:, 0:lanes] = face[:part]
    theirs_ref[half:, lanes : 2 * lanes] = face[part:]
    theirs_ref[half:, 2 * lanes :] = jnp.zeros((part, theirs_ref.shape[1] - 2 * lanes), BF)


def spread(count):
    return 1.0 + lax.broadcasted_iota(jnp.int32, (1, count), 1).astype(F32) * (1.0 / count)


def first_sum_kernel(core_ref, mine_ref, other_ref, grad_ref, out_ref, faces_ref):
    half = mine_ref.shape[0]
    out_ref[...] = (mine_ref[...] + other_ref[0:half, :].astype(F32)).astype(BF)
    count, channels, lanes = grad_ref.shape
    part = channels // 2
    even = core_ref[0] == 0
    low, high = grad_ref[0].astype(F32), grad_ref[count - 1].astype(F32)
    faces_ref[0:channels, :] = jnp.where(even, high, low).astype(BF)
    faces_ref[channels : channels + part, :] = other_ref[half:, 0:lanes]
    faces_ref[channels + part :, :] = other_ref[half:, lanes : 2 * lanes]


def faces_sum_kernel(mine_ref, other_ref, faces_ref, out_ref, own_ref, sibling_ref):
    channels = own_ref.shape[0]
    out_ref[...] = (mine_ref[...].astype(F32) + other_ref[...].astype(F32)).astype(BF)
    own_ref[...] = faces_ref[0:channels, :]
    sibling_ref[...] = faces_ref[channels:, :]


def sum_kernel(mine_ref, other_ref, *refs):
    out_ref = refs[-1]
    out_ref[...] = (mine_ref[...].astype(F32) + other_ref[...].astype(F32)).astype(out_ref.dtype)


def back_inner_kernel(
    rows_ref, grad_ref, result2_ref, weight_ref, after_ref,
    result_ref, total_ref, back_ref, moved_ref,
):
    count, channels, lanes = grad_ref.shape
    bricks = lanes // PLANE
    back_weights(weight_ref, back_ref)
    shifted(grad_ref, moved_ref, rows_ref, bricks, channels)
    total_ref[...] = jnp.zeros(total_ref.shape, F32)
    for x in range(count):
        at = slice(channels * x, channels * (x + 3))
        total_ref[at, :] += dot(back_ref[...], moved_ref[x])
    for t in range(count // 2):
        out = from_planes(result2_ref[2 * t].astype(F32), result2_ref[2 * t + 1].astype(F32))
        for m in range(bricks):
            result_ref[m, :, 128 * t : 128 * t + 128] = out[m].astype(BF)


def back_outer_kernel(
    core_ref, rows_ref, first_ref, second_ref, total_ref, cot_ref, occ_ref, weight_ref, after_ref,
    in_grad_ref, done_ref,
):
    bricks, channels, voxels = cot_ref.shape
    count = voxels // PLANE
    done_ref[...] = jnp.zeros(done_ref.shape, F32)
    low, high = load_faces(core_ref, first_ref, second_ref)
    moved_low = shifted_face(low, rows_ref, -1, bricks)
    moved_high = shifted_face(high, rows_ref, 1, bricks)
    add_low = dot(weight_ref[2 * channels : 3 * channels, :], moved_low)
    add_high = dot(weight_ref[0:channels, :], moved_high)
    keep = occ_ref[...].astype(F32)
    for t in range(count // 2):
        at = slice(128 * t, 128 * t + 128)
        first = total_ref[channels * (2 * t + 1) : channels * (2 * t + 2), :]
        second = total_ref[channels * (2 * t + 2) : channels * (2 * t + 3), :]
        if t == 0:
            first = first + add_low
        if t == count // 2 - 1:
            second = second + add_high
        back = from_planes(first, second)
        for m in range(bricks):
            in_grad_ref[m, :, at] = (
                keep[m : m + 1, at] * (cot_ref[m, :, at].astype(F32) + back[m])
            ).astype(BF)


def final_kernel(normaliser, own_ref, mine_ref, other_ref, weight_ref, bias_ref, whole_ref):
    half, columns = mine_ref.shape
    channels = weight_ref.shape[1]
    own = own_ref[0]
    whole_ref[pl.ds(own * half, half), :] = mine_ref[...]
    whole_ref[pl.ds((1 - own) * half, half), :] = other_ref[...]
    for r in range(3):
        rows = slice(channels * r, channels * (r + 1))
        for t in range(columns // 128):
            tile = whole_ref[rows, 128 * t : 128 * t + 128] * normaliser
            weight_ref[9 * (2 - r) + 2 * t] = tile[:, :channels]
            if 2 * t + 1 < 9:
                weight_ref[9 * (2 - r) + 2 * t + 1] = pltpu.roll(tile, 128 - channels, 1)[:, :channels]
            elif r == 0:
                copies = pltpu.roll(tile, 128 - channels, 1)[:, :channels]
                copies = copies / (spread(channels) * channels)
                column = jnp.sum(copies, axis=1, keepdims=True)
                at = (channels, channels)
                same = lax.broadcasted_iota(jnp.int32, at, 0) == lax.broadcasted_iota(jnp.int32, at, 1)
                bias_ref[...] = jnp.sum(jnp.where(same, column, 0.0), axis=0, keepdims=True)


def call(body, outs, ins, scratch=(), flops=0):
    shapes = [jax.ShapeDtypeStruct(shape, dtype) for shape, dtype in outs]
    moved = sum(math.prod(s.shape) * s.dtype.itemsize for s in shapes)
    moved += sum(math.prod(x.shape) * x.dtype.itemsize for _, x in ins)
    return pl.pallas_call(
        body,
        out_shape=shapes,
        in_specs=[spec for spec, _ in ins],
        out_specs=[VMEM] * len(shapes),
        scratch_shapes=list(scratch),
        compiler_params=pltpu.CompilerParams(vmem_limit_bytes=32 << 20),
        cost_estimate=pl.CostEstimate(flops=flops, bytes_accessed=moved, transcendentals=0),
    )(*[pltpu.with_memory_space_constraint(x, pltpu.HBM) if s is HBM else x for s, x in ins])


def face_pairs():
    spaces, reps = lax.axis_size("space"), lax.axis_size("rep")
    pairs = []
    for space in range(spaces):
        for rep in range(reps):
            step = 1 if rep % 2 == 0 else -1
            there, to = space + step, rep
            if not 0 <= there < spaces:
                there, to = space, rep ^ 1
            pairs.append((space * reps + rep, there * reps + to))
    return pairs


def on_device(feats, cotangent, weight, bias, neighbours, occupancy):
    x, cot, near, occ = feats[0], cotangent[0], neighbours[0], occupancy[0]
    bricks, channels, voxels = x.shape
    count, lanes = voxels // PLANE, bricks * PLANE
    width = 9 * channels
    plane = ((channels, lanes), BF)
    core = (lax.axis_index("rep") % 2).astype(jnp.int32)
    cores = core[None]
    first, second, rows, x, occ, cot, weight, bias = call(
        stage_kernel,
        [
            plane, plane, ((32, lanes), jnp.int32), (x.shape, BF), (occ.shape, jnp.int32), (x.shape, BF),
            (weight.shape, BF), ((1, channels), F32),
        ],
        [(SMEM, cores), (HBM, x), (HBM, occ), (HBM, near), (HBM, cot), (HBM, weight), (HBM, bias[None])],
        [pltpu.SMEM(near.shape, jnp.int32), pltpu.SemaphoreType.DMA((6,))],
    )
    axes = ("space", "rep")
    pairs = face_pairs()
    first = lax.ppermute(first, axes, pairs)
    second = lax.ppermute(second, axes, [(j, i) for i, j in pairs])
    moved, pre, cot2, occ2, ahead = call(
        inner_kernel,
        [
            ((count, width, lanes), BF),
            ((count, channels, lanes), F32),
            ((count, channels, lanes), BF),
            ((count, 8, lanes), F32),
            ((3 * channels, width), BF),
        ],
        [(VMEM, rows), (VMEM, x), (VMEM, cot), (VMEM, occ), (VMEM, weight), (VMEM, bias)],
        [
            pltpu.VMEM((count, channels, lanes), BF),
            pltpu.VMEM((channels * (count + 2), lanes), F32),
        ],
        flops=2 * 27 * channels * channels * bricks * voxels,
    )
    devices = lax.axis_size("space") * lax.axis_size("rep")
    me = lax.axis_index("space") * lax.axis_size("rep") + lax.axis_index("rep")
    own = (lax.population_count(me.astype(jnp.int32)) & 1)[None]
    half, columns = 3 * channels // 2, width + 64
    result2, grad, mine, theirs = call(
        outer_kernel,
        [
            ((count, channels, lanes), BF),
            ((count, channels, lanes), BF),
            ((half, columns), F32),
            ((half + channels // 2, columns), BF),
        ],
        [
            (SMEM, cores), (SMEM, own), (VMEM, rows), (VMEM, first), (VMEM, second), (VMEM, moved),
            (VMEM, pre), (VMEM, cot2), (VMEM, occ2), (VMEM, ahead),
        ],
        [
            pltpu.VMEM((channels * (count + 2), lanes), BF),
            pltpu.VMEM((3 * channels, columns), F32),
        ],
        flops=2 * 27 * channels * channels * bricks * voxels,
    )
    partner = [(i, i ^ 1) for i in range(devices)]
    other = lax.ppermute(theirs, axes, partner)
    sent = ((half, columns), BF)
    mine, faces = call(
        first_sum_kernel,
        [sent, ((2 * channels, lanes), BF)],
        [(SMEM, cores), (VMEM, mine), (VMEM, other), (VMEM, grad)],
    )
    bits = [1 << i for i in range(1, (devices).bit_length() - 1)]
    turn = len(bits) // 2
    rounds = list(zip(bits, bits[turn:] + bits[:turn]))
    for i, steps in enumerate(rounds):
        joined = [(j, j ^ 1 ^ steps[j.bit_count() % 2]) for j in range(devices)]
        other = lax.ppermute(mine, axes, joined)
        held = []
        if i == 0:
            faces = lax.ppermute(faces, axes, pairs)
        if i == 1:
            mine, first, second = call(
                faces_sum_kernel, [sent, plane, plane], [(VMEM, mine), (VMEM, other), (VMEM, faces)]
            )
            continue
        if i == 2:
            second = lax.ppermute(second, axes, partner)
            result, total, back = call(
                back_inner_kernel,
                [
                    ((bricks, channels, voxels), BF),
                    ((channels * (count + 2), lanes), F32),
                    ((3 * channels, width), BF),
                ],
                [(VMEM, rows), (VMEM, grad), (VMEM, result2), (VMEM, weight), (ANY, mine)],
                [pltpu.VMEM((count, width, lanes), BF)],
                flops=2 * 27 * channels * channels * bricks * voxels,
            )
            held = [total, second]
        if i == 3:
            in_grad, done = call(
                back_outer_kernel,
                [((bricks, channels, voxels), BF), ((8, 128), F32)],
                [
                    (SMEM, cores), (VMEM, rows), (VMEM, first), (VMEM, second), (VMEM, total),
                    (VMEM, cot), (VMEM, occ), (VMEM, back), (ANY, mine),
                ],
                flops=2 * 6 * channels * channels * bricks * voxels,
            )
            held = [done]
        last = i == len(rounds) - 1
        (mine,) = call(
            sum_kernel,
            [(sent[0], F32 if last else BF)],
            [(VMEM, mine), (VMEM, other)] + [(ANY, h) for h in held],
        )
    other = lax.ppermute(mine, axes, partner)
    normaliser = 1.0 / math.sqrt(
        feats.shape[0] * lax.axis_size("rep") * bricks * lax.axis_size("space") * voxels
    )
    weight_grad, bias_grad = call(
        functools.partial(final_kernel, normaliser),
        [(weight.shape, F32), ((1, channels), F32)],
        [(SMEM, own), (VMEM, mine), (VMEM, other)],
        [pltpu.VMEM((3 * channels, columns), F32)],
    )
    return result[None], in_grad[None], weight_grad, bias_grad[0]


def solution(mesh):
    placed = (
        P("rep", "space", None, None),
        P("rep", "space", None, None),
        P(),
        P(),
        P("rep", "space", None),
        P("rep", "space", None),
    )
    return jax.shard_map(
        on_device,
        mesh=mesh,
        in_specs=placed,
        out_specs=(P("rep", "space", None, None), P("rep", "space", None, None), P(), P()),
        check_vma=False,
    )
```

```python
import functools
import math

import jax
import jax.numpy as jnp
from jax import lax
from jax.experimental import pallas as pl
from jax.experimental.pallas import tpu as pltpu
from jax.sharding import PartitionSpec as P

BF, F32 = jnp.bfloat16, jnp.float32
DIRECTIONS = [
    (a, b, c) for a in (-1, 0, 1) for b in (-1, 0, 1) for c in (-1, 0, 1) if (a, b, c) != (0, 0, 0)
]
PLANE = 64
VMEM = pl.BlockSpec(memory_space=pltpu.VMEM)
ANY = pl.BlockSpec(memory_space=pl.ANY)
HBM = pl.BlockSpec(memory_space=pltpu.HBM)
SMEM = pl.BlockSpec(memory_space=pltpu.SMEM)


def to_planes(tiles):
    low = lax.broadcasted_iota(jnp.int32, tiles[0].shape, 1) < PLANE
    turned = [pltpu.roll(tile, PLANE, 1) for tile in tiles]
    first, second = [], []
    for m in range(0, len(tiles), 2):
        first.append(jnp.where(low, tiles[m], turned[m + 1]))
        second.append(jnp.where(low, turned[m], tiles[m + 1]))
    return jnp.concatenate(first, axis=1), jnp.concatenate(second, axis=1)


def from_planes(first, second):
    low = lax.broadcasted_iota(jnp.int32, (first.shape[0], 128), 1) < PLANE
    tiles = []
    for g in range(first.shape[1] // 128):
        one = first[:, 128 * g : 128 * g + 128]
        two = second[:, 128 * g : 128 * g + 128]
        tiles.append(jnp.where(low, one, pltpu.roll(two, PLANE, 1)))
        tiles.append(jnp.where(low, pltpu.roll(one, PLANE, 1), two))
    return tiles


SHIFTS = [(a, b, c) for a in (-1, 0, 1) for b in (-1, 0, 1) for c in (-1, 0, 1)]


def fill_slot_rows(near_ref, rows_ref, bricks):
    lane = lax.broadcasted_iota(jnp.int32, (1, bricks * PLANE), 1)
    brick = lane // PLANE
    for d, shift in enumerate(SHIFTS):
        if shift == (0, 0, 0):
            rows_ref[d : d + 1, :] = brick * PLANE
            continue
        j = DIRECTIONS.index(shift)
        found = jnp.full(lane.shape, -(1 << 20), jnp.int32)
        for n in range(bricks):
            chosen = near_ref[n, j]
            row = jnp.where(chosen >= 0, lax.rem(chosen, bricks) * PLANE, -(1 << 20))
            found = jnp.where(brick == n, row, found)
        rows_ref[d : d + 1, :] = found


def slot_rows(rows_ref, dx):
    rows = {}
    for d, (a, b, c) in enumerate(SHIFTS):
        if a == dx:
            rows[b, c] = rows_ref[d : d + 1, :]
    return rows


def selection(rows, b, c, bricks):
    size = bricks * PLANE
    lane = lax.broadcasted_iota(jnp.int32, (1, size), 1)
    y = ((lane >> 3) & 7) + (b - 1)
    z = (lane & 7) + (c - 1)
    out_y = (y < 0) | (y > 7)
    out_z = (z < 0) | (z > 7)
    base = rows[0, 0]
    if b != 1:
        base = jnp.where(out_y, rows[b - 1, 0], base)
    if c != 1:
        base = jnp.where(out_z, rows[0, c - 1], base)
    if b != 1 and c != 1:
        base = jnp.where(out_y & out_z, rows[b - 1, c - 1], base)
    source = base + (y & 7) * 8 + (z & 7)
    row = lax.broadcasted_iota(jnp.int32, (size, size), 0)
    return jnp.where(row == source, 1.0, 0.0).astype(BF)


def dot(x, y):
    return lax.dot_general(x, y, (((1,), (0,)), ((), ())), preferred_element_type=F32)


def dot_t(x, y):
    return lax.dot_general(x, y, (((1,), (1,)), ((), ())), preferred_element_type=F32)


def store_faces(core_ref, low, high, first_ref, second_ref):
    even = core_ref[0] == 0

    @pl.when(even)
    def _():
        first_ref[...] = high
        second_ref[...] = low

    @pl.when(jnp.logical_not(even))
    def _():
        first_ref[...] = low
        second_ref[...] = high


def load_faces(core_ref, first_ref, second_ref):
    even = core_ref[0] == 0
    first, second = first_ref[...].astype(F32), second_ref[...].astype(F32)
    return jnp.where(even, first, second).astype(BF), jnp.where(even, second, first).astype(BF)


def stage_kernel(
    core_ref, feats_ref, occ_ref, near_ref, first_ref, second_ref, rows_ref, x_ref, keep_ref,
    near_held_ref, sems,
):
    pairs = ((near_ref, near_held_ref), (occ_ref, keep_ref), (feats_ref, x_ref))
    copies = [pltpu.make_async_copy(a, b, sems.at[i]) for i, (a, b) in enumerate(pairs)]
    for copy in copies:
        copy.start()
    bricks, _, voxels = x_ref.shape
    copies[0].wait()
    fill_slot_rows(near_held_ref, rows_ref, bricks)
    copies[1].wait()
    copies[2].wait()
    keep = keep_ref[...].astype(F32)
    faces = []
    for i, start in enumerate((0, voxels - 128)):
        at = slice(start, start + 128)
        tiles = [x_ref[m, :, at].astype(F32) * keep[m : m + 1, at] for m in range(bricks)]
        faces.append(to_planes(tiles)[i].astype(BF))
    store_faces(core_ref, faces[0], faces[1], first_ref, second_ref)


def ahead_weights(weight_ref, ahead_ref):
    channels = weight_ref.shape[1]
    for r in range(3):
        blocks = [weight_ref[9 * (2 - r) + k].astype(F32) for k in range(9)]
        ahead_ref[channels * r : channels * (r + 1), :] = jnp.concatenate(blocks, axis=1).astype(BF)


def back_weights(weight_ref, back_ref):
    channels = weight_ref.shape[1]
    for r in range(3):
        blocks = [weight_ref[9 * r + 8 - k].astype(F32).T for k in range(9)]
        back_ref[channels * r : channels * (r + 1), :] = jnp.concatenate(blocks, axis=1).astype(BF)


def shifted(planes_ref, moved_ref, rows_ref, bricks, channels):
    rows = slot_rows(rows_ref, 0)
    count = planes_ref.shape[0]
    flat = planes_ref[...].reshape(count * channels, bricks * PLANE)
    for b in range(3):
        for c in range(3):
            k = 3 * b + c
            if k == 4:
                part = flat
            else:
                part = dot(flat, selection(rows, b, c, bricks)).astype(BF)
            moved_ref[:, channels * k : channels * (k + 1), :] = part.reshape(
                count, channels, bricks * PLANE
            )


def shifted_face(face, rows_ref, dx, bricks):
    rows = slot_rows(rows_ref, dx)
    parts = []
    for b in range(3):
        for c in range(3):
            parts.append(dot(face, selection(rows, b, c, bricks)).astype(BF))
    return jnp.concatenate(parts, axis=0)


def inner_kernel(
    rows_ref, feats_ref, occ_ref, cot_from_ref, weight_from_ref, bias_from_ref,
    moved_ref, pre_ref, cot2_ref, occ2_ref, ahead_ref, cot_ref, weight_ref,
    planes_ref, total_ref, bias_ref, sems,
):
    bricks, channels, voxels = feats_ref.shape
    pairs = ((cot_from_ref, cot_ref), (weight_from_ref, weight_ref), (bias_from_ref, bias_ref))
    copies = [pltpu.make_async_copy(a, b, sems.at[i]) for i, (a, b) in enumerate(pairs)]
    for copy in copies:
        copy.start()
    keep = occ_ref[...].astype(F32)
    for t in range(voxels // 128):
        at = slice(128 * t, 128 * t + 128)
        kept = [jnp.broadcast_to(keep[m : m + 1, at], (channels, 128)) for m in range(bricks)]
        first, second = to_planes([feats_ref[m, :, at].astype(F32) * kept[m] for m in range(bricks)])
        planes_ref[2 * t] = first.astype(BF)
        planes_ref[2 * t + 1] = second.astype(BF)
        first, second = to_planes([kept[m][:8] for m in range(bricks)])
        occ2_ref[2 * t] = first
        occ2_ref[2 * t + 1] = second
    shifted(planes_ref, moved_ref, rows_ref, bricks, channels)
    for copy in copies:
        copy.wait()
    for t in range(voxels // 128):
        at = slice(128 * t, 128 * t + 128)
        kept = [jnp.broadcast_to(keep[m : m + 1, at], (channels, 128)) for m in range(bricks)]
        first, second = to_planes([cot_ref[m, :, at].astype(F32) * kept[m] for m in range(bricks)])
        cot2_ref[2 * t] = first.astype(BF)
        cot2_ref[2 * t + 1] = second.astype(BF)
    ahead_weights(weight_ref, ahead_ref)
    count = planes_ref.shape[0]
    at = (channels, channels)
    same = lax.broadcasted_iota(jnp.int32, at, 0) == lax.broadcasted_iota(jnp.int32, at, 1)
    column = jnp.sum(jnp.where(same, bias_ref[...], 0.0), axis=1, keepdims=True)
    start = jnp.broadcast_to(column, (channels, bricks * PLANE))
    for x in range(count + 2):
        total_ref[channels * x : channels * (x + 1), :] = start
    for x in range(count):
        at = slice(channels * x, channels * (x + 3))
        total_ref[at, :] += dot(ahead_ref[...], moved_ref[x])
    pre_ref[...] = total_ref[channels : channels * (count + 1), :].reshape(pre_ref.shape)


def half_terms(padded_ref, moved_ref, low_ref, high_ref, start, half):
    count, channels = moved_ref.shape[0], padded_ref.shape[0] // (moved_ref.shape[0] + 4)

    def rows(x):
        return padded_ref[pl.ds(pl.multiple_of(channels * (x + 1) + start, 32), half), :]

    terms = dot_t(rows(-1), low_ref[...])
    for x in range(count):
        terms = terms + dot_t(rows(x), moved_ref[x])
    return terms + dot_t(rows(count), high_ref[...])


def store_terms(terms, copies_ref, start, out_ref):
    half, width = terms.shape
    channels = copies_ref.shape[0]
    out_ref[0:half, 0:width] = terms.astype(out_ref.dtype)
    copies = jnp.where(start == 0, copies_ref[...], 0.0)
    copies = jnp.concatenate([copies, jnp.zeros((half - channels, copies.shape[1]), F32)], axis=0)
    out_ref[0:half, width:] = copies.astype(out_ref.dtype)


def outer_kernel(
    core_ref, own_ref, rows_ref, first_ref, second_ref, moved_ref, pre_ref, cot2_ref, occ2_ref,
    weight_ref,
    result_ref, grad_ref, theirs_ref, padded_ref, moved_low_ref, moved_high_ref, copies_ref,
):
    count, channels, lanes = pre_ref.shape
    bricks = lanes // PLANE
    low, high = load_faces(core_ref, first_ref, second_ref)
    moved_low_ref[...] = shifted_face(low, rows_ref, -1, bricks)
    moved_high_ref[...] = shifted_face(high, rows_ref, 1, bricks)
    add_low = dot(weight_ref[2 * channels : 3 * channels, :], moved_low_ref[...])
    add_high = dot(weight_ref[0:channels, :], moved_high_ref[...])
    padded_ref[0 : 2 * channels, :] = jnp.zeros((2 * channels, lanes), BF)
    padded_ref[channels * (count + 2) :, :] = jnp.zeros((2 * channels, lanes), BF)
    bias = jnp.zeros((channels, lanes), F32)
    for x in range(count):
        pre = pre_ref[x]
        if x == 0:
            pre = pre + add_low
        if x == count - 1:
            pre = pre + add_high
        keep = jnp.broadcast_to(occ2_ref[x][0:1], (channels, lanes))
        sig = jax.nn.sigmoid(pre)
        masked = moved_ref[x, 4 * channels : 5 * channels, :].astype(F32)
        result_ref[x] = (masked + keep * pre * sig).astype(BF)
        grad = (cot2_ref[x].astype(F32) * sig * (1.0 + pre * (1.0 - sig))).astype(BF)
        grad_ref[x] = grad
        padded_ref[channels * (x + 2) : channels * (x + 3), :] = grad
        bias = bias + grad.astype(F32)
    copies_ref[...] = jnp.sum(bias, axis=1, keepdims=True) * spread(copies_ref.shape[1])
    part = channels // 2
    half = theirs_ref.shape[0] - part
    start = (1 - own_ref[0]) * half
    terms = half_terms(padded_ref, moved_ref, moved_low_ref, moved_high_ref, start, half)
    store_terms(terms, copies_ref, start, theirs_ref)
    even = core_ref[0] == 0
    low, high = grad_ref[0].astype(F32), grad_ref[count - 1].astype(F32)
    face = jnp.where(even, low, high).astype(BF)
    theirs_ref[half:, 0:lanes] = face[:part]
    theirs_ref[half:, lanes : 2 * lanes] = face[part:]
    theirs_ref[half:, 2 * lanes :] = jnp.zeros((part, theirs_ref.shape[1] - 2 * lanes), BF)


def own_kernel(own_ref, padded_ref, moved_ref, low_ref, high_ref, copies_ref, mine_ref):
    half = mine_ref.shape[0]
    start = own_ref[0] * half
    terms = half_terms(padded_ref, moved_ref, low_ref, high_ref, start, half)
    store_terms(terms, copies_ref, start, mine_ref)


def spread(count):
    return 1.0 + lax.broadcasted_iota(jnp.int32, (1, count), 1).astype(F32) * (1.0 / count)


def first_sum_kernel(core_ref, mine_ref, other_ref, grad_ref, out_ref, faces_ref):
    half = mine_ref.shape[0]
    out_ref[...] = (mine_ref[...] + other_ref[0:half, :].astype(F32)).astype(BF)
    count, channels, lanes = grad_ref.shape
    part = channels // 2
    even = core_ref[0] == 0
    low, high = grad_ref[0].astype(F32), grad_ref[count - 1].astype(F32)
    faces_ref[0:channels, :] = jnp.where(even, high, low).astype(BF)
    faces_ref[channels : channels + part, :] = other_ref[half:, 0:lanes]
    faces_ref[channels + part :, :] = other_ref[half:, lanes : 2 * lanes]


def faces_sum_kernel(mine_ref, other_ref, faces_ref, out_ref, own_ref, sibling_ref):
    channels = own_ref.shape[0]
    out_ref[...] = (mine_ref[...].astype(F32) + other_ref[...].astype(F32)).astype(BF)
    own_ref[...] = faces_ref[0:channels, :]
    sibling_ref[...] = faces_ref[channels:, :]


def sum_kernel(mine_ref, other_ref, *refs):
    out_ref = refs[-1]
    out_ref[...] = (mine_ref[...].astype(F32) + other_ref[...].astype(F32)).astype(out_ref.dtype)


def back_inner_kernel(
    rows_ref, grad_ref, result2_ref, weight_ref, after_ref,
    result_ref, total_ref, back_ref, moved_ref,
):
    count, channels, lanes = grad_ref.shape
    bricks = lanes // PLANE
    back_weights(weight_ref, back_ref)
    shifted(grad_ref, moved_ref, rows_ref, bricks, channels)
    total_ref[...] = jnp.zeros(total_ref.shape, F32)
    for x in range(count):
        at = slice(channels * x, channels * (x + 3))
        total_ref[at, :] += dot(back_ref[...], moved_ref[x])
    for t in range(count // 2):
        out = from_planes(result2_ref[2 * t].astype(F32), result2_ref[2 * t + 1].astype(F32))
        for m in range(bricks):
            result_ref[m, :, 128 * t : 128 * t + 128] = out[m].astype(BF)


def back_outer_kernel(
    core_ref, rows_ref, first_ref, second_ref, total_ref, cot_ref, occ_ref, weight_ref, after_ref,
    in_grad_ref, done_ref,
):
    bricks, channels, voxels = cot_ref.shape
    count = voxels // PLANE
    done_ref[...] = jnp.zeros(done_ref.shape, F32)
    low, high = load_faces(core_ref, first_ref, second_ref)
    moved_low = shifted_face(low, rows_ref, -1, bricks)
    moved_high = shifted_face(high, rows_ref, 1, bricks)
    add_low = dot(weight_ref[2 * channels : 3 * channels, :], moved_low)
    add_high = dot(weight_ref[0:channels, :], moved_high)
    keep = occ_ref[...].astype(F32)
    for t in range(count // 2):
        at = slice(128 * t, 128 * t + 128)
        first = total_ref[channels * (2 * t + 1) : channels * (2 * t + 2), :]
        second = total_ref[channels * (2 * t + 2) : channels * (2 * t + 3), :]
        if t == 0:
            first = first + add_low
        if t == count // 2 - 1:
            second = second + add_high
        back = from_planes(first, second)
        for m in range(bricks):
            in_grad_ref[m, :, at] = (
                keep[m : m + 1, at] * (cot_ref[m, :, at].astype(F32) + back[m])
            ).astype(BF)


def final_kernel(normaliser, own_ref, mine_ref, other_ref, weight_ref, bias_ref, whole_ref):
    half, columns = mine_ref.shape
    channels = weight_ref.shape[1]
    own = own_ref[0]
    whole_ref[pl.ds(own * half, half), :] = mine_ref[...]
    whole_ref[pl.ds((1 - own) * half, half), :] = other_ref[...]
    for r in range(3):
        rows = slice(channels * r, channels * (r + 1))
        for t in range(columns // 128):
            tile = whole_ref[rows, 128 * t : 128 * t + 128] * normaliser
            weight_ref[9 * (2 - r) + 2 * t] = tile[:, :channels]
            if 2 * t + 1 < 9:
                weight_ref[9 * (2 - r) + 2 * t + 1] = pltpu.roll(tile, 128 - channels, 1)[:, :channels]
            elif r == 0:
                copies = pltpu.roll(tile, 128 - channels, 1)[:, :channels]
                copies = copies / (spread(channels) * channels)
                column = jnp.sum(copies, axis=1, keepdims=True)
                at = (channels, channels)
                same = lax.broadcasted_iota(jnp.int32, at, 0) == lax.broadcasted_iota(jnp.int32, at, 1)
                bias_ref[...] = jnp.sum(jnp.where(same, column, 0.0), axis=0, keepdims=True)


def call(body, outs, ins, scratch=(), flops=0):
    shapes = [jax.ShapeDtypeStruct(shape, dtype) for shape, dtype in outs]
    moved = sum(math.prod(s.shape) * s.dtype.itemsize for s in shapes)
    moved += sum(math.prod(x.shape) * x.dtype.itemsize for _, x in ins)
    return pl.pallas_call(
        body,
        out_shape=shapes,
        in_specs=[spec for spec, _ in ins],
        out_specs=[VMEM] * len(shapes),
        scratch_shapes=list(scratch),
        compiler_params=pltpu.CompilerParams(vmem_limit_bytes=32 << 20),
        cost_estimate=pl.CostEstimate(flops=flops, bytes_accessed=moved, transcendentals=0),
    )(*[pltpu.with_memory_space_constraint(x, pltpu.HBM) if s is HBM else x for s, x in ins])


def face_pairs():
    spaces, reps = lax.axis_size("space"), lax.axis_size("rep")
    pairs = []
    for space in range(spaces):
        for rep in range(reps):
            step = 1 if rep % 2 == 0 else -1
            there, to = space + step, rep
            if not 0 <= there < spaces:
                there, to = space, rep ^ 1
            pairs.append((space * reps + rep, there * reps + to))
    return pairs


def on_device(feats, cotangent, weight, bias, neighbours, occupancy):
    x, cot, near, occ = feats[0], cotangent[0], neighbours[0], occupancy[0]
    bricks, channels, voxels = x.shape
    count, lanes = voxels // PLANE, bricks * PLANE
    width = 9 * channels
    plane = ((channels, lanes), BF)
    core = (lax.axis_index("rep") % 2).astype(jnp.int32)
    cores = core[None]
    first, second, rows, x, occ = call(
        stage_kernel,
        [plane, plane, ((32, lanes), jnp.int32), (x.shape, BF), (occ.shape, jnp.int32)],
        [(SMEM, cores), (HBM, x), (HBM, occ), (HBM, near)],
        [pltpu.SMEM(near.shape, jnp.int32), pltpu.SemaphoreType.DMA((3,))],
    )
    axes = ("space", "rep")
    pairs = face_pairs()
    first = lax.ppermute(first, axes, pairs)
    second = lax.ppermute(second, axes, [(j, i) for i, j in pairs])
    moved, pre, cot2, occ2, ahead, cot, weight = call(
        inner_kernel,
        [
            ((count, width, lanes), BF),
            ((count, channels, lanes), F32),
            ((count, channels, lanes), BF),
            ((count, 8, lanes), F32),
            ((3 * channels, width), BF),
            (cot.shape, BF),
            (weight.shape, BF),
        ],
        [(VMEM, rows), (VMEM, x), (VMEM, occ), (HBM, cot), (HBM, weight), (HBM, bias[None])],
        [
            pltpu.VMEM((count, channels, lanes), BF),
            pltpu.VMEM((channels * (count + 2), lanes), F32),
            pltpu.VMEM((1, channels), F32),
            pltpu.SemaphoreType.DMA((3,)),
        ],
        flops=2 * 27 * channels * channels * bricks * voxels,
    )
    devices = lax.axis_size("space") * lax.axis_size("rep")
    me = lax.axis_index("space") * lax.axis_size("rep") + lax.axis_index("rep")
    own = (lax.population_count(me.astype(jnp.int32)) & 1)[None]
    half, columns = 3 * channels // 2, width + 64
    result2, grad, theirs, padded, moved_low, moved_high, copies = call(
        outer_kernel,
        [
            ((count, channels, lanes), BF),
            ((count, channels, lanes), BF),
            ((half + channels // 2, columns), BF),
            ((channels * (count + 4), lanes), BF),
            ((width, lanes), BF),
            ((width, lanes), BF),
            ((channels, columns - width), F32),
        ],
        [
            (SMEM, cores), (SMEM, own), (VMEM, rows), (VMEM, first), (VMEM, second), (VMEM, moved),
            (VMEM, pre), (VMEM, cot2), (VMEM, occ2), (VMEM, ahead),
        ],
        flops=2 * 27 * channels * channels * bricks * voxels,
    )
    partner = [(i, i ^ 1) for i in range(devices)]
    other = lax.ppermute(theirs, axes, partner)
    (mine,) = call(
        own_kernel,
        [((half, columns), F32)],
        [
            (SMEM, own), (VMEM, padded), (VMEM, moved), (VMEM, moved_low), (VMEM, moved_high),
            (VMEM, copies),
        ],
        flops=27 * channels * channels * bricks * voxels,
    )
    sent = ((half, columns), BF)
    mine, faces = call(
        first_sum_kernel,
        [sent, ((2 * channels, lanes), BF)],
        [(SMEM, cores), (VMEM, mine), (VMEM, other), (VMEM, grad)],
    )
    bits = [1 << i for i in range(1, (devices).bit_length() - 1)]
    rounds = list(zip(bits[:1] + bits[-1:] + bits[1:-1], bits[-1:] + bits[1:-1] + bits[:1]))
    for i, steps in enumerate(rounds):
        joined = [(j, j ^ 1 ^ steps[j.bit_count() % 2]) for j in range(devices)]
        other = lax.ppermute(mine, axes, joined)
        held = []
        if i == 0:
            faces = lax.ppermute(faces, axes, pairs)
            result, total, back = call(
                back_inner_kernel,
                [
                    ((bricks, channels, voxels), BF),
                    ((channels * (count + 2), lanes), F32),
                    ((3 * channels, width), BF),
                ],
                [(VMEM, rows), (VMEM, grad), (VMEM, result2), (VMEM, weight), (ANY, mine)],
                [pltpu.VMEM((count, width, lanes), BF)],
                flops=2 * 27 * channels * channels * bricks * voxels,
            )
            held = [total]
        if i == 2:
            first, second = faces[:channels], lax.ppermute(faces[channels:], axes, partner)
            held = [second]
        if i == 3:
            in_grad, done = call(
                back_outer_kernel,
                [((bricks, channels, voxels), BF), ((8, 128), F32)],
                [
                    (SMEM, cores), (VMEM, rows), (VMEM, first), (VMEM, second), (VMEM, total),
                    (VMEM, cot), (VMEM, occ), (VMEM, back), (ANY, mine),
                ],
                flops=2 * 6 * channels * channels * bricks * voxels,
            )
            held = [done]
        last = i == len(rounds) - 1
        (mine,) = call(
            sum_kernel,
            [(sent[0], F32 if last else BF)],
            [(VMEM, mine), (VMEM, other)] + [(ANY, h) for h in held],
        )
    other = lax.ppermute(mine, axes, partner)
    normaliser = 1.0 / math.sqrt(
        feats.shape[0] * lax.axis_size("rep") * bricks * lax.axis_size("space") * voxels
    )
    weight_grad, bias_grad = call(
        functools.partial(final_kernel, normaliser),
        [(weight.shape, F32), ((1, channels), F32)],
        [(SMEM, own), (VMEM, mine), (VMEM, other)],
        [pltpu.VMEM((3 * channels, columns), F32)],
    )
    return result[None], in_grad[None], weight_grad, bias_grad[0]


def solution(mesh):
    placed = (
        P("rep", "space", None, None),
        P("rep", "space", None, None),
        P(),
        P(),
        P("rep", "space", None),
        P("rep", "space", None),
    )
    return jax.shard_map(
        on_device,
        mesh=mesh,
        in_specs=placed,
        out_specs=(P("rep", "space", None, None), P("rep", "space", None, None), P(), P()),
        check_vma=False,
    )
```

```python
import functools
import math

import jax
import jax.numpy as jnp
from jax import lax
from jax.experimental import pallas as pl
from jax.experimental.pallas import tpu as pltpu
from jax.sharding import PartitionSpec as P

BF, F32 = jnp.bfloat16, jnp.float32
DIRECTIONS = [
    (a, b, c) for a in (-1, 0, 1) for b in (-1, 0, 1) for c in (-1, 0, 1) if (a, b, c) != (0, 0, 0)
]
PLANE = 64
VMEM = pl.BlockSpec(memory_space=pltpu.VMEM)
ANY = pl.BlockSpec(memory_space=pl.ANY)
HBM = pl.BlockSpec(memory_space=pltpu.HBM)
SMEM = pl.BlockSpec(memory_space=pltpu.SMEM)


def to_planes(tiles):
    low = lax.broadcasted_iota(jnp.int32, tiles[0].shape, 1) < PLANE
    turned = [pltpu.roll(tile, PLANE, 1) for tile in tiles]
    first, second = [], []
    for m in range(0, len(tiles), 2):
        first.append(jnp.where(low, tiles[m], turned[m + 1]))
        second.append(jnp.where(low, turned[m], tiles[m + 1]))
    return jnp.concatenate(first, axis=1), jnp.concatenate(second, axis=1)


def from_planes(first, second):
    low = lax.broadcasted_iota(jnp.int32, (first.shape[0], 128), 1) < PLANE
    tiles = []
    for g in range(first.shape[1] // 128):
        one = first[:, 128 * g : 128 * g + 128]
        two = second[:, 128 * g : 128 * g + 128]
        tiles.append(jnp.where(low, one, pltpu.roll(two, PLANE, 1)))
        tiles.append(jnp.where(low, pltpu.roll(one, PLANE, 1), two))
    return tiles


SHIFTS = [(a, b, c) for a in (-1, 0, 1) for b in (-1, 0, 1) for c in (-1, 0, 1)]


def fill_slot_rows(near_ref, rows_ref, bricks):
    lane = lax.broadcasted_iota(jnp.int32, (1, bricks * PLANE), 1)
    brick = lane // PLANE
    for d, shift in enumerate(SHIFTS):
        if shift == (0, 0, 0):
            rows_ref[d : d + 1, :] = brick * PLANE
            continue
        j = DIRECTIONS.index(shift)
        found = jnp.full(lane.shape, -(1 << 20), jnp.int32)
        for n in range(bricks):
            chosen = near_ref[n, j]
            row = jnp.where(chosen >= 0, lax.rem(chosen, bricks) * PLANE, -(1 << 20))
            found = jnp.where(brick == n, row, found)
        rows_ref[d : d + 1, :] = found


def slot_rows(rows_ref, dx):
    rows = {}
    for d, (a, b, c) in enumerate(SHIFTS):
        if a == dx:
            rows[b, c] = rows_ref[d : d + 1, :]
    return rows


def selection(rows, b, c, bricks):
    size = bricks * PLANE
    lane = lax.broadcasted_iota(jnp.int32, (1, size), 1)
    y = ((lane >> 3) & 7) + (b - 1)
    z = (lane & 7) + (c - 1)
    out_y = (y < 0) | (y > 7)
    out_z = (z < 0) | (z > 7)
    base = rows[0, 0]
    if b != 1:
        base = jnp.where(out_y, rows[b - 1, 0], base)
    if c != 1:
        base = jnp.where(out_z, rows[0, c - 1], base)
    if b != 1 and c != 1:
        base = jnp.where(out_y & out_z, rows[b - 1, c - 1], base)
    source = base + (y & 7) * 8 + (z & 7)
    row = lax.broadcasted_iota(jnp.int32, (size, size), 0)
    return jnp.where(row == source, 1.0, 0.0).astype(BF)


def phase(scalar_ref):
    return pl.when(scalar_ref[0] >= 0)


def dot(x, y):
    return lax.dot_general(x, y, (((1,), (0,)), ((), ())), preferred_element_type=F32)


def dot_t(x, y):
    return lax.dot_general(x, y, (((1,), (1,)), ((), ())), preferred_element_type=F32)


def store_faces(core_ref, low, high, first_ref, second_ref):
    even = core_ref[0] == 0

    @pl.when(even)
    def _():
        first_ref[...] = high
        second_ref[...] = low

    @pl.when(jnp.logical_not(even))
    def _():
        first_ref[...] = low
        second_ref[...] = high


def load_faces(core_ref, first_ref, second_ref):
    even = core_ref[0] == 0
    first, second = first_ref[...].astype(F32), second_ref[...].astype(F32)
    return jnp.where(even, first, second).astype(BF), jnp.where(even, second, first).astype(BF)


def stage_kernel(
    core_ref, feats_ref, occ_ref, near_ref, first_ref, second_ref, rows_ref, x_ref, keep_ref,
    near_held_ref, sems,
):
    pairs = ((near_ref, near_held_ref), (occ_ref, keep_ref), (feats_ref, x_ref))
    copies = [pltpu.make_async_copy(a, b, sems.at[i]) for i, (a, b) in enumerate(pairs)]
    for copy in copies:
        copy.start()
    bricks, _, voxels = x_ref.shape
    copies[0].wait()
    fill_slot_rows(near_held_ref, rows_ref, bricks)
    copies[1].wait()
    copies[2].wait()
    keep = keep_ref[...].astype(F32)
    faces = []
    for i, start in enumerate((0, voxels - 128)):
        at = slice(start, start + 128)
        tiles = [x_ref[m, :, at].astype(F32) * keep[m : m + 1, at] for m in range(bricks)]
        faces.append(to_planes(tiles)[i].astype(BF))
    store_faces(core_ref, faces[0], faces[1], first_ref, second_ref)


def ahead_weights(weight_ref, ahead_ref):
    channels = weight_ref.shape[1]
    for r in range(3):
        blocks = [weight_ref[9 * (2 - r) + k].astype(F32) for k in range(9)]
        ahead_ref[channels * r : channels * (r + 1), :] = jnp.concatenate(blocks, axis=1).astype(BF)


def back_weights(weight_ref, back_ref):
    channels = weight_ref.shape[1]
    for r in range(3):
        blocks = [weight_ref[9 * r + 8 - k].astype(F32).T for k in range(9)]
        back_ref[channels * r : channels * (r + 1), :] = jnp.concatenate(blocks, axis=1).astype(BF)


def shifted(planes_ref, moved_ref, rows_ref, bricks, channels):
    rows = slot_rows(rows_ref, 0)
    count = planes_ref.shape[0]
    flat = planes_ref[...].reshape(count * channels, bricks * PLANE)
    for b in range(3):
        for c in range(3):
            k = 3 * b + c
            if k == 4:
                part = flat
            else:
                part = dot(flat, selection(rows, b, c, bricks)).astype(BF)
            moved_ref[:, channels * k : channels * (k + 1), :] = part.reshape(
                count, channels, bricks * PLANE
            )


def add_products(core_ref, weight_ref, moved_ref, total_ref):
    channels = weight_ref.shape[0] // 3

    @phase(core_ref)
    def _():
        for x in range(moved_ref.shape[0]):
            at = slice(channels * x, channels * (x + 3))
            total_ref[at, :] += dot(weight_ref[...], moved_ref[x])


def shifted_face(face, rows_ref, dx, bricks):
    rows = slot_rows(rows_ref, dx)
    parts = []
    for b in range(3):
        for c in range(3):
            parts.append(dot(face, selection(rows, b, c, bricks)).astype(BF))
    return jnp.concatenate(parts, axis=0)


def inner_kernel(
    core_ref, rows_ref, feats_ref, occ_ref, cot_from_ref, weight_from_ref, bias_from_ref,
    moved_ref, pre_ref, cot2_ref, occ2_ref, ahead_ref, cot_ref, weight_ref,
    planes_ref, total_ref, bias_ref, sems,
):
    bricks, channels, voxels = feats_ref.shape
    pairs = ((cot_from_ref, cot_ref), (weight_from_ref, weight_ref), (bias_from_ref, bias_ref))
    copies = [pltpu.make_async_copy(a, b, sems.at[i]) for i, (a, b) in enumerate(pairs)]
    for copy in copies:
        copy.start()
    keep = occ_ref[...].astype(F32)
    for t in range(voxels // 128):
        at = slice(128 * t, 128 * t + 128)
        kept = [jnp.broadcast_to(keep[m : m + 1, at], (channels, 128)) for m in range(bricks)]
        first, second = to_planes([feats_ref[m, :, at].astype(F32) * kept[m] for m in range(bricks)])
        planes_ref[2 * t] = first.astype(BF)
        planes_ref[2 * t + 1] = second.astype(BF)
        first, second = to_planes([kept[m][:8] for m in range(bricks)])
        occ2_ref[2 * t] = first
        occ2_ref[2 * t + 1] = second
    shifted(planes_ref, moved_ref, rows_ref, bricks, channels)
    for copy in copies:
        copy.wait()
    for t in range(voxels // 128):
        at = slice(128 * t, 128 * t + 128)
        kept = [jnp.broadcast_to(keep[m : m + 1, at], (channels, 128)) for m in range(bricks)]
        first, second = to_planes([cot_ref[m, :, at].astype(F32) * kept[m] for m in range(bricks)])
        cot2_ref[2 * t] = first.astype(BF)
        cot2_ref[2 * t + 1] = second.astype(BF)
    ahead_weights(weight_ref, ahead_ref)
    count = planes_ref.shape[0]
    at = (channels, channels)
    same = lax.broadcasted_iota(jnp.int32, at, 0) == lax.broadcasted_iota(jnp.int32, at, 1)
    column = jnp.sum(jnp.where(same, bias_ref[...], 0.0), axis=1, keepdims=True)
    start = jnp.broadcast_to(column, (channels, bricks * PLANE))
    for x in range(count + 2):
        total_ref[channels * x : channels * (x + 1), :] = start
    add_products(core_ref, ahead_ref, moved_ref, total_ref)
    pre_ref[...] = total_ref[channels : channels * (count + 1), :].reshape(pre_ref.shape)


def half_terms(padded_ref, moved_ref, low_ref, high_ref, start, half):
    count, channels = moved_ref.shape[0], padded_ref.shape[0] // (moved_ref.shape[0] + 4)

    def rows(x):
        return padded_ref[pl.ds(pl.multiple_of(channels * (x + 1) + start, 32), half), :]

    terms = dot_t(rows(-1), low_ref[...])
    for x in range(count):
        terms = terms + dot_t(rows(x), moved_ref[x])
    return terms + dot_t(rows(count), high_ref[...])


def store_terms(terms, copies_ref, start, out_ref):
    half = terms.shape[0]
    unit = half // 3
    full = terms.shape[1] // 128
    for t in range(full):
        out_ref[half * t : half * (t + 1), :] = terms[:, 128 * t : 128 * t + 128].astype(out_ref.dtype)
    last = terms[:, 128 * full :]
    copies = jnp.where(start == 0, copies_ref[...], 0.0)
    one = jnp.concatenate([last[:unit], last[unit : 2 * unit]], axis=1)
    two = jnp.concatenate([last[2 * unit :], copies], axis=1)
    at = half * full
    out_ref[at : at + unit, :] = one.astype(out_ref.dtype)
    out_ref[at + unit : at + 2 * unit, :] = two.astype(out_ref.dtype)


def outer_kernel(
    core_ref, own_ref, rows_ref, first_ref, second_ref, moved_ref, pre_ref, cot2_ref, occ2_ref,
    weight_ref,
    result_ref, grad_ref, theirs_ref, padded_ref, moved_low_ref, moved_high_ref, copies_ref,
):
    count, channels, lanes = pre_ref.shape
    bricks = lanes // PLANE
    low, high = load_faces(core_ref, first_ref, second_ref)
    moved_low_ref[...] = shifted_face(low, rows_ref, -1, bricks)
    moved_high_ref[...] = shifted_face(high, rows_ref, 1, bricks)
    add_low = dot(weight_ref[2 * channels : 3 * channels, :], moved_low_ref[...])
    add_high = dot(weight_ref[0:channels, :], moved_high_ref[...])
    padded_ref[0 : 2 * channels, :] = jnp.zeros((2 * channels, lanes), BF)
    padded_ref[channels * (count + 2) :, :] = jnp.zeros((2 * channels, lanes), BF)
    bias = jnp.zeros((channels, lanes), F32)
    for x in range(count):
        pre = pre_ref[x]
        if x == 0:
            pre = pre + add_low
        if x == count - 1:
            pre = pre + add_high
        keep = jnp.broadcast_to(occ2_ref[x][0:1], (channels, lanes))
        sig = jax.nn.sigmoid(pre)
        masked = moved_ref[x, 4 * channels : 5 * channels, :].astype(F32)
        result_ref[x] = (masked + keep * pre * sig).astype(BF)
        grad = (cot2_ref[x].astype(F32) * sig * (1.0 + pre * (1.0 - sig))).astype(BF)
        grad_ref[x] = grad
        padded_ref[channels * (x + 2) : channels * (x + 3), :] = grad
        bias = bias + grad.astype(F32)
    at = (channels, channels)
    same = lax.broadcasted_iota(jnp.int32, at, 0) == lax.broadcasted_iota(jnp.int32, at, 1)
    row = jnp.sum(jnp.where(same, jnp.sum(bias, axis=1, keepdims=True), 0.0), axis=0, keepdims=True)
    copies_ref[...] = row * spread(copies_ref.shape)
    half = 3 * channels // 2
    start = (1 - own_ref[0]) * half
    terms = half_terms(padded_ref, moved_ref, moved_low_ref, moved_high_ref, start, half)
    store_terms(terms, copies_ref, start, theirs_ref)
    even = core_ref[0] == 0
    low, high = grad_ref[0].astype(F32), grad_ref[count - 1].astype(F32)
    face = jnp.where(even, low, high).astype(BF)
    size = theirs_ref.shape[0] - channels * (lanes // 128)
    for t in range(lanes // 128):
        theirs_ref[size + channels * t : size + channels * (t + 1), :] = face[:, 128 * t : 128 * t + 128]


def own_kernel(own_ref, padded_ref, moved_ref, low_ref, high_ref, copies_ref, mine_ref):
    half = 3 * copies_ref.shape[1] // 2
    start = own_ref[0] * half
    terms = half_terms(padded_ref, moved_ref, low_ref, high_ref, start, half)
    store_terms(terms, copies_ref, start, mine_ref)


def spread(shape):
    return 1.0 + lax.broadcasted_iota(jnp.int32, shape, 0).astype(F32) * (1.0 / shape[0])


def first_sum_kernel(core_ref, mine_ref, other_ref, grad_ref, out_ref, faces_ref):
    size = mine_ref.shape[0]
    out_ref[...] = (mine_ref[...] + other_ref[0:size, :].astype(F32)).astype(BF)
    count, channels, lanes = grad_ref.shape
    even = core_ref[0] == 0
    low, high = grad_ref[0].astype(F32), grad_ref[count - 1].astype(F32)
    faces_ref[0:channels, :] = jnp.where(even, high, low).astype(BF)
    for t in range(lanes // 128):
        rows = slice(size + channels * t, size + channels * (t + 1))
        faces_ref[channels:, 128 * t : 128 * t + 128] = other_ref[rows, :]


def sum_kernel(mine_ref, other_ref, *refs):
    out_ref = refs[-1]
    out_ref[...] = (mine_ref[...].astype(F32) + other_ref[...].astype(F32)).astype(out_ref.dtype)


def back_inner_kernel(
    core_ref, rows_ref, grad_ref, result2_ref, weight_ref, after_ref,
    result_ref, total_ref, back_ref, moved_ref,
):
    count, channels, lanes = grad_ref.shape
    bricks = lanes // PLANE
    back_weights(weight_ref, back_ref)
    shifted(grad_ref, moved_ref, rows_ref, bricks, channels)
    total_ref[...] = jnp.zeros(total_ref.shape, F32)
    add_products(core_ref, back_ref, moved_ref, total_ref)
    for t in range(count // 2):
        out = from_planes(result2_ref[2 * t].astype(F32), result2_ref[2 * t + 1].astype(F32))
        for m in range(bricks):
            result_ref[m, :, 128 * t : 128 * t + 128] = out[m].astype(BF)


def back_outer_kernel(
    core_ref, rows_ref, first_ref, second_ref, total_ref, cot_ref, occ_ref, weight_ref, after_ref,
    in_grad_ref, done_ref,
):
    bricks, channels, voxels = cot_ref.shape
    count = voxels // PLANE
    done_ref[...] = jnp.zeros(done_ref.shape, F32)
    low, high = load_faces(core_ref, first_ref, second_ref)
    moved_low = shifted_face(low, rows_ref, -1, bricks)
    moved_high = shifted_face(high, rows_ref, 1, bricks)
    add_low = dot(weight_ref[2 * channels : 3 * channels, :], moved_low)
    add_high = dot(weight_ref[0:channels, :], moved_high)
    keep = occ_ref[...].astype(F32)
    for t in range(count // 2):
        at = slice(128 * t, 128 * t + 128)
        first = total_ref[channels * (2 * t + 1) : channels * (2 * t + 2), :]
        second = total_ref[channels * (2 * t + 2) : channels * (2 * t + 3), :]
        if t == 0:
            first = first + add_low
        if t == count // 2 - 1:
            second = second + add_high
        back = from_planes(first, second)
        for m in range(bricks):
            in_grad_ref[m, :, at] = (
                keep[m : m + 1, at] * (cot_ref[m, :, at].astype(F32) + back[m])
            ).astype(BF)


def arrived_bias(scale, source_ref, channels):
    unit = channels // 2
    rows = source_ref.shape[0]
    tile = pltpu.roll(source_ref[rows - unit : rows, :], 128 - channels, 1)[:, :channels]
    return jnp.sum(tile * (scale / (spread(tile.shape) * unit)), axis=0, keepdims=True)


def store_half(scale, mine, source_ref, weight_ref, held_ref, sems):
    half, unit, channels = 3 * held_ref.shape[3] // 2, held_ref.shape[2], held_ref.shape[3]
    copies = []
    for j in range(3):
        for t in range(4):
            rows = slice(half * t + unit * j, half * t + unit * (j + 1))
            tile = source_ref[rows, :] * scale
            held_ref[j, 2 * t] = tile[:, :channels]
            held_ref[j, 2 * t + 1] = pltpu.roll(tile, 128 - channels, 1)[:, :channels]
        at = 4 * half + unit * (j // 2)
        tile = source_ref[at : at + unit, :] * scale
        if j == 1:
            tile = pltpu.roll(tile, 128 - channels, 1)
        held_ref[j, 8] = tile[:, :channels]
        u = 3 * mine + j
        place = weight_ref.at[
            pl.ds(9 * (2 - u // 2), 9), pl.ds(pl.multiple_of(unit * (u % 2), unit), unit), :
        ]
        copies.append(pltpu.make_async_copy(held_ref.at[j], place, sems.at[j]))
        copies[-1].start()
    return copies


def own_half_kernel(scale, own_ref, source_ref, weight_ref, bias_ref, held_ref, sems):
    copies = store_half(scale, own_ref[0], source_ref, weight_ref, held_ref, sems)
    bias_ref[...] = arrived_bias(scale, source_ref, held_ref.shape[3])
    for copy in copies:
        copy.wait()


def other_half_kernel(
    scale, own_ref, source_ref, begun_ref, own_bias_ref,
    weight_ref, bias_ref, held_ref, bias_held_ref, sems,
):
    bias = arrived_bias(scale, source_ref, held_ref.shape[3])
    bias_held_ref[...] = jnp.where(own_ref[0] == 0, own_bias_ref[...], bias)
    copies = [pltpu.make_async_copy(bias_held_ref, bias_ref, sems.at[3])]
    copies[0].start()
    copies += store_half(scale, 1 - own_ref[0], source_ref, weight_ref, held_ref, sems)
    for copy in copies:
        copy.wait()


def call(body, outs, ins, scratch=(), flops=0, out_specs=None, aliases=None):
    shapes = [jax.ShapeDtypeStruct(shape, dtype) for shape, dtype in outs]
    moved = sum(math.prod(s.shape) * s.dtype.itemsize for s in shapes)
    moved += sum(math.prod(x.shape) * x.dtype.itemsize for _, x in ins)
    return pl.pallas_call(
        body,
        out_shape=shapes,
        in_specs=[spec for spec, _ in ins],
        out_specs=out_specs or [VMEM] * len(shapes),
        input_output_aliases=aliases or {},
        scratch_shapes=list(scratch),
        compiler_params=pltpu.CompilerParams(vmem_limit_bytes=32 << 20),
        cost_estimate=pl.CostEstimate(flops=flops, bytes_accessed=moved, transcendentals=0),
    )(*[pltpu.with_memory_space_constraint(x, pltpu.HBM) if s is HBM else x for s, x in ins])


def face_pairs():
    spaces, reps = lax.axis_size("space"), lax.axis_size("rep")
    pairs = []
    for space in range(spaces):
        for rep in range(reps):
            step = 1 if rep % 2 == 0 else -1
            there, to = space + step, rep
            if not 0 <= there < spaces:
                there, to = space, rep ^ 1
            pairs.append((space * reps + rep, there * reps + to))
    return pairs


def on_device(feats, cotangent, weight, bias, neighbours, occupancy):
    x, cot, near, occ = feats[0], cotangent[0], neighbours[0], occupancy[0]
    bricks, channels, voxels = x.shape
    count, lanes = voxels // PLANE, bricks * PLANE
    width = 9 * channels
    plane = ((channels, lanes), BF)
    core = (lax.axis_index("rep") % 2).astype(jnp.int32)
    cores = core[None]
    first, second, rows, x, occ = call(
        stage_kernel,
        [plane, plane, ((32, lanes), jnp.int32), (x.shape, BF), (occ.shape, jnp.int32)],
        [(SMEM, cores), (HBM, x), (HBM, occ), (HBM, near)],
        [pltpu.SMEM(near.shape, jnp.int32), pltpu.SemaphoreType.DMA((3,))],
    )
    axes = ("space", "rep")
    pairs = face_pairs()
    first = lax.ppermute(first, axes, pairs)
    second = lax.ppermute(second, axes, [(j, i) for i, j in pairs])
    moved, pre, cot2, occ2, ahead, cot, weight = call(
        inner_kernel,
        [
            ((count, width, lanes), BF),
            ((count, channels, lanes), F32),
            ((count, channels, lanes), BF),
            ((count, 8, lanes), F32),
            ((3 * channels, width), BF),
            (cot.shape, BF),
            (weight.shape, BF),
        ],
        [(SMEM, cores), (VMEM, rows), (VMEM, x), (VMEM, occ), (HBM, cot), (HBM, weight), (HBM, bias[None])],
        [
            pltpu.VMEM((count, channels, lanes), BF),
            pltpu.VMEM((channels * (count + 2), lanes), F32),
            pltpu.VMEM((1, channels), F32),
            pltpu.SemaphoreType.DMA((3,)),
        ],
        flops=2 * 27 * channels * channels * bricks * voxels,
    )
    devices = lax.axis_size("space") * lax.axis_size("rep")
    me = lax.axis_index("space") * lax.axis_size("rep") + lax.axis_index("rep")
    own = (lax.population_count(me.astype(jnp.int32)) & 1)[None]
    size = 3 * channels // 2 * (width // 128) + channels
    result2, grad, theirs, padded, moved_low, moved_high, copies = call(
        outer_kernel,
        [
            ((count, channels, lanes), BF),
            ((count, channels, lanes), BF),
            ((size + channels * lanes // 128, 128), BF),
            ((channels * (count + 4), lanes), BF),
            ((width, lanes), BF),
            ((width, lanes), BF),
            ((channels // 2, channels), F32),
        ],
        [
            (SMEM, cores), (SMEM, own), (VMEM, rows), (VMEM, first), (VMEM, second), (VMEM, moved),
            (VMEM, pre), (VMEM, cot2), (VMEM, occ2), (VMEM, ahead),
        ],
        flops=2 * 27 * channels * channels * bricks * voxels,
    )
    partner = [(i, i ^ 1) for i in range(devices)]
    other = lax.ppermute(theirs, axes, partner)
    (mine,) = call(
        own_kernel,
        [((size, 128), F32)],
        [
            (SMEM, own), (VMEM, padded), (VMEM, moved), (VMEM, moved_low), (VMEM, moved_high),
            (VMEM, copies),
        ],
        flops=27 * channels * channels * bricks * voxels,
    )
    sent = ((size, 128), BF)
    mine, faces = call(
        first_sum_kernel,
        [sent, ((2 * channels, lanes), BF)],
        [(SMEM, cores), (VMEM, mine), (VMEM, other), (VMEM, grad)],
    )
    bits = [1 << i for i in range(1, (devices).bit_length() - 1)]
    rounds = list(zip(bits[:1] + bits[-1:] + bits[1:-1], bits[-1:] + bits[1:-1] + bits[:1]))
    for i, steps in enumerate(rounds):
        joined = [(j, j ^ 1 ^ steps[j.bit_count() % 2]) for j in range(devices)]
        other = lax.ppermute(mine, axes, joined)
        held = []
        if i == 0:
            faces = lax.ppermute(faces, axes, pairs)
            result, total, back = call(
                back_inner_kernel,
                [
                    ((bricks, channels, voxels), BF),
                    ((channels * (count + 2), lanes), F32),
                    ((3 * channels, width), BF),
                ],
                [
                    (SMEM, cores), (VMEM, rows), (VMEM, grad), (VMEM, result2), (VMEM, weight),
                    (ANY, mine),
                ],
                [pltpu.VMEM((count, width, lanes), BF)],
                flops=2 * 27 * channels * channels * bricks * voxels,
            )
            held = [total]
        if i == 2:
            first, second = faces[:channels], lax.ppermute(faces[channels:], axes, partner)
            held = [second]
        if i == 3:
            in_grad, done = call(
                back_outer_kernel,
                [((bricks, channels, voxels), BF), ((8, 128), F32)],
                [
                    (SMEM, cores), (VMEM, rows), (VMEM, first), (VMEM, second), (VMEM, total),
                    (VMEM, cot), (VMEM, occ), (VMEM, back), (ANY, mine),
                ],
                flops=2 * 6 * channels * channels * bricks * voxels,
            )
            held = [done]
        last = i == len(rounds) - 1
        (mine,) = call(
            sum_kernel,
            [(sent[0], F32 if last else BF)],
            [(VMEM, mine), (VMEM, other)] + [(ANY, h) for h in held],
        )
    other = lax.ppermute(mine, axes, partner)
    normaliser = 1.0 / math.sqrt(
        feats.shape[0] * lax.axis_size("rep") * bricks * lax.axis_size("space") * voxels
    )
    held = pltpu.VMEM((3, 9, channels // 2, channels), F32)
    outs = [(weight.shape, F32), ((1, channels), F32)]
    weight_grad, bias_grad = call(
        functools.partial(own_half_kernel, normaliser),
        outs,
        [(SMEM, own), (VMEM, mine)],
        [held, pltpu.SemaphoreType.DMA((3,))],
        out_specs=[HBM, VMEM],
    )
    weight_grad, bias_grad = call(
        functools.partial(other_half_kernel, normaliser),
        outs,
        [(SMEM, own), (VMEM, other), (ANY, weight_grad), (VMEM, bias_grad)],
        [held, pltpu.VMEM((1, channels), F32), pltpu.SemaphoreType.DMA((4,))],
        out_specs=[HBM, HBM],
        aliases={2: 0},
    )
    return result[None], in_grad[None], weight_grad, bias_grad[0]


def solution(mesh):
    placed = (
        P("rep", "space", None, None),
        P("rep", "space", None, None),
        P(),
        P(),
        P("rep", "space", None),
        P("rep", "space", None),
    )
    return jax.shard_map(
        on_device,
        mesh=mesh,
        in_specs=placed,
        out_specs=(P("rep", "space", None, None), P("rep", "space", None, None), P(), P()),
        check_vma=False,
    )
```

```python
import functools
import math

import jax
import jax.numpy as jnp
from jax import lax
from jax.experimental import pallas as pl
from jax.experimental.pallas import tpu as pltpu
from jax.sharding import PartitionSpec as P

BF, F32 = jnp.bfloat16, jnp.float32
DIRECTIONS = [
    (a, b, c) for a in (-1, 0, 1) for b in (-1, 0, 1) for c in (-1, 0, 1) if (a, b, c) != (0, 0, 0)
]
PLANE = 64
VMEM = pl.BlockSpec(memory_space=pltpu.VMEM)
ANY = pl.BlockSpec(memory_space=pl.ANY)
HBM = pl.BlockSpec(memory_space=pltpu.HBM)
SMEM = pl.BlockSpec(memory_space=pltpu.SMEM)


def to_planes(tiles):
    low = lax.broadcasted_iota(jnp.int32, tiles[0].shape, 1) < PLANE
    turned = [pltpu.roll(tile, PLANE, 1) for tile in tiles]
    first, second = [], []
    for m in range(0, len(tiles), 2):
        first.append(jnp.where(low, tiles[m], turned[m + 1]))
        second.append(jnp.where(low, turned[m], tiles[m + 1]))
    return jnp.concatenate(first, axis=1), jnp.concatenate(second, axis=1)


def from_planes(first, second):
    low = lax.broadcasted_iota(jnp.int32, (first.shape[0], 128), 1) < PLANE
    tiles = []
    for g in range(first.shape[1] // 128):
        one = first[:, 128 * g : 128 * g + 128]
        two = second[:, 128 * g : 128 * g + 128]
        tiles.append(jnp.where(low, one, pltpu.roll(two, PLANE, 1)))
        tiles.append(jnp.where(low, pltpu.roll(one, PLANE, 1), two))
    return tiles


SHIFTS = [(a, b, c) for a in (-1, 0, 1) for b in (-1, 0, 1) for c in (-1, 0, 1)]


def fill_slot_rows(near_ref, rows_ref, bricks):
    lane = lax.broadcasted_iota(jnp.int32, (1, bricks * PLANE), 1)
    brick = lane // PLANE
    for d, shift in enumerate(SHIFTS):
        if shift == (0, 0, 0):
            rows_ref[d : d + 1, :] = brick * PLANE
            continue
        j = DIRECTIONS.index(shift)
        found = jnp.full(lane.shape, -(1 << 20), jnp.int32)
        for n in range(bricks):
            chosen = near_ref[n, j]
            row = jnp.where(chosen >= 0, lax.rem(chosen, bricks) * PLANE, -(1 << 20))
            found = jnp.where(brick == n, row, found)
        rows_ref[d : d + 1, :] = found


def slot_rows(rows_ref, dx):
    rows = {}
    for d, (a, b, c) in enumerate(SHIFTS):
        if a == dx:
            rows[b, c] = rows_ref[d : d + 1, :]
    return rows


def selection(rows, b, c, bricks):
    size = bricks * PLANE
    lane = lax.broadcasted_iota(jnp.int32, (1, size), 1)
    y = ((lane >> 3) & 7) + (b - 1)
    z = (lane & 7) + (c - 1)
    out_y = (y < 0) | (y > 7)
    out_z = (z < 0) | (z > 7)
    base = rows[0, 0]
    if b != 1:
        base = jnp.where(out_y, rows[b - 1, 0], base)
    if c != 1:
        base = jnp.where(out_z, rows[0, c - 1], base)
    if b != 1 and c != 1:
        base = jnp.where(out_y & out_z, rows[b - 1, c - 1], base)
    source = base + (y & 7) * 8 + (z & 7)
    row = lax.broadcasted_iota(jnp.int32, (size, size), 0)
    return jnp.where(row == source, 1.0, 0.0).astype(BF)


def phase(scalar_ref):
    return pl.when(scalar_ref[0] >= 0)


def dot(x, y):
    return lax.dot_general(x, y, (((1,), (0,)), ((), ())), preferred_element_type=F32)


def dot_t(x, y):
    return lax.dot_general(x, y, (((1,), (1,)), ((), ())), preferred_element_type=F32)


def load_faces(core_ref, first_ref, second_ref):
    even = core_ref[0] == 0
    first, second = first_ref[...].astype(F32), second_ref[...].astype(F32)
    return jnp.where(even, first, second).astype(BF), jnp.where(even, second, first).astype(BF)


def stage_kernel(
    core_ref, feats_ref, occ_ref, near_ref, cot_from_ref, weight_from_ref, bias_from_ref,
    first_ref, rows_ref, x_ref, keep_ref, cot_ref, weight_ref, bias_ref, near_held_ref, sems,
):
    pairs = (
        (near_ref, near_held_ref), (occ_ref, keep_ref), (feats_ref, x_ref), (cot_from_ref, cot_ref),
        (weight_from_ref, weight_ref), (bias_from_ref, bias_ref),
    )
    copies = [pltpu.make_async_copy(a, b, sems.at[i]) for i, (a, b) in enumerate(pairs)]
    for copy in copies:
        copy.start()
    bricks, _, voxels = x_ref.shape
    copies[0].wait()
    fill_slot_rows(near_held_ref, rows_ref, bricks)
    copies[1].wait()
    copies[2].wait()
    keep = keep_ref[...].astype(F32)
    faces = []
    for i, start in enumerate((0, voxels - 128)):
        at = slice(start, start + 128)
        tiles = [x_ref[m, :, at].astype(F32) * keep[m : m + 1, at] for m in range(bricks)]
        faces.append(to_planes(tiles)[i])
    first_ref[...] = jnp.where(core_ref[0] == 0, faces[1], faces[0]).astype(BF)
    for copy in copies[3:]:
        copy.wait()


def planes_kernel(core_ref, feats_ref, occ_ref, planes_ref, occ2_ref, second_ref):
    bricks, channels, voxels = feats_ref.shape
    keep = occ_ref[...].astype(F32)
    for t in range(voxels // 128):
        at = slice(128 * t, 128 * t + 128)
        kept = [jnp.broadcast_to(keep[m : m + 1, at], (channels, 128)) for m in range(bricks)]
        first, second = to_planes([feats_ref[m, :, at].astype(F32) * kept[m] for m in range(bricks)])
        planes_ref[2 * t] = first.astype(BF)
        planes_ref[2 * t + 1] = second.astype(BF)
        first, second = to_planes([kept[m][:8] for m in range(bricks)])
        occ2_ref[2 * t] = first
        occ2_ref[2 * t + 1] = second
    low, high = planes_ref[0].astype(F32), planes_ref[planes_ref.shape[0] - 1].astype(F32)
    second_ref[...] = jnp.where(core_ref[0] == 0, low, high).astype(BF)


def ahead_weights(weight_ref, ahead_ref):
    channels = weight_ref.shape[1]
    for r in range(3):
        blocks = [weight_ref[9 * (2 - r) + k].astype(F32) for k in range(9)]
        ahead_ref[channels * r : channels * (r + 1), :] = jnp.concatenate(blocks, axis=1).astype(BF)


def back_weights(weight_ref, back_ref):
    channels = weight_ref.shape[1]
    for r in range(3):
        blocks = [weight_ref[9 * r + 8 - k].astype(F32).T for k in range(9)]
        back_ref[channels * r : channels * (r + 1), :] = jnp.concatenate(blocks, axis=1).astype(BF)


def shifted(flat, moved_ref, rows_ref, bricks, channels):
    rows = slot_rows(rows_ref, 0)
    count = moved_ref.shape[0]
    for b in range(3):
        for c in range(3):
            k = 3 * b + c
            if k == 4:
                part = flat
            else:
                part = dot(flat, selection(rows, b, c, bricks)).astype(BF)
            moved_ref[:, channels * k : channels * (k + 1), :] = part.reshape(
                count, channels, bricks * PLANE
            )


def add_products(core_ref, weight_ref, moved_ref, total_ref):
    channels = weight_ref.shape[0] // 3

    @phase(core_ref)
    def _():
        for x in range(moved_ref.shape[0]):
            at = slice(channels * x, channels * (x + 3))
            total_ref[at, :] += dot(weight_ref[...], moved_ref[x])


def shifted_face(face, rows, bricks):
    parts = []
    for b in range(3):
        for c in range(3):
            parts.append(dot(face, selection(rows, b, c, bricks)).astype(BF))
    return jnp.concatenate(parts, axis=0)


def side_rows(rows_ref, low):
    below, above = slot_rows(rows_ref, -1), slot_rows(rows_ref, 1)
    return {key: jnp.where(low, below[key], above[key]) for key in below}


def inner_kernel(
    core_ref, rows_ref, planes_ref, occ_ref, cot_ref, weight_ref, bias_ref,
    moved_ref, pre_ref, cot2_ref, ahead_ref, total_ref,
):
    bricks, channels, voxels = cot_ref.shape
    flat = planes_ref[...].reshape(planes_ref.shape[0] * channels, bricks * PLANE)
    shifted(flat, moved_ref, rows_ref, bricks, channels)
    keep = occ_ref[...].astype(F32)
    for t in range(voxels // 128):
        at = slice(128 * t, 128 * t + 128)
        kept = [jnp.broadcast_to(keep[m : m + 1, at], (channels, 128)) for m in range(bricks)]
        first, second = to_planes([cot_ref[m, :, at].astype(F32) * kept[m] for m in range(bricks)])
        cot2_ref[2 * t] = first.astype(BF)
        cot2_ref[2 * t + 1] = second.astype(BF)
    ahead_weights(weight_ref, ahead_ref)
    count = planes_ref.shape[0]
    at = (channels, channels)
    same = lax.broadcasted_iota(jnp.int32, at, 0) == lax.broadcasted_iota(jnp.int32, at, 1)
    column = jnp.sum(jnp.where(same, bias_ref[...], 0.0), axis=1, keepdims=True)
    start = jnp.broadcast_to(column, (channels, bricks * PLANE))
    for x in range(count + 2):
        total_ref[channels * x : channels * (x + 1), :] = start
    add_products(core_ref, ahead_ref, moved_ref, total_ref)
    pre_ref[...] = total_ref[channels : channels * (count + 1), :].reshape(pre_ref.shape)


def terms_of(padded_ref, x, start, half, moved):
    channels = moved.shape[0] // 9
    rows = pl.ds(pl.multiple_of(channels * (x + 1) + start, 32), half)
    return dot_t(padded_ref[rows, :], moved)


def activate(pre, masked, cot, keep):
    sig = jax.nn.sigmoid(pre)
    result = (masked + keep * pre * sig).astype(BF)
    return result, (cot * sig * (1.0 + pre * (1.0 - sig))).astype(BF)


def store_terms(terms, copies_ref, start, out_ref):
    half = terms.shape[0]
    unit = half // 3
    full = terms.shape[1] // 128
    for t in range(full):
        out_ref[half * t : half * (t + 1), :] = terms[:, 128 * t : 128 * t + 128].astype(out_ref.dtype)
    last = terms[:, 128 * full :]
    copies = jnp.where(start == 0, copies_ref[...], 0.0)
    one = jnp.concatenate([last[:unit], last[unit : 2 * unit]], axis=1)
    two = jnp.concatenate([last[2 * unit :], copies], axis=1)
    at = half * full
    out_ref[at : at + unit, :] = one.astype(out_ref.dtype)
    out_ref[at + unit : at + 2 * unit, :] = two.astype(out_ref.dtype)


def first_outer_kernel(
    core_ref, own_ref, rows_ref, face_ref, moved_ref, pre_ref, cot2_ref, occ2_ref, weight_ref,
    result_ref, padded_ref, face_moved_ref, partial_ref, bias_ref,
):
    count, channels, lanes = pre_ref.shape
    bricks = lanes // PLANE
    even = core_ref[0] == 0
    face_moved_ref[...] = shifted_face(face_ref[...], side_rows(rows_ref, even), bricks)
    at = pl.multiple_of(jnp.where(even, 2 * channels, 0), channels)
    add = dot(weight_ref[pl.ds(at, channels), :], face_moved_ref[...])
    padded_ref[0 : 2 * channels, :] = jnp.zeros((2 * channels, lanes), BF)
    padded_ref[channels * (count + 2) :, :] = jnp.zeros((2 * channels, lanes), BF)
    bias = jnp.zeros((channels, lanes), F32)
    for x in range(count):
        pre = pre_ref[x]
        if x in (0, count - 1):
            pre = pre + add
        keep = jnp.broadcast_to(occ2_ref[x][0:1], (channels, lanes))
        masked = moved_ref[x, 4 * channels : 5 * channels, :].astype(F32)
        result, grad = activate(pre, masked, cot2_ref[x].astype(F32), keep)
        if x in (0, count - 1):
            there = even if x == 0 else jnp.logical_not(even)
            grad = jnp.where(there, grad.astype(F32), 0.0).astype(BF)
        result_ref[x] = result
        padded_ref[channels * (x + 2) : channels * (x + 3), :] = grad
        bias = bias + grad.astype(F32)
    bias_ref[...] = bias
    half = partial_ref.shape[0]
    start = (1 - own_ref[0]) * half
    terms = terms_of(padded_ref, jnp.where(even, -1, count), start, half, face_moved_ref[...])
    for x in range(count):
        terms = terms + terms_of(padded_ref, x, start, half, moved_ref[x])
    partial_ref[...] = terms


def second_outer_kernel(
    core_ref, own_ref, rows_ref, face_ref, moved_ref, pre_ref, cot2_ref, occ2_ref, weight_ref,
    begun_ref, partial_ref, bias_ref,
    result_ref, padded_ref, face_moved_ref, theirs_ref, copies_ref,
    late_ref,
):
    count, channels, lanes = pre_ref.shape
    bricks = lanes // PLANE
    even = core_ref[0] == 0
    plane = jnp.where(even, count - 1, 0)
    inward = jnp.where(even, -1, 1)
    face_moved_ref[...] = shifted_face(
        face_ref[...], side_rows(rows_ref, jnp.logical_not(even)), bricks
    )
    at = pl.multiple_of(jnp.where(even, 0, 2 * channels), channels)
    add = dot(weight_ref[pl.ds(at, channels), :], face_moved_ref[...])
    keep = jnp.broadcast_to(occ2_ref[plane][0:1], (channels, lanes))
    masked = moved_ref[plane, 4 * channels : 5 * channels, :].astype(F32)
    cot = cot2_ref[plane].astype(F32)
    result, grad = activate(pre_ref[plane] + add, masked, cot, keep)
    result_ref[...] = result
    padded_ref[...] = begun_ref[...]
    padded_ref[pl.ds(pl.multiple_of(channels * (plane + 2), channels), channels), :] = grad
    late_ref[...] = jnp.zeros(late_ref.shape, BF)
    late_ref[2 * channels : 3 * channels, :] = grad
    same = lax.broadcasted_iota(jnp.int32, (channels, channels), 0)
    same = same == lax.broadcasted_iota(jnp.int32, (channels, channels), 1)
    bias = jnp.sum(bias_ref[...] + grad.astype(F32), axis=1, keepdims=True)
    row = jnp.sum(jnp.where(same, bias, 0.0), axis=0, keepdims=True)
    copies_ref[...] = row * spread(copies_ref.shape)
    half = partial_ref.shape[0]
    start = (1 - own_ref[0]) * half
    terms = partial_ref[...] + terms_of(late_ref, -inward, start, half, face_moved_ref[...])
    terms = terms + terms_of(late_ref, 0, start, half, moved_ref[plane])
    terms = terms + terms_of(late_ref, inward, start, half, moved_ref[plane + inward])
    store_terms(terms, copies_ref, start, theirs_ref)
    low = padded_ref[2 * channels : 3 * channels, :].astype(F32)
    high = padded_ref[channels * (count + 1) : channels * (count + 2), :].astype(F32)
    face = jnp.where(even, low, high).astype(BF)
    size = theirs_ref.shape[0] - channels * (lanes // 128)
    for t in range(lanes // 128):
        theirs_ref[size + channels * t : size + channels * (t + 1), :] = face[:, 128 * t : 128 * t + 128]


def own_kernel(
    core_ref, own_ref, padded_ref, moved_ref, first_ref, second_ref, copies_ref, mine_ref
):
    count = moved_ref.shape[0]
    half = 3 * copies_ref.shape[1] // 2
    start = own_ref[0] * half
    even = core_ref[0] == 0
    terms = terms_of(padded_ref, jnp.where(even, -1, count), start, half, first_ref[...])
    for x in range(count):
        terms = terms + terms_of(padded_ref, x, start, half, moved_ref[x])
    terms = terms + terms_of(padded_ref, jnp.where(even, count, -1), start, half, second_ref[...])
    store_terms(terms, copies_ref, start, mine_ref)


def spread(shape):
    return 1.0 + lax.broadcasted_iota(jnp.int32, shape, 0).astype(F32) * (1.0 / shape[0])


def first_sum_kernel(core_ref, mine_ref, other_ref, padded_ref, out_ref, faces_ref):
    size = mine_ref.shape[0]
    out_ref[...] = (mine_ref[...] + other_ref[0:size, :].astype(F32)).astype(BF)
    channels, lanes = faces_ref.shape[0] // 2, faces_ref.shape[1]
    end = padded_ref.shape[0] - 2 * channels
    even = core_ref[0] == 0
    low = padded_ref[2 * channels : 3 * channels, :].astype(F32)
    high = padded_ref[end - channels : end, :].astype(F32)
    faces_ref[0:channels, :] = jnp.where(even, high, low).astype(BF)
    for t in range(lanes // 128):
        rows = slice(size + channels * t, size + channels * (t + 1))
        faces_ref[channels:, 128 * t : 128 * t + 128] = other_ref[rows, :]


def sum_kernel(mine_ref, other_ref, *refs):
    out_ref = refs[-1]
    out_ref[...] = (mine_ref[...].astype(F32) + other_ref[...].astype(F32)).astype(out_ref.dtype)


def back_inner_kernel(
    core_ref, rows_ref, padded_ref, result2_ref, late_ref, weight_ref, after_ref,
    result_ref, total_ref, back_ref, moved_ref,
):
    count, channels, lanes = result2_ref.shape
    bricks = lanes // PLANE
    back_weights(weight_ref, back_ref)
    flat = padded_ref[2 * channels : channels * (count + 2), :]
    shifted(flat, moved_ref, rows_ref, bricks, channels)
    total_ref[...] = jnp.zeros(total_ref.shape, F32)
    add_products(core_ref, back_ref, moved_ref, total_ref)
    even = core_ref[0] == 0
    late = late_ref[...].astype(F32)
    for t in range(count // 2):
        first, second = result2_ref[2 * t].astype(F32), result2_ref[2 * t + 1].astype(F32)
        if t == 0:
            first = jnp.where(even, first, late)
        if t == count // 2 - 1:
            second = jnp.where(even, late, second)
        out = from_planes(first, second)
        for m in range(bricks):
            result_ref[m, :, 128 * t : 128 * t + 128] = out[m].astype(BF)


def back_outer_kernel(
    core_ref, rows_ref, first_ref, second_ref, total_ref, cot_ref, occ_ref, weight_ref, after_ref,
    in_grad_ref, done_ref,
):
    bricks, channels, voxels = cot_ref.shape
    count = voxels // PLANE
    done_ref[...] = jnp.zeros(done_ref.shape, F32)
    low, high = load_faces(core_ref, first_ref, second_ref)
    moved_low = shifted_face(low, slot_rows(rows_ref, -1), bricks)
    moved_high = shifted_face(high, slot_rows(rows_ref, 1), bricks)
    add_low = dot(weight_ref[2 * channels : 3 * channels, :], moved_low)
    add_high = dot(weight_ref[0:channels, :], moved_high)
    keep = occ_ref[...].astype(F32)
    for t in range(count // 2):
        at = slice(128 * t, 128 * t + 128)
        first = total_ref[channels * (2 * t + 1) : channels * (2 * t + 2), :]
        second = total_ref[channels * (2 * t + 2) : channels * (2 * t + 3), :]
        if t == 0:
            first = first + add_low
        if t == count // 2 - 1:
            second = second + add_high
        back = from_planes(first, second)
        for m in range(bricks):
            in_grad_ref[m, :, at] = (
                keep[m : m + 1, at] * (cot_ref[m, :, at].astype(F32) + back[m])
            ).astype(BF)


def arrived_bias(scale, source_ref, channels):
    unit = channels // 2
    rows = source_ref.shape[0]
    tile = pltpu.roll(source_ref[rows - unit : rows, :], 128 - channels, 1)[:, :channels]
    return jnp.sum(tile * (scale / (spread(tile.shape) * unit)), axis=0, keepdims=True)


def store_half(scale, mine, source_ref, weight_ref, held_ref, sems):
    half, unit, channels = 3 * held_ref.shape[3] // 2, held_ref.shape[2], held_ref.shape[3]
    copies = []
    for j in range(3):
        for t in range(4):
            rows = slice(half * t + unit * j, half * t + unit * (j + 1))
            tile = source_ref[rows, :] * scale
            held_ref[j, 2 * t] = tile[:, :channels]
            held_ref[j, 2 * t + 1] = pltpu.roll(tile, 128 - channels, 1)[:, :channels]
        at = 4 * half + unit * (j // 2)
        tile = source_ref[at : at + unit, :] * scale
        if j == 1:
            tile = pltpu.roll(tile, 128 - channels, 1)
        held_ref[j, 8] = tile[:, :channels]
        u = 3 * mine + j
        place = weight_ref.at[
            pl.ds(9 * (2 - u // 2), 9), pl.ds(pl.multiple_of(unit * (u % 2), unit), unit), :
        ]
        copies.append(pltpu.make_async_copy(held_ref.at[j], place, sems.at[j]))
        copies[-1].start()
    return copies


def own_half_kernel(scale, own_ref, source_ref, weight_ref, bias_ref, held_ref, sems):
    copies = store_half(scale, own_ref[0], source_ref, weight_ref, held_ref, sems)
    bias_ref[...] = arrived_bias(scale, source_ref, held_ref.shape[3])
    for copy in copies:
        copy.wait()


def other_half_kernel(
    scale, own_ref, source_ref, begun_ref, own_bias_ref,
    weight_ref, bias_ref, held_ref, bias_held_ref, sems,
):
    bias = arrived_bias(scale, source_ref, held_ref.shape[3])
    bias_held_ref[...] = jnp.where(own_ref[0] == 0, own_bias_ref[...], bias)
    copies = [pltpu.make_async_copy(bias_held_ref, bias_ref, sems.at[3])]
    copies[0].start()
    copies += store_half(scale, 1 - own_ref[0], source_ref, weight_ref, held_ref, sems)
    for copy in copies:
        copy.wait()


def call(body, outs, ins, scratch=(), flops=0, out_specs=None, aliases=None):
    shapes = [jax.ShapeDtypeStruct(shape, dtype) for shape, dtype in outs]
    moved = sum(math.prod(s.shape) * s.dtype.itemsize for s in shapes)
    moved += sum(math.prod(x.shape) * x.dtype.itemsize for _, x in ins)
    return pl.pallas_call(
        body,
        out_shape=shapes,
        in_specs=[spec for spec, _ in ins],
        out_specs=out_specs or [VMEM] * len(shapes),
        input_output_aliases=aliases or {},
        scratch_shapes=list(scratch),
        compiler_params=pltpu.CompilerParams(vmem_limit_bytes=32 << 20),
        cost_estimate=pl.CostEstimate(flops=flops, bytes_accessed=moved, transcendentals=0),
    )(*[pltpu.with_memory_space_constraint(x, pltpu.HBM) if s is HBM else x for s, x in ins])


def face_pairs():
    spaces, reps = lax.axis_size("space"), lax.axis_size("rep")
    pairs = []
    for space in range(spaces):
        for rep in range(reps):
            step = 1 if rep % 2 == 0 else -1
            there, to = space + step, rep
            if not 0 <= there < spaces:
                there, to = space, rep ^ 1
            pairs.append((space * reps + rep, there * reps + to))
    return pairs


def on_device(feats, cotangent, weight, bias, neighbours, occupancy):
    x, cot, near, occ = feats[0], cotangent[0], neighbours[0], occupancy[0]
    bricks, channels, voxels = x.shape
    count, lanes = voxels // PLANE, bricks * PLANE
    width = 9 * channels
    plane = ((channels, lanes), BF)
    core = (lax.axis_index("rep") % 2).astype(jnp.int32)
    cores = core[None]
    first, rows, x, occ, cot, weight, bias = call(
        stage_kernel,
        [
            plane, ((32, lanes), jnp.int32), (x.shape, BF), (occ.shape, jnp.int32), (x.shape, BF),
            (weight.shape, BF), ((1, channels), F32),
        ],
        [
            (SMEM, cores), (HBM, x), (HBM, occ), (HBM, near), (HBM, cot), (HBM, weight),
            (HBM, bias[None]),
        ],
        [pltpu.SMEM(near.shape, jnp.int32), pltpu.SemaphoreType.DMA((6,))],
    )
    axes = ("space", "rep")
    pairs = face_pairs()
    first = lax.ppermute(first, axes, pairs)
    planes, occ2, second = call(
        planes_kernel,
        [((count, channels, lanes), BF), ((count, 8, lanes), F32), plane],
        [(SMEM, cores), (VMEM, x), (VMEM, occ)],
    )
    second = lax.ppermute(second, axes, [(j, i) for i, j in pairs])
    moved, pre, cot2, ahead = call(
        inner_kernel,
        [
            ((count, width, lanes), BF),
            ((count, channels, lanes), F32),
            ((count, channels, lanes), BF),
            ((3 * channels, width), BF),
        ],
        [
            (SMEM, cores), (VMEM, rows), (VMEM, planes), (VMEM, occ), (VMEM, cot), (VMEM, weight),
            (VMEM, bias),
        ],
        [pltpu.VMEM((channels * (count + 2), lanes), F32)],
        flops=2 * 27 * channels * channels * bricks * voxels,
    )
    devices = lax.axis_size("space") * lax.axis_size("rep")
    me = lax.axis_index("space") * lax.axis_size("rep") + lax.axis_index("rep")
    own = (lax.population_count(me.astype(jnp.int32)) & 1)[None]
    size = 3 * channels // 2 * (width // 128) + channels
    field = [(VMEM, moved), (VMEM, pre), (VMEM, cot2), (VMEM, occ2), (VMEM, ahead)]
    result2, begun, moved_first, partial, bias_part = call(
        first_outer_kernel,
        [
            ((count, channels, lanes), BF),
            ((channels * (count + 4), lanes), BF),
            ((width, lanes), BF),
            ((3 * channels // 2, width), F32),
            ((channels, lanes), F32),
        ],
        [(SMEM, cores), (SMEM, own), (VMEM, rows), (VMEM, first)] + field,
        flops=14 * channels * channels * bricks * voxels,
    )
    late, padded, moved_second, theirs, copies = call(
        second_outer_kernel,
        [
            plane,
            ((channels * (count + 4), lanes), BF),
            ((width, lanes), BF),
            ((size + channels * lanes // 128, 128), BF),
            ((channels // 2, channels), F32),
        ],
        [(SMEM, cores), (SMEM, own), (VMEM, rows), (VMEM, second)]
        + field
        + [(VMEM, begun), (VMEM, partial), (VMEM, bias_part)],
        [pltpu.VMEM((5 * channels, lanes), BF)],
        flops=14 * channels * channels * bricks * voxels,
    )
    partner = [(i, i ^ 1) for i in range(devices)]
    other = lax.ppermute(theirs, axes, partner)
    (mine,) = call(
        own_kernel,
        [((size, 128), F32)],
        [
            (SMEM, cores), (SMEM, own), (VMEM, padded), (VMEM, moved), (VMEM, moved_first),
            (VMEM, moved_second), (VMEM, copies),
        ],
        flops=27 * channels * channels * bricks * voxels,
    )
    sent = ((size, 128), BF)
    mine, faces = call(
        first_sum_kernel,
        [sent, ((2 * channels, lanes), BF)],
        [(SMEM, cores), (VMEM, mine), (VMEM, other), (VMEM, padded)],
    )
    bits = [1 << i for i in range(1, (devices).bit_length() - 1)]
    rounds = list(zip(bits[:1] + bits[-1:] + bits[1:-1], bits[-1:] + bits[1:-1] + bits[:1]))
    for i, steps in enumerate(rounds):
        joined = [(j, j ^ 1 ^ steps[j.bit_count() % 2]) for j in range(devices)]
        other = lax.ppermute(mine, axes, joined)
        held = []
        if i == 0:
            faces = lax.ppermute(faces, axes, pairs)
            result, total, back = call(
                back_inner_kernel,
                [
                    ((bricks, channels, voxels), BF),
                    ((channels * (count + 2), lanes), F32),
                    ((3 * channels, width), BF),
                ],
                [
                    (SMEM, cores), (VMEM, rows), (VMEM, padded), (VMEM, result2), (VMEM, late),
                    (VMEM, weight), (ANY, mine),
                ],
                [pltpu.VMEM((count, width, lanes), BF)],
                flops=2 * 27 * channels * channels * bricks * voxels,
            )
            held = [total]
        if i == 2:
            first, second = faces[:channels], lax.ppermute(faces[channels:], axes, partner)
            held = [second]
        if i == 3:
            in_grad, done = call(
                back_outer_kernel,
                [((bricks, channels, voxels), BF), ((8, 128), F32)],
                [
                    (SMEM, cores), (VMEM, rows), (VMEM, first), (VMEM, second), (VMEM, total),
                    (VMEM, cot), (VMEM, occ), (VMEM, back), (ANY, mine),
                ],
                flops=2 * 6 * channels * channels * bricks * voxels,
            )
            held = [done]
        last = i == len(rounds) - 1
        (mine,) = call(
            sum_kernel,
            [(sent[0], F32 if last else BF)],
            [(VMEM, mine), (VMEM, other)] + [(ANY, h) for h in held],
        )
    other = lax.ppermute(mine, axes, partner)
    normaliser = 1.0 / math.sqrt(
        feats.shape[0] * lax.axis_size("rep") * bricks * lax.axis_size("space") * voxels
    )
    held = pltpu.VMEM((3, 9, channels // 2, channels), F32)
    outs = [(weight.shape, F32), ((1, channels), F32)]
    weight_grad, bias_grad = call(
        functools.partial(own_half_kernel, normaliser),
        outs,
        [(SMEM, own), (VMEM, mine)],
        [held, pltpu.SemaphoreType.DMA((3,))],
        out_specs=[HBM, VMEM],
    )
    weight_grad, bias_grad = call(
        functools.partial(other_half_kernel, normaliser),
        outs,
        [(SMEM, own), (VMEM, other), (ANY, weight_grad), (VMEM, bias_grad)],
        [held, pltpu.VMEM((1, channels), F32), pltpu.SemaphoreType.DMA((4,))],
        out_specs=[HBM, HBM],
        aliases={2: 0},
    )
    return result[None], in_grad[None], weight_grad, bias_grad[0]


def solution(mesh):
    placed = (
        P("rep", "space", None, None),
        P("rep", "space", None, None),
        P(),
        P(),
        P("rep", "space", None),
        P("rep", "space", None),
    )
    return jax.shard_map(
        on_device,
        mesh=mesh,
        in_specs=placed,
        out_specs=(P("rep", "space", None, None), P("rep", "space", None, None), P(), P()),
        check_vma=False,
    )
```

```python
import functools
import math

import jax
import jax.numpy as jnp
from jax import lax
from jax.experimental import pallas as pl
from jax.experimental.pallas import tpu as pltpu
from jax.sharding import PartitionSpec as P

BF, F32 = jnp.bfloat16, jnp.float32
DIRECTIONS = [
    (a, b, c) for a in (-1, 0, 1) for b in (-1, 0, 1) for c in (-1, 0, 1) if (a, b, c) != (0, 0, 0)
]
PLANE = 64
VMEM = pl.BlockSpec(memory_space=pltpu.VMEM)
ANY = pl.BlockSpec(memory_space=pl.ANY)
HBM = pl.BlockSpec(memory_space=pltpu.HBM)
SMEM = pl.BlockSpec(memory_space=pltpu.SMEM)


def to_planes(tiles):
    low = lax.broadcasted_iota(jnp.int32, tiles[0].shape, 1) < PLANE
    turned = [pltpu.roll(tile, PLANE, 1) for tile in tiles]
    first, second = [], []
    for m in range(0, len(tiles), 2):
        first.append(jnp.where(low, tiles[m], turned[m + 1]))
        second.append(jnp.where(low, turned[m], tiles[m + 1]))
    return jnp.concatenate(first, axis=1), jnp.concatenate(second, axis=1)


def from_planes(first, second):
    low = lax.broadcasted_iota(jnp.int32, (first.shape[0], 128), 1) < PLANE
    tiles = []
    for g in range(first.shape[1] // 128):
        one = first[:, 128 * g : 128 * g + 128]
        two = second[:, 128 * g : 128 * g + 128]
        tiles.append(jnp.where(low, one, pltpu.roll(two, PLANE, 1)))
        tiles.append(jnp.where(low, pltpu.roll(one, PLANE, 1), two))
    return tiles


SHIFTS = [(a, b, c) for a in (-1, 0, 1) for b in (-1, 0, 1) for c in (-1, 0, 1)]


def fill_slot_rows(near_ref, rows_ref, bricks):
    lane = lax.broadcasted_iota(jnp.int32, (1, bricks * PLANE), 1)
    brick = lane // PLANE
    for d, shift in enumerate(SHIFTS):
        if shift == (0, 0, 0):
            rows_ref[d : d + 1, :] = brick * PLANE
            continue
        j = DIRECTIONS.index(shift)
        found = jnp.full(lane.shape, -(1 << 20), jnp.int32)
        for n in range(bricks):
            chosen = near_ref[n, j]
            row = jnp.where(chosen >= 0, lax.rem(chosen, bricks) * PLANE, -(1 << 20))
            found = jnp.where(brick == n, row, found)
        rows_ref[d : d + 1, :] = found


def slot_rows(rows_ref, dx):
    rows = {}
    for d, (a, b, c) in enumerate(SHIFTS):
        if a == dx:
            rows[b, c] = rows_ref[d : d + 1, :]
    return rows


def selection(rows, b, c, bricks):
    size = bricks * PLANE
    lane = lax.broadcasted_iota(jnp.int32, (1, size), 1)
    y = ((lane >> 3) & 7) + (b - 1)
    z = (lane & 7) + (c - 1)
    out_y = (y < 0) | (y > 7)
    out_z = (z < 0) | (z > 7)
    base = rows[0, 0]
    if b != 1:
        base = jnp.where(out_y, rows[b - 1, 0], base)
    if c != 1:
        base = jnp.where(out_z, rows[0, c - 1], base)
    if b != 1 and c != 1:
        base = jnp.where(out_y & out_z, rows[b - 1, c - 1], base)
    source = base + (y & 7) * 8 + (z & 7)
    row = lax.broadcasted_iota(jnp.int32, (size, size), 0)
    return jnp.where(row == source, 1.0, 0.0).astype(BF)


def phase(scalar_ref):
    return pl.when(scalar_ref[0] >= 0)


def dot(x, y):
    return lax.dot_general(x, y, (((1,), (0,)), ((), ())), preferred_element_type=F32)


def dot_t(x, y):
    return lax.dot_general(x, y, (((1,), (1,)), ((), ())), preferred_element_type=F32)


def load_faces(core_ref, first_ref, second_ref):
    even = core_ref[0] == 0
    first, second = first_ref[...].astype(F32), second_ref[...].astype(F32)
    return jnp.where(even, first, second).astype(BF), jnp.where(even, second, first).astype(BF)


def stage_kernel(
    core_ref, feats_ref, occ_ref, near_ref, cot_from_ref, weight_from_ref, bias_from_ref,
    first_ref, rows_ref, x_ref, keep_ref, cot_ref, weight_ref, bias_ref, near_held_ref, sems,
):
    pairs = (
        (near_ref, near_held_ref), (occ_ref, keep_ref), (feats_ref, x_ref), (cot_from_ref, cot_ref),
        (weight_from_ref, weight_ref), (bias_from_ref, bias_ref),
    )
    copies = [pltpu.make_async_copy(a, b, sems.at[i]) for i, (a, b) in enumerate(pairs)]
    for copy in copies:
        copy.start()
    bricks, _, voxels = x_ref.shape
    copies[0].wait()
    fill_slot_rows(near_held_ref, rows_ref, bricks)
    copies[1].wait()
    copies[2].wait()
    keep = keep_ref[...].astype(F32)
    faces = []
    for i, start in enumerate((0, voxels - 128)):
        at = slice(start, start + 128)
        tiles = [x_ref[m, :, at].astype(F32) * keep[m : m + 1, at] for m in range(bricks)]
        faces.append(to_planes(tiles)[i])
    first_ref[...] = jnp.where(core_ref[0] == 0, faces[1], faces[0]).astype(BF)
    for copy in copies[3:]:
        copy.wait()


def planes_kernel(core_ref, feats_ref, occ_ref, planes_ref, occ2_ref, second_ref):
    bricks, channels, voxels = feats_ref.shape
    keep = occ_ref[...].astype(F32)
    for t in range(voxels // 128):
        at = slice(128 * t, 128 * t + 128)
        kept = [jnp.broadcast_to(keep[m : m + 1, at], (channels, 128)) for m in range(bricks)]
        first, second = to_planes([feats_ref[m, :, at].astype(F32) * kept[m] for m in range(bricks)])
        planes_ref[2 * t] = first.astype(BF)
        planes_ref[2 * t + 1] = second.astype(BF)
        first, second = to_planes([kept[m][:8] for m in range(bricks)])
        occ2_ref[2 * t] = first
        occ2_ref[2 * t + 1] = second
    low, high = planes_ref[0].astype(F32), planes_ref[planes_ref.shape[0] - 1].astype(F32)
    second_ref[...] = jnp.where(core_ref[0] == 0, low, high).astype(BF)


def ahead_weights(weight_ref, ahead_ref):
    channels = weight_ref.shape[1]
    for r in range(3):
        blocks = [weight_ref[9 * (2 - r) + k].astype(F32) for k in range(9)]
        ahead_ref[channels * r : channels * (r + 1), :] = jnp.concatenate(blocks, axis=1).astype(BF)


def back_weights(weight_ref, back_ref):
    channels = weight_ref.shape[1]
    for r in range(3):
        blocks = [weight_ref[9 * r + 8 - k].astype(F32).T for k in range(9)]
        back_ref[channels * r : channels * (r + 1), :] = jnp.concatenate(blocks, axis=1).astype(BF)


def shifted(flat, moved_ref, rows_ref, bricks, channels):
    rows = slot_rows(rows_ref, 0)
    count = moved_ref.shape[0]
    for b in range(3):
        for c in range(3):
            k = 3 * b + c
            if k == 4:
                part = flat
            else:
                part = dot(flat, selection(rows, b, c, bricks)).astype(BF)
            moved_ref[:, channels * k : channels * (k + 1), :] = part.reshape(
                count, channels, bricks * PLANE
            )


def add_products(core_ref, weight_ref, moved_ref, total_ref):
    channels = weight_ref.shape[0] // 3

    @phase(core_ref)
    def _():
        for x in range(moved_ref.shape[0]):
            at = slice(channels * x, channels * (x + 3))
            total_ref[at, :] += dot(weight_ref[...], moved_ref[x])


def shifted_face(face, rows, bricks):
    parts = []
    for b in range(3):
        for c in range(3):
            parts.append(dot(face, selection(rows, b, c, bricks)).astype(BF))
    return jnp.concatenate(parts, axis=0)


def side_rows(rows_ref, low):
    below, above = slot_rows(rows_ref, -1), slot_rows(rows_ref, 1)
    return {key: jnp.where(low, below[key], above[key]) for key in below}


def inner_kernel(
    core_ref, rows_ref, planes_ref, occ_ref, cot_ref, weight_ref, bias_ref,
    moved_ref, pre_ref, cot2_ref, ahead_ref, total_ref,
):
    bricks, channels, voxels = cot_ref.shape
    flat = planes_ref[...].reshape(planes_ref.shape[0] * channels, bricks * PLANE)
    shifted(flat, moved_ref, rows_ref, bricks, channels)
    keep = occ_ref[...].astype(F32)
    for t in range(voxels // 128):
        at = slice(128 * t, 128 * t + 128)
        kept = [jnp.broadcast_to(keep[m : m + 1, at], (channels, 128)) for m in range(bricks)]
        first, second = to_planes([cot_ref[m, :, at].astype(F32) * kept[m] for m in range(bricks)])
        cot2_ref[2 * t] = first.astype(BF)
        cot2_ref[2 * t + 1] = second.astype(BF)
    ahead_weights(weight_ref, ahead_ref)
    count = planes_ref.shape[0]
    at = (channels, channels)
    same = lax.broadcasted_iota(jnp.int32, at, 0) == lax.broadcasted_iota(jnp.int32, at, 1)
    column = jnp.sum(jnp.where(same, bias_ref[...], 0.0), axis=1, keepdims=True)
    start = jnp.broadcast_to(column, (channels, bricks * PLANE))
    for x in range(count + 2):
        total_ref[channels * x : channels * (x + 1), :] = start
    add_products(core_ref, ahead_ref, moved_ref, total_ref)
    pre_ref[...] = total_ref[channels : channels * (count + 1), :].reshape(pre_ref.shape)


def terms_of(padded_ref, x, start, half, moved):
    channels = moved.shape[0] // 9
    rows = pl.ds(pl.multiple_of(channels * (x + 1) + start, 32), half)
    return dot_t(padded_ref[rows, :], moved)


def activate(pre, masked, cot, keep):
    sig = jax.nn.sigmoid(pre)
    result = (masked + keep * pre * sig).astype(BF)
    return result, (cot * sig * (1.0 + pre * (1.0 - sig))).astype(BF)


def store_terms(terms, copies_ref, start, out_ref):
    half = terms.shape[0]
    unit = half // 3
    full = terms.shape[1] // 128
    for t in range(full):
        out_ref[half * t : half * (t + 1), :] = terms[:, 128 * t : 128 * t + 128].astype(out_ref.dtype)
    last = terms[:, 128 * full :]
    copies = jnp.where(start == 0, copies_ref[...], 0.0)
    one = jnp.concatenate([last[:unit], last[unit : 2 * unit]], axis=1)
    two = jnp.concatenate([last[2 * unit :], copies], axis=1)
    at = half * full
    out_ref[at : at + unit, :] = one.astype(out_ref.dtype)
    out_ref[at + unit : at + 2 * unit, :] = two.astype(out_ref.dtype)


def first_outer_kernel(
    core_ref, own_ref, rows_ref, face_ref, moved_ref, pre_ref, cot2_ref, occ2_ref, weight_ref,
    result_ref, padded_ref, face_moved_ref, partial_ref, bias_ref,
):
    count, channels, lanes = pre_ref.shape
    bricks = lanes // PLANE
    even = core_ref[0] == 0
    face_moved_ref[...] = shifted_face(face_ref[...], side_rows(rows_ref, even), bricks)
    at = pl.multiple_of(jnp.where(even, 2 * channels, 0), channels)
    add = dot(weight_ref[pl.ds(at, channels), :], face_moved_ref[...])
    padded_ref[0 : 2 * channels, :] = jnp.zeros((2 * channels, lanes), BF)
    padded_ref[channels * (count + 2) :, :] = jnp.zeros((2 * channels, lanes), BF)
    bias = jnp.zeros((channels, lanes), F32)
    for x in range(count):
        pre = pre_ref[x]
        if x in (0, count - 1):
            pre = pre + add
        keep = jnp.broadcast_to(occ2_ref[x][0:1], (channels, lanes))
        masked = moved_ref[x, 4 * channels : 5 * channels, :].astype(F32)
        result, grad = activate(pre, masked, cot2_ref[x].astype(F32), keep)
        if x in (0, count - 1):
            there = even if x == 0 else jnp.logical_not(even)
            grad = jnp.where(there, grad.astype(F32), 0.0).astype(BF)
        result_ref[x] = result
        padded_ref[channels * (x + 2) : channels * (x + 3), :] = grad
        bias = bias + grad.astype(F32)
    bias_ref[...] = bias
    half = partial_ref.shape[0]
    start = (1 - own_ref[0]) * half
    terms = terms_of(padded_ref, jnp.where(even, -1, count), start, half, face_moved_ref[...])
    for x in range(count):
        terms = terms + terms_of(padded_ref, x, start, half, moved_ref[x])
    partial_ref[...] = terms


def second_outer_kernel(
    core_ref, own_ref, rows_ref, face_ref, moved_ref, pre_ref, cot2_ref, occ2_ref, weight_ref,
    begun_ref, partial_ref, bias_ref,
    result_ref, padded_ref, face_moved_ref, theirs_ref, copies_ref,
    late_ref,
):
    count, channels, lanes = pre_ref.shape
    bricks = lanes // PLANE
    even = core_ref[0] == 0
    plane = jnp.where(even, count - 1, 0)
    inward = jnp.where(even, -1, 1)
    face_moved_ref[...] = shifted_face(
        face_ref[...], side_rows(rows_ref, jnp.logical_not(even)), bricks
    )
    at = pl.multiple_of(jnp.where(even, 0, 2 * channels), channels)
    add = dot(weight_ref[pl.ds(at, channels), :], face_moved_ref[...])
    keep = jnp.broadcast_to(occ2_ref[plane][0:1], (channels, lanes))
    masked = moved_ref[plane, 4 * channels : 5 * channels, :].astype(F32)
    cot = cot2_ref[plane].astype(F32)
    result, grad = activate(pre_ref[plane] + add, masked, cot, keep)
    result_ref[...] = result
    padded_ref[...] = begun_ref[...]
    padded_ref[pl.ds(pl.multiple_of(channels * (plane + 2), channels), channels), :] = grad
    late_ref[...] = jnp.zeros(late_ref.shape, BF)
    late_ref[2 * channels : 3 * channels, :] = grad
    same = lax.broadcasted_iota(jnp.int32, (channels, channels), 0)
    same = same == lax.broadcasted_iota(jnp.int32, (channels, channels), 1)
    bias = jnp.sum(bias_ref[...] + grad.astype(F32), axis=1, keepdims=True)
    row = jnp.sum(jnp.where(same, bias, 0.0), axis=0, keepdims=True)
    copies_ref[...] = row * spread(copies_ref.shape)
    half = partial_ref.shape[0]
    start = (1 - own_ref[0]) * half
    terms = partial_ref[...] + terms_of(late_ref, -inward, start, half, face_moved_ref[...])
    terms = terms + terms_of(late_ref, 0, start, half, moved_ref[plane])
    terms = terms + terms_of(late_ref, inward, start, half, moved_ref[plane + inward])
    store_terms(terms, copies_ref, start, theirs_ref)
    low = padded_ref[2 * channels : 3 * channels, :].astype(F32)
    high = padded_ref[channels * (count + 1) : channels * (count + 2), :].astype(F32)
    face = jnp.where(even, low, high).astype(BF)
    size = theirs_ref.shape[0] - channels * (lanes // 128)
    for t in range(lanes // 128):
        theirs_ref[size + channels * t : size + channels * (t + 1), :] = face[:, 128 * t : 128 * t + 128]


def own_kernel(
    core_ref, own_ref, padded_ref, moved_ref, first_ref, second_ref, copies_ref, mine_ref
):
    count = moved_ref.shape[0]
    half = 3 * copies_ref.shape[1] // 2
    start = own_ref[0] * half
    even = core_ref[0] == 0
    terms = terms_of(padded_ref, jnp.where(even, -1, count), start, half, first_ref[...])
    for x in range(count):
        terms = terms + terms_of(padded_ref, x, start, half, moved_ref[x])
    terms = terms + terms_of(padded_ref, jnp.where(even, count, -1), start, half, second_ref[...])
    store_terms(terms, copies_ref, start, mine_ref)


def spread(shape):
    return 1.0 + lax.broadcasted_iota(jnp.int32, shape, 0).astype(F32) * (1.0 / shape[0])


def first_sum_kernel(core_ref, mine_ref, other_ref, padded_ref, out_ref, faces_ref):
    size = mine_ref.shape[0]
    out_ref[...] = (mine_ref[...] + other_ref[0:size, :].astype(F32)).astype(BF)
    channels, lanes = faces_ref.shape[0] // 2, faces_ref.shape[1]
    end = padded_ref.shape[0] - 2 * channels
    even = core_ref[0] == 0
    low = padded_ref[2 * channels : 3 * channels, :].astype(F32)
    high = padded_ref[end - channels : end, :].astype(F32)
    faces_ref[0:channels, :] = jnp.where(even, high, low).astype(BF)
    for t in range(lanes // 128):
        rows = slice(size + channels * t, size + channels * (t + 1))
        faces_ref[channels:, 128 * t : 128 * t + 128] = other_ref[rows, :]


def sum_kernel(mine_ref, other_ref, *refs):
    out_ref = refs[-1]
    out_ref[...] = (mine_ref[...].astype(F32) + other_ref[...].astype(F32)).astype(out_ref.dtype)


def back_inner_kernel(
    core_ref, rows_ref, padded_ref, result2_ref, late_ref, weight_ref, after_ref,
    result_ref, total_ref, back_ref, moved_ref,
):
    count, channels, lanes = result2_ref.shape
    bricks = lanes // PLANE
    back_weights(weight_ref, back_ref)
    flat = padded_ref[2 * channels : channels * (count + 2), :]
    shifted(flat, moved_ref, rows_ref, bricks, channels)
    total_ref[...] = jnp.zeros(total_ref.shape, F32)
    add_products(core_ref, back_ref, moved_ref, total_ref)
    even = core_ref[0] == 0
    late = late_ref[...].astype(F32)
    for t in range(count // 2):
        first, second = result2_ref[2 * t].astype(F32), result2_ref[2 * t + 1].astype(F32)
        if t == 0:
            first = jnp.where(even, first, late)
        if t == count // 2 - 1:
            second = jnp.where(even, late, second)
        out = from_planes(first, second)
        for m in range(bricks):
            result_ref[m, :, 128 * t : 128 * t + 128] = out[m].astype(BF)


def back_outer_kernel(
    core_ref, rows_ref, first_ref, second_ref, total_ref, cot_ref, occ_ref, weight_ref, after_ref,
    in_grad_ref, done_ref,
):
    bricks, channels, voxels = cot_ref.shape
    count = voxels // PLANE
    done_ref[...] = jnp.zeros(done_ref.shape, F32)
    low, high = load_faces(core_ref, first_ref, second_ref)
    moved_low = shifted_face(low, slot_rows(rows_ref, -1), bricks)
    moved_high = shifted_face(high, slot_rows(rows_ref, 1), bricks)
    add_low = dot(weight_ref[2 * channels : 3 * channels, :], moved_low)
    add_high = dot(weight_ref[0:channels, :], moved_high)
    keep = occ_ref[...].astype(F32)
    for t in range(count // 2):
        at = slice(128 * t, 128 * t + 128)
        first = total_ref[channels * (2 * t + 1) : channels * (2 * t + 2), :]
        second = total_ref[channels * (2 * t + 2) : channels * (2 * t + 3), :]
        if t == 0:
            first = first + add_low
        if t == count // 2 - 1:
            second = second + add_high
        back = from_planes(first, second)
        for m in range(bricks):
            in_grad_ref[m, :, at] = (
                keep[m : m + 1, at] * (cot_ref[m, :, at].astype(F32) + back[m])
            ).astype(BF)


def arrived_bias(scale, source_ref, channels):
    unit = channels // 2
    rows = source_ref.shape[0]
    tile = pltpu.roll(source_ref[rows - unit : rows, :], 128 - channels, 1)[:, :channels]
    return jnp.sum(tile * (scale / (spread(tile.shape) * unit)), axis=0, keepdims=True)


def store_half(scale, mine, source_ref, weight_ref, held_ref, sems):
    half, unit, channels = 3 * held_ref.shape[3] // 2, held_ref.shape[2], held_ref.shape[3]
    copies = []
    for j in range(3):
        for t in range(4):
            rows = slice(half * t + unit * j, half * t + unit * (j + 1))
            tile = source_ref[rows, :] * scale
            held_ref[j, 2 * t] = tile[:, :channels]
            held_ref[j, 2 * t + 1] = pltpu.roll(tile, 128 - channels, 1)[:, :channels]
        at = 4 * half + unit * (j // 2)
        tile = source_ref[at : at + unit, :] * scale
        if j == 1:
            tile = pltpu.roll(tile, 128 - channels, 1)
        held_ref[j, 8] = tile[:, :channels]
        u = 3 * mine + j
        place = weight_ref.at[
            pl.ds(9 * (2 - u // 2), 9), pl.ds(pl.multiple_of(unit * (u % 2), unit), unit), :
        ]
        copies.append(pltpu.make_async_copy(held_ref.at[j], place, sems.at[j]))
        copies[-1].start()
    return copies


def own_half_kernel(scale, own_ref, source_ref, weight_ref, bias_ref, held_ref, sems):
    copies = store_half(scale, own_ref[0], source_ref, weight_ref, held_ref, sems)
    bias_ref[...] = arrived_bias(scale, source_ref, held_ref.shape[3])
    for copy in copies:
        copy.wait()


def other_half_kernel(
    scale, own_ref, source_ref, begun_ref, own_bias_ref,
    weight_ref, bias_ref, held_ref, bias_held_ref, sems,
):
    bias = arrived_bias(scale, source_ref, held_ref.shape[3])
    bias_held_ref[...] = jnp.where(own_ref[0] == 0, own_bias_ref[...], bias)
    copies = [pltpu.make_async_copy(bias_held_ref, bias_ref, sems.at[3])]
    copies[0].start()
    copies += store_half(scale, 1 - own_ref[0], source_ref, weight_ref, held_ref, sems)
    for copy in copies:
        copy.wait()


def call(body, outs, ins, scratch=(), flops=0, out_specs=None, aliases=None):
    shapes = [jax.ShapeDtypeStruct(shape, dtype) for shape, dtype in outs]
    moved = sum(math.prod(s.shape) * s.dtype.itemsize for s in shapes)
    moved += sum(math.prod(x.shape) * x.dtype.itemsize for _, x in ins)
    return pl.pallas_call(
        body,
        out_shape=shapes,
        in_specs=[spec for spec, _ in ins],
        out_specs=out_specs or [VMEM] * len(shapes),
        input_output_aliases=aliases or {},
        scratch_shapes=list(scratch),
        compiler_params=pltpu.CompilerParams(vmem_limit_bytes=32 << 20),
        cost_estimate=pl.CostEstimate(flops=flops, bytes_accessed=moved, transcendentals=0),
    )(*[pltpu.with_memory_space_constraint(x, pltpu.HBM) if s is HBM else x for s, x in ins])


def face_pairs():
    spaces, reps = lax.axis_size("space"), lax.axis_size("rep")
    pairs = []
    for space in range(spaces):
        for rep in range(reps):
            step = 1 if rep % 2 == 0 else -1
            there, to = space + step, rep
            if not 0 <= there < spaces:
                there, to = space, rep ^ 1
            pairs.append((space * reps + rep, there * reps + to))
    return pairs


def on_device(feats, cotangent, weight, bias, neighbours, occupancy):
    x, cot, near, occ = feats[0], cotangent[0], neighbours[0], occupancy[0]
    bricks, channels, voxels = x.shape
    count, lanes = voxels // PLANE, bricks * PLANE
    width = 9 * channels
    plane = ((channels, lanes), BF)
    core = (lax.axis_index("rep") % 2).astype(jnp.int32)
    cores = core[None]
    first, rows, x, occ, cot, weight, bias = call(
        stage_kernel,
        [
            plane, ((32, lanes), jnp.int32), (x.shape, BF), (occ.shape, jnp.int32), (x.shape, BF),
            (weight.shape, BF), ((1, channels), F32),
        ],
        [
            (SMEM, cores), (HBM, x), (HBM, occ), (HBM, near), (HBM, cot), (HBM, weight),
            (HBM, bias[None]),
        ],
        [pltpu.SMEM(near.shape, jnp.int32), pltpu.SemaphoreType.DMA((6,))],
    )
    axes = ("space", "rep")
    pairs = face_pairs()
    first = lax.ppermute(first, axes, pairs)
    planes, occ2, second = call(
        planes_kernel,
        [((count, channels, lanes), BF), ((count, 8, lanes), F32), plane],
        [(SMEM, cores), (VMEM, x), (VMEM, occ)],
    )
    second = lax.ppermute(second, axes, [(j, i) for i, j in pairs])
    moved, pre, cot2, ahead = call(
        inner_kernel,
        [
            ((count, width, lanes), BF),
            ((count, channels, lanes), F32),
            ((count, channels, lanes), BF),
            ((3 * channels, width), BF),
        ],
        [
            (SMEM, cores), (VMEM, rows), (VMEM, planes), (VMEM, occ), (VMEM, cot), (VMEM, weight),
            (VMEM, bias),
        ],
        [pltpu.VMEM((channels * (count + 2), lanes), F32)],
        flops=2 * 27 * channels * channels * bricks * voxels,
    )
    devices = lax.axis_size("space") * lax.axis_size("rep")
    me = lax.axis_index("space") * lax.axis_size("rep") + lax.axis_index("rep")
    own = (lax.population_count(me.astype(jnp.int32)) & 1)[None]
    size = 3 * channels // 2 * (width // 128) + channels
    field = [(VMEM, moved), (VMEM, pre), (VMEM, cot2), (VMEM, occ2), (VMEM, ahead)]
    result2, begun, moved_first, partial, bias_part = call(
        first_outer_kernel,
        [
            ((count, channels, lanes), BF),
            ((channels * (count + 4), lanes), BF),
            ((width, lanes), BF),
            ((3 * channels // 2, width), F32),
            ((channels, lanes), F32),
        ],
        [(SMEM, cores), (SMEM, own), (VMEM, rows), (VMEM, first)] + field,
        flops=14 * channels * channels * bricks * voxels,
    )
    late, padded, moved_second, theirs, copies = call(
        second_outer_kernel,
        [
            plane,
            ((channels * (count + 4), lanes), BF),
            ((width, lanes), BF),
            ((size + channels * lanes // 128, 128), BF),
            ((channels // 2, channels), F32),
        ],
        [(SMEM, cores), (SMEM, own), (VMEM, rows), (VMEM, second)]
        + field
        + [(VMEM, begun), (VMEM, partial), (VMEM, bias_part)],
        [pltpu.VMEM((5 * channels, lanes), BF)],
        flops=14 * channels * channels * bricks * voxels,
    )
    partner = [(i, i ^ 1) for i in range(devices)]
    other = lax.ppermute(theirs, axes, partner)
    (mine,) = call(
        own_kernel,
        [((size, 128), F32)],
        [
            (SMEM, cores), (SMEM, own), (VMEM, padded), (VMEM, moved), (VMEM, moved_first),
            (VMEM, moved_second), (VMEM, copies),
        ],
        flops=27 * channels * channels * bricks * voxels,
    )
    sent = ((size, 128), BF)
    mine, faces = call(
        first_sum_kernel,
        [sent, ((2 * channels, lanes), BF)],
        [(SMEM, cores), (VMEM, mine), (VMEM, other), (VMEM, padded)],
    )
    bits = [1 << i for i in range(1, (devices).bit_length() - 1)]
    order = bits[1:2] + bits[-1:] + bits[:1] + bits[2:-1]
    rounds = list(zip(order, order[1:] + order[:1]))
    for i, steps in enumerate(rounds):
        joined = [(j, j ^ 1 ^ steps[j.bit_count() % 2]) for j in range(devices)]
        other = lax.ppermute(mine, axes, joined)
        held = []
        if i == 0:
            faces = lax.ppermute(faces, axes, pairs)
            result, total, back = call(
                back_inner_kernel,
                [
                    ((bricks, channels, voxels), BF),
                    ((channels * (count + 2), lanes), F32),
                    ((3 * channels, width), BF),
                ],
                [
                    (SMEM, cores), (VMEM, rows), (VMEM, padded), (VMEM, result2), (VMEM, late),
                    (VMEM, weight), (ANY, mine),
                ],
                [pltpu.VMEM((count, width, lanes), BF)],
                flops=2 * 27 * channels * channels * bricks * voxels,
            )
            held = [total]
        if i == 2:
            first, second = faces[:channels], lax.ppermute(faces[channels:], axes, partner)
            held = [second]
        if i == 3:
            in_grad, done = call(
                back_outer_kernel,
                [((bricks, channels, voxels), BF), ((8, 128), F32)],
                [
                    (SMEM, cores), (VMEM, rows), (VMEM, first), (VMEM, second), (VMEM, total),
                    (VMEM, cot), (VMEM, occ), (VMEM, back), (ANY, mine),
                ],
                flops=2 * 6 * channels * channels * bricks * voxels,
            )
            held = [done]
        last = i == len(rounds) - 1
        (mine,) = call(
            sum_kernel,
            [(sent[0], F32 if last else BF)],
            [(VMEM, mine), (VMEM, other)] + [(ANY, h) for h in held],
        )
    other = lax.ppermute(mine, axes, partner)
    normaliser = 1.0 / math.sqrt(
        feats.shape[0] * lax.axis_size("rep") * bricks * lax.axis_size("space") * voxels
    )
    held = pltpu.VMEM((3, 9, channels // 2, channels), F32)
    outs = [(weight.shape, F32), ((1, channels), F32)]
    weight_grad, bias_grad = call(
        functools.partial(own_half_kernel, normaliser),
        outs,
        [(SMEM, own), (VMEM, mine)],
        [held, pltpu.SemaphoreType.DMA((3,))],
        out_specs=[HBM, VMEM],
    )
    weight_grad, bias_grad = call(
        functools.partial(other_half_kernel, normaliser),
        outs,
        [(SMEM, own), (VMEM, other), (ANY, weight_grad), (VMEM, bias_grad)],
        [held, pltpu.VMEM((1, channels), F32), pltpu.SemaphoreType.DMA((4,))],
        out_specs=[HBM, HBM],
        aliases={2: 0},
    )
    return result[None], in_grad[None], weight_grad, bias_grad[0]


def solution(mesh):
    placed = (
        P("rep", "space", None, None),
        P("rep", "space", None, None),
        P(),
        P(),
        P("rep", "space", None),
        P("rep", "space", None),
    )
    return jax.shard_map(
        on_device,
        mesh=mesh,
        in_specs=placed,
        out_specs=(P("rep", "space", None, None), P("rep", "space", None, None), P(), P()),
        check_vma=False,
    )
```

```python
import functools
import math

import jax
import jax.numpy as jnp
from jax import lax
from jax.experimental import pallas as pl
from jax.experimental.pallas import tpu as pltpu
from jax.sharding import PartitionSpec as P

BF, F32 = jnp.bfloat16, jnp.float32
DIRECTIONS = [
    (a, b, c) for a in (-1, 0, 1) for b in (-1, 0, 1) for c in (-1, 0, 1) if (a, b, c) != (0, 0, 0)
]
PLANE = 64
VMEM = pl.BlockSpec(memory_space=pltpu.VMEM)
ANY = pl.BlockSpec(memory_space=pl.ANY)
HBM = pl.BlockSpec(memory_space=pltpu.HBM)
SMEM = pl.BlockSpec(memory_space=pltpu.SMEM)


def to_planes(tiles):
    low = lax.broadcasted_iota(jnp.int32, tiles[0].shape, 1) < PLANE
    turned = [pltpu.roll(tile, PLANE, 1) for tile in tiles]
    first, second = [], []
    for m in range(0, len(tiles), 2):
        first.append(jnp.where(low, tiles[m], turned[m + 1]))
        second.append(jnp.where(low, turned[m], tiles[m + 1]))
    return jnp.concatenate(first, axis=1), jnp.concatenate(second, axis=1)


def from_planes(first, second):
    low = lax.broadcasted_iota(jnp.int32, (first.shape[0], 128), 1) < PLANE
    tiles = []
    for g in range(first.shape[1] // 128):
        one = first[:, 128 * g : 128 * g + 128]
        two = second[:, 128 * g : 128 * g + 128]
        tiles.append(jnp.where(low, one, pltpu.roll(two, PLANE, 1)))
        tiles.append(jnp.where(low, pltpu.roll(one, PLANE, 1), two))
    return tiles


SHIFTS = [(a, b, c) for a in (-1, 0, 1) for b in (-1, 0, 1) for c in (-1, 0, 1)]


def fill_slot_rows(near_ref, rows_ref, bricks):
    lane = lax.broadcasted_iota(jnp.int32, (1, bricks * PLANE), 1)
    brick = lane // PLANE
    for d, shift in enumerate(SHIFTS):
        if shift == (0, 0, 0):
            rows_ref[d : d + 1, :] = brick * PLANE
            continue
        j = DIRECTIONS.index(shift)
        found = jnp.full(lane.shape, -(1 << 20), jnp.int32)
        for n in range(bricks):
            chosen = near_ref[n, j]
            row = jnp.where(chosen >= 0, lax.rem(chosen, bricks) * PLANE, -(1 << 20))
            found = jnp.where(brick == n, row, found)
        rows_ref[d : d + 1, :] = found


def slot_rows(rows_ref, dx):
    rows = {}
    for d, (a, b, c) in enumerate(SHIFTS):
        if a == dx:
            rows[b, c] = rows_ref[d : d + 1, :]
    return rows


def selection(rows, b, c, bricks):
    size = bricks * PLANE
    lane = lax.broadcasted_iota(jnp.int32, (1, size), 1)
    y = ((lane >> 3) & 7) + (b - 1)
    z = (lane & 7) + (c - 1)
    out_y = (y < 0) | (y > 7)
    out_z = (z < 0) | (z > 7)
    base = rows[0, 0]
    if b != 1:
        base = jnp.where(out_y, rows[b - 1, 0], base)
    if c != 1:
        base = jnp.where(out_z, rows[0, c - 1], base)
    if b != 1 and c != 1:
        base = jnp.where(out_y & out_z, rows[b - 1, c - 1], base)
    source = base + (y & 7) * 8 + (z & 7)
    row = lax.broadcasted_iota(jnp.int32, (size, size), 0)
    return jnp.where(row == source, 1.0, 0.0).astype(BF)


def phase(scalar_ref):
    return pl.when(scalar_ref[0] >= 0)


def dot(x, y):
    return lax.dot_general(x, y, (((1,), (0,)), ((), ())), preferred_element_type=F32)


def dot_t(x, y):
    return lax.dot_general(x, y, (((1,), (1,)), ((), ())), preferred_element_type=F32)


def load_faces(core_ref, first_ref, second_ref):
    upward = core_ref[0] == 0
    first, second = first_ref[...].astype(F32), second_ref[...].astype(F32)
    return jnp.where(upward, first, second).astype(BF), jnp.where(upward, second, first).astype(BF)


def stage_kernel(
    core_ref, feats_ref, occ_ref, near_ref, cot_from_ref, weight_from_ref, bias_from_ref,
    first_ref, rows_ref, x_ref, keep_ref, cot_ref, weight_ref, bias_ref, near_held_ref, sems,
):
    pairs = (
        (near_ref, near_held_ref), (occ_ref, keep_ref), (feats_ref, x_ref), (cot_from_ref, cot_ref),
        (weight_from_ref, weight_ref), (bias_from_ref, bias_ref),
    )
    copies = [pltpu.make_async_copy(a, b, sems.at[i]) for i, (a, b) in enumerate(pairs)]
    for copy in copies:
        copy.start()
    bricks, _, voxels = x_ref.shape
    copies[0].wait()
    fill_slot_rows(near_held_ref, rows_ref, bricks)
    copies[1].wait()
    copies[2].wait()
    keep = keep_ref[...].astype(F32)
    faces = []
    for i, start in enumerate((0, voxels - 128)):
        at = slice(start, start + 128)
        tiles = [x_ref[m, :, at].astype(F32) * keep[m : m + 1, at] for m in range(bricks)]
        faces.append(to_planes(tiles)[i])
    first_ref[...] = jnp.where(core_ref[0] == 0, faces[1], faces[0]).astype(BF)
    for copy in copies[3:]:
        copy.wait()


def planes_kernel(core_ref, feats_ref, occ_ref, planes_ref, occ2_ref, second_ref):
    bricks, channels, voxels = feats_ref.shape
    keep = occ_ref[...].astype(F32)
    for t in range(voxels // 128):
        at = slice(128 * t, 128 * t + 128)
        kept = [jnp.broadcast_to(keep[m : m + 1, at], (channels, 128)) for m in range(bricks)]
        first, second = to_planes([feats_ref[m, :, at].astype(F32) * kept[m] for m in range(bricks)])
        planes_ref[2 * t] = first.astype(BF)
        planes_ref[2 * t + 1] = second.astype(BF)
        first, second = to_planes([kept[m][:8] for m in range(bricks)])
        occ2_ref[2 * t] = first
        occ2_ref[2 * t + 1] = second
    low, high = planes_ref[0].astype(F32), planes_ref[planes_ref.shape[0] - 1].astype(F32)
    second_ref[...] = jnp.where(core_ref[0] == 0, low, high).astype(BF)


def ahead_weights(weight_ref, ahead_ref):
    channels = weight_ref.shape[1]
    for r in range(3):
        blocks = [weight_ref[9 * (2 - r) + k].astype(F32) for k in range(9)]
        ahead_ref[channels * r : channels * (r + 1), :] = jnp.concatenate(blocks, axis=1).astype(BF)


def back_weights(weight_ref, back_ref):
    channels = weight_ref.shape[1]
    for r in range(3):
        blocks = [weight_ref[9 * r + 8 - k].astype(F32).T for k in range(9)]
        back_ref[channels * r : channels * (r + 1), :] = jnp.concatenate(blocks, axis=1).astype(BF)


def shifted(flat, moved_ref, rows_ref, bricks, channels):
    rows = slot_rows(rows_ref, 0)
    count = moved_ref.shape[0]
    for b in range(3):
        for c in range(3):
            k = 3 * b + c
            if k == 4:
                part = flat
            else:
                part = dot(flat, selection(rows, b, c, bricks)).astype(BF)
            moved_ref[:, channels * k : channels * (k + 1), :] = part.reshape(
                count, channels, bricks * PLANE
            )


def add_products(core_ref, weight_ref, moved_ref, total_ref):
    channels = weight_ref.shape[0] // 3

    @phase(core_ref)
    def _():
        for x in range(moved_ref.shape[0]):
            at = slice(channels * x, channels * (x + 3))
            total_ref[at, :] += dot(weight_ref[...], moved_ref[x])


def shifted_face(face, rows, bricks):
    parts = []
    for b in range(3):
        for c in range(3):
            parts.append(dot(face, selection(rows, b, c, bricks)).astype(BF))
    return jnp.concatenate(parts, axis=0)


def side_rows(rows_ref, low):
    below, above = slot_rows(rows_ref, -1), slot_rows(rows_ref, 1)
    return {key: jnp.where(low, below[key], above[key]) for key in below}


def inner_kernel(
    core_ref, rows_ref, planes_ref, occ_ref, cot_ref, weight_ref, bias_ref,
    moved_ref, pre_ref, cot2_ref, ahead_ref, total_ref,
):
    bricks, channels, voxels = cot_ref.shape
    flat = planes_ref[...].reshape(planes_ref.shape[0] * channels, bricks * PLANE)
    shifted(flat, moved_ref, rows_ref, bricks, channels)
    keep = occ_ref[...].astype(F32)
    for t in range(voxels // 128):
        at = slice(128 * t, 128 * t + 128)
        kept = [jnp.broadcast_to(keep[m : m + 1, at], (channels, 128)) for m in range(bricks)]
        first, second = to_planes([cot_ref[m, :, at].astype(F32) * kept[m] for m in range(bricks)])
        cot2_ref[2 * t] = first.astype(BF)
        cot2_ref[2 * t + 1] = second.astype(BF)
    ahead_weights(weight_ref, ahead_ref)
    count = planes_ref.shape[0]
    at = (channels, channels)
    same = lax.broadcasted_iota(jnp.int32, at, 0) == lax.broadcasted_iota(jnp.int32, at, 1)
    column = jnp.sum(jnp.where(same, bias_ref[...], 0.0), axis=1, keepdims=True)
    start = jnp.broadcast_to(column, (channels, bricks * PLANE))
    for x in range(count + 2):
        total_ref[channels * x : channels * (x + 1), :] = start
    add_products(core_ref, ahead_ref, moved_ref, total_ref)
    pre_ref[...] = total_ref[channels : channels * (count + 1), :].reshape(pre_ref.shape)


def terms_of(padded_ref, x, start, half, moved):
    channels = moved.shape[0] // 9
    rows = pl.ds(pl.multiple_of(channels * (x + 1) + start, 32), half)
    return dot_t(padded_ref[rows, :], moved)


def activate(pre, masked, cot, keep):
    sig = jax.nn.sigmoid(pre)
    result = (masked + keep * pre * sig).astype(BF)
    return result, (cot * sig * (1.0 + pre * (1.0 - sig))).astype(BF)


def store_terms(terms, copies_ref, start, out_ref):
    half = terms.shape[0]
    unit = half // 3
    full = terms.shape[1] // 128
    for t in range(full):
        out_ref[half * t : half * (t + 1), :] = terms[:, 128 * t : 128 * t + 128].astype(out_ref.dtype)
    last = terms[:, 128 * full :]
    copies = jnp.where(start == 0, copies_ref[...], 0.0)
    one = jnp.concatenate([last[:unit], last[unit : 2 * unit]], axis=1)
    two = jnp.concatenate([last[2 * unit :], copies], axis=1)
    at = half * full
    out_ref[at : at + unit, :] = one.astype(out_ref.dtype)
    out_ref[at + unit : at + 2 * unit, :] = two.astype(out_ref.dtype)


def first_outer_kernel(
    core_ref, own_ref, rows_ref, face_ref, moved_ref, pre_ref, cot2_ref, occ2_ref, weight_ref,
    result_ref, padded_ref, face_moved_ref, partial_ref, bias_ref,
):
    count, channels, lanes = pre_ref.shape
    bricks = lanes // PLANE
    upward = core_ref[0] == 0
    face_moved_ref[...] = shifted_face(face_ref[...], side_rows(rows_ref, upward), bricks)
    at = pl.multiple_of(jnp.where(upward, 2 * channels, 0), channels)
    add = dot(weight_ref[pl.ds(at, channels), :], face_moved_ref[...])
    padded_ref[0 : 2 * channels, :] = jnp.zeros((2 * channels, lanes), BF)
    padded_ref[channels * (count + 2) :, :] = jnp.zeros((2 * channels, lanes), BF)
    bias = jnp.zeros((channels, lanes), F32)
    for x in range(count):
        pre = pre_ref[x]
        if x in (0, count - 1):
            pre = pre + add
        keep = jnp.broadcast_to(occ2_ref[x][0:1], (channels, lanes))
        masked = moved_ref[x, 4 * channels : 5 * channels, :].astype(F32)
        result, grad = activate(pre, masked, cot2_ref[x].astype(F32), keep)
        if x in (0, count - 1):
            there = upward if x == 0 else jnp.logical_not(upward)
            grad = jnp.where(there, grad.astype(F32), 0.0).astype(BF)
        result_ref[x] = result
        padded_ref[channels * (x + 2) : channels * (x + 3), :] = grad
        bias = bias + grad.astype(F32)
    bias_ref[...] = bias
    half = partial_ref.shape[0]
    start = (1 - own_ref[0]) * half
    terms = terms_of(padded_ref, jnp.where(upward, -1, count), start, half, face_moved_ref[...])
    for x in range(count):
        terms = terms + terms_of(padded_ref, x, start, half, moved_ref[x])
    partial_ref[...] = terms


def second_outer_kernel(
    core_ref, own_ref, rows_ref, face_ref, moved_ref, pre_ref, cot2_ref, occ2_ref, weight_ref,
    begun_ref, partial_ref, bias_ref,
    result_ref, padded_ref, face_moved_ref, theirs_ref, copies_ref,
    late_ref,
):
    count, channels, lanes = pre_ref.shape
    bricks = lanes // PLANE
    upward = core_ref[0] == 0
    plane = jnp.where(upward, count - 1, 0)
    inward = jnp.where(upward, -1, 1)
    face_moved_ref[...] = shifted_face(
        face_ref[...], side_rows(rows_ref, jnp.logical_not(upward)), bricks
    )
    at = pl.multiple_of(jnp.where(upward, 0, 2 * channels), channels)
    add = dot(weight_ref[pl.ds(at, channels), :], face_moved_ref[...])
    keep = jnp.broadcast_to(occ2_ref[plane][0:1], (channels, lanes))
    masked = moved_ref[plane, 4 * channels : 5 * channels, :].astype(F32)
    cot = cot2_ref[plane].astype(F32)
    result, grad = activate(pre_ref[plane] + add, masked, cot, keep)
    result_ref[...] = result
    padded_ref[...] = begun_ref[...]
    padded_ref[pl.ds(pl.multiple_of(channels * (plane + 2), channels), channels), :] = grad
    late_ref[...] = jnp.zeros(late_ref.shape, BF)
    late_ref[2 * channels : 3 * channels, :] = grad
    same = lax.broadcasted_iota(jnp.int32, (channels, channels), 0)
    same = same == lax.broadcasted_iota(jnp.int32, (channels, channels), 1)
    bias = jnp.sum(bias_ref[...] + grad.astype(F32), axis=1, keepdims=True)
    row = jnp.sum(jnp.where(same, bias, 0.0), axis=0, keepdims=True)
    copies_ref[...] = row * spread(copies_ref.shape)
    half = partial_ref.shape[0]
    start = (1 - own_ref[0]) * half
    terms = partial_ref[...] + terms_of(late_ref, -inward, start, half, face_moved_ref[...])
    terms = terms + terms_of(late_ref, 0, start, half, moved_ref[plane])
    terms = terms + terms_of(late_ref, inward, start, half, moved_ref[plane + inward])
    store_terms(terms, copies_ref, start, theirs_ref)
    low = padded_ref[2 * channels : 3 * channels, :].astype(F32)
    high = padded_ref[channels * (count + 1) : channels * (count + 2), :].astype(F32)
    face = jnp.where(upward, low, high).astype(BF)
    size = theirs_ref.shape[0] - channels * (lanes // 128)
    for t in range(lanes // 128):
        theirs_ref[size + channels * t : size + channels * (t + 1), :] = face[:, 128 * t : 128 * t + 128]


def own_kernel(
    core_ref, own_ref, padded_ref, moved_ref, first_ref, second_ref, copies_ref, mine_ref
):
    count = moved_ref.shape[0]
    half = 3 * copies_ref.shape[1] // 2
    start = own_ref[0] * half
    upward = core_ref[0] == 0
    terms = terms_of(padded_ref, jnp.where(upward, -1, count), start, half, first_ref[...])
    for x in range(count):
        terms = terms + terms_of(padded_ref, x, start, half, moved_ref[x])
    terms = terms + terms_of(padded_ref, jnp.where(upward, count, -1), start, half, second_ref[...])
    store_terms(terms, copies_ref, start, mine_ref)


def spread(shape):
    return 1.0 + lax.broadcasted_iota(jnp.int32, shape, 0).astype(F32) * (1.0 / shape[0])


def first_sum_kernel(core_ref, mine_ref, other_ref, padded_ref, out_ref, faces_ref):
    size = mine_ref.shape[0]
    out_ref[...] = (mine_ref[...] + other_ref[0:size, :].astype(F32)).astype(BF)
    channels, lanes = faces_ref.shape[0] // 2, faces_ref.shape[1]
    end = padded_ref.shape[0] - 2 * channels
    upward = core_ref[0] == 0
    low = padded_ref[2 * channels : 3 * channels, :].astype(F32)
    high = padded_ref[end - channels : end, :].astype(F32)
    faces_ref[0:channels, :] = jnp.where(upward, high, low).astype(BF)
    for t in range(lanes // 128):
        rows = slice(size + channels * t, size + channels * (t + 1))
        faces_ref[channels:, 128 * t : 128 * t + 128] = other_ref[rows, :]


def sum_kernel(mine_ref, other_ref, *refs):
    out_ref = refs[-1]
    out_ref[...] = (mine_ref[...].astype(F32) + other_ref[...].astype(F32)).astype(out_ref.dtype)


def back_inner_kernel(
    core_ref, rows_ref, padded_ref, result2_ref, late_ref, weight_ref, after_ref,
    result_ref, total_ref, back_ref, moved_ref,
):
    count, channels, lanes = result2_ref.shape
    bricks = lanes // PLANE
    back_weights(weight_ref, back_ref)
    flat = padded_ref[2 * channels : channels * (count + 2), :]
    shifted(flat, moved_ref, rows_ref, bricks, channels)
    total_ref[...] = jnp.zeros(total_ref.shape, F32)
    add_products(core_ref, back_ref, moved_ref, total_ref)
    upward = core_ref[0] == 0
    late = late_ref[...].astype(F32)
    for t in range(count // 2):
        first, second = result2_ref[2 * t].astype(F32), result2_ref[2 * t + 1].astype(F32)
        if t == 0:
            first = jnp.where(upward, first, late)
        if t == count // 2 - 1:
            second = jnp.where(upward, late, second)
        out = from_planes(first, second)
        for m in range(bricks):
            result_ref[m, :, 128 * t : 128 * t + 128] = out[m].astype(BF)


def back_outer_kernel(
    core_ref, rows_ref, first_ref, second_ref, total_ref, cot_ref, occ_ref, weight_ref, after_ref,
    in_grad_ref, done_ref,
):
    bricks, channels, voxels = cot_ref.shape
    count = voxels // PLANE
    done_ref[...] = jnp.zeros(done_ref.shape, F32)
    low, high = load_faces(core_ref, first_ref, second_ref)
    moved_low = shifted_face(low, slot_rows(rows_ref, -1), bricks)
    moved_high = shifted_face(high, slot_rows(rows_ref, 1), bricks)
    add_low = dot(weight_ref[2 * channels : 3 * channels, :], moved_low)
    add_high = dot(weight_ref[0:channels, :], moved_high)
    keep = occ_ref[...].astype(F32)
    for t in range(count // 2):
        at = slice(128 * t, 128 * t + 128)
        first = total_ref[channels * (2 * t + 1) : channels * (2 * t + 2), :]
        second = total_ref[channels * (2 * t + 2) : channels * (2 * t + 3), :]
        if t == 0:
            first = first + add_low
        if t == count // 2 - 1:
            second = second + add_high
        back = from_planes(first, second)
        for m in range(bricks):
            in_grad_ref[m, :, at] = (
                keep[m : m + 1, at] * (cot_ref[m, :, at].astype(F32) + back[m])
            ).astype(BF)


def arrived_bias(scale, source_ref, channels):
    unit = channels // 2
    rows = source_ref.shape[0]
    tile = pltpu.roll(source_ref[rows - unit : rows, :], 128 - channels, 1)[:, :channels]
    return jnp.sum(tile * (scale / (spread(tile.shape) * unit)), axis=0, keepdims=True)


def store_half(scale, mine, source_ref, weight_ref, held_ref, sems):
    half, unit, channels = 3 * held_ref.shape[3] // 2, held_ref.shape[2], held_ref.shape[3]
    copies = []
    for j in range(3):
        for t in range(4):
            rows = slice(half * t + unit * j, half * t + unit * (j + 1))
            tile = source_ref[rows, :] * scale
            held_ref[j, 2 * t] = tile[:, :channels]
            held_ref[j, 2 * t + 1] = pltpu.roll(tile, 128 - channels, 1)[:, :channels]
        at = 4 * half + unit * (j // 2)
        tile = source_ref[at : at + unit, :] * scale
        if j == 1:
            tile = pltpu.roll(tile, 128 - channels, 1)
        held_ref[j, 8] = tile[:, :channels]
        u = 3 * mine + j
        place = weight_ref.at[
            pl.ds(9 * (2 - u // 2), 9), pl.ds(pl.multiple_of(unit * (u % 2), unit), unit), :
        ]
        copies.append(pltpu.make_async_copy(held_ref.at[j], place, sems.at[j]))
        copies[-1].start()
    return copies


def own_half_kernel(scale, own_ref, source_ref, weight_ref, bias_ref, held_ref, sems):
    copies = store_half(scale, own_ref[0], source_ref, weight_ref, held_ref, sems)
    bias_ref[...] = arrived_bias(scale, source_ref, held_ref.shape[3])
    for copy in copies:
        copy.wait()


def other_half_kernel(
    scale, own_ref, source_ref, begun_ref, own_bias_ref,
    weight_ref, bias_ref, held_ref, bias_held_ref, sems,
):
    bias = arrived_bias(scale, source_ref, held_ref.shape[3])
    bias_held_ref[...] = jnp.where(own_ref[0] == 0, own_bias_ref[...], bias)
    copies = [pltpu.make_async_copy(bias_held_ref, bias_ref, sems.at[3])]
    copies[0].start()
    copies += store_half(scale, 1 - own_ref[0], source_ref, weight_ref, held_ref, sems)
    for copy in copies:
        copy.wait()


def call(body, outs, ins, scratch=(), flops=0, out_specs=None, aliases=None):
    shapes = [jax.ShapeDtypeStruct(shape, dtype) for shape, dtype in outs]
    moved = sum(math.prod(s.shape) * s.dtype.itemsize for s in shapes)
    moved += sum(math.prod(x.shape) * x.dtype.itemsize for _, x in ins)
    return pl.pallas_call(
        body,
        out_shape=shapes,
        in_specs=[spec for spec, _ in ins],
        out_specs=out_specs or [VMEM] * len(shapes),
        input_output_aliases=aliases or {},
        scratch_shapes=list(scratch),
        compiler_params=pltpu.CompilerParams(vmem_limit_bytes=32 << 20),
        cost_estimate=pl.CostEstimate(flops=flops, bytes_accessed=moved, transcendentals=0),
    )(*[pltpu.with_memory_space_constraint(x, pltpu.HBM) if s is HBM else x for s, x in ins])


def face_pairs():
    spaces, reps = lax.axis_size("space"), lax.axis_size("rep")
    pairs = []
    for space in range(spaces):
        for rep in range(reps):
            step = 1 if rep % 2 == 1 else -1
            there, to = space + step, rep
            if not 0 <= there < spaces:
                there, to = space, rep ^ 1
            pairs.append((space * reps + rep, there * reps + to))
    return pairs


def on_device(feats, cotangent, weight, bias, neighbours, occupancy):
    x, cot, near, occ = feats[0], cotangent[0], neighbours[0], occupancy[0]
    bricks, channels, voxels = x.shape
    count, lanes = voxels // PLANE, bricks * PLANE
    width = 9 * channels
    plane = ((channels, lanes), BF)
    core = 1 - (lax.axis_index("rep") % 2).astype(jnp.int32)
    cores = core[None]
    first, rows, x, occ, cot, weight, bias = call(
        stage_kernel,
        [
            plane, ((32, lanes), jnp.int32), (x.shape, BF), (occ.shape, jnp.int32), (x.shape, BF),
            (weight.shape, BF), ((1, channels), F32),
        ],
        [
            (SMEM, cores), (HBM, x), (HBM, occ), (HBM, near), (HBM, cot), (HBM, weight),
            (HBM, bias[None]),
        ],
        [pltpu.SMEM(near.shape, jnp.int32), pltpu.SemaphoreType.DMA((6,))],
    )
    axes = ("space", "rep")
    pairs = face_pairs()
    first = lax.ppermute(first, axes, pairs)
    planes, occ2, second = call(
        planes_kernel,
        [((count, channels, lanes), BF), ((count, 8, lanes), F32), plane],
        [(SMEM, cores), (VMEM, x), (VMEM, occ)],
    )
    second = lax.ppermute(second, axes, [(j, i) for i, j in pairs])
    moved, pre, cot2, ahead = call(
        inner_kernel,
        [
            ((count, width, lanes), BF),
            ((count, channels, lanes), F32),
            ((count, channels, lanes), BF),
            ((3 * channels, width), BF),
        ],
        [
            (SMEM, cores), (VMEM, rows), (VMEM, planes), (VMEM, occ), (VMEM, cot), (VMEM, weight),
            (VMEM, bias),
        ],
        [pltpu.VMEM((channels * (count + 2), lanes), F32)],
        flops=2 * 27 * channels * channels * bricks * voxels,
    )
    devices = lax.axis_size("space") * lax.axis_size("rep")
    me = lax.axis_index("space") * lax.axis_size("rep") + lax.axis_index("rep")
    own = (lax.population_count(me.astype(jnp.int32)) & 1)[None]
    size = 3 * channels // 2 * (width // 128) + channels
    field = [(VMEM, moved), (VMEM, pre), (VMEM, cot2), (VMEM, occ2), (VMEM, ahead)]
    result2, begun, moved_first, partial, bias_part = call(
        first_outer_kernel,
        [
            ((count, channels, lanes), BF),
            ((channels * (count + 4), lanes), BF),
            ((width, lanes), BF),
            ((3 * channels // 2, width), F32),
            ((channels, lanes), F32),
        ],
        [(SMEM, cores), (SMEM, own), (VMEM, rows), (VMEM, first)] + field,
        flops=14 * channels * channels * bricks * voxels,
    )
    late, padded, moved_second, theirs, copies = call(
        second_outer_kernel,
        [
            plane,
            ((channels * (count + 4), lanes), BF),
            ((width, lanes), BF),
            ((size + channels * lanes // 128, 128), BF),
            ((channels // 2, channels), F32),
        ],
        [(SMEM, cores), (SMEM, own), (VMEM, rows), (VMEM, second)]
        + field
        + [(VMEM, begun), (VMEM, partial), (VMEM, bias_part)],
        [pltpu.VMEM((5 * channels, lanes), BF)],
        flops=14 * channels * channels * bricks * voxels,
    )
    partner = [(i, i ^ 1) for i in range(devices)]
    other = lax.ppermute(theirs, axes, partner)
    (mine,) = call(
        own_kernel,
        [((size, 128), F32)],
        [
            (SMEM, cores), (SMEM, own), (VMEM, padded), (VMEM, moved), (VMEM, moved_first),
            (VMEM, moved_second), (VMEM, copies),
        ],
        flops=27 * channels * channels * bricks * voxels,
    )
    sent = ((size, 128), BF)
    mine, faces = call(
        first_sum_kernel,
        [sent, ((2 * channels, lanes), BF)],
        [(SMEM, cores), (VMEM, mine), (VMEM, other), (VMEM, padded)],
    )
    bits = [1 << i for i in range(1, (devices).bit_length() - 1)]
    order = bits[1:2] + bits[-1:] + bits[:1] + bits[2:-1]
    rounds = list(zip(order, order[1:] + order[:1]))
    for i, steps in enumerate(rounds):
        joined = [(j, j ^ 1 ^ steps[j.bit_count() % 2]) for j in range(devices)]
        other = lax.ppermute(mine, axes, joined)
        held = []
        if i == 0:
            faces = lax.ppermute(faces, axes, pairs)
            result, total, back = call(
                back_inner_kernel,
                [
                    ((bricks, channels, voxels), BF),
                    ((channels * (count + 2), lanes), F32),
                    ((3 * channels, width), BF),
                ],
                [
                    (SMEM, cores), (VMEM, rows), (VMEM, padded), (VMEM, result2), (VMEM, late),
                    (VMEM, weight), (ANY, mine),
                ],
                [pltpu.VMEM((count, width, lanes), BF)],
                flops=2 * 27 * channels * channels * bricks * voxels,
            )
            held = [total]
        if i == 2:
            first, second = faces[:channels], lax.ppermute(faces[channels:], axes, partner)
            held = [second]
        if i == 3:
            in_grad, done = call(
                back_outer_kernel,
                [((bricks, channels, voxels), BF), ((8, 128), F32)],
                [
                    (SMEM, cores), (VMEM, rows), (VMEM, first), (VMEM, second), (VMEM, total),
                    (VMEM, cot), (VMEM, occ), (VMEM, back), (ANY, mine),
                ],
                flops=2 * 6 * channels * channels * bricks * voxels,
            )
            held = [done]
        last = i == len(rounds) - 1
        (mine,) = call(
            sum_kernel,
            [(sent[0], F32 if last else BF)],
            [(VMEM, mine), (VMEM, other)] + [(ANY, h) for h in held],
        )
    other = lax.ppermute(mine, axes, partner)
    normaliser = 1.0 / math.sqrt(
        feats.shape[0] * lax.axis_size("rep") * bricks * lax.axis_size("space") * voxels
    )
    held = pltpu.VMEM((3, 9, channels // 2, channels), F32)
    outs = [(weight.shape, F32), ((1, channels), F32)]
    weight_grad, bias_grad = call(
        functools.partial(own_half_kernel, normaliser),
        outs,
        [(SMEM, own), (VMEM, mine)],
        [held, pltpu.SemaphoreType.DMA((3,))],
        out_specs=[HBM, VMEM],
    )
    weight_grad, bias_grad = call(
        functools.partial(other_half_kernel, normaliser),
        outs,
        [(SMEM, own), (VMEM, other), (ANY, weight_grad), (VMEM, bias_grad)],
        [held, pltpu.VMEM((1, channels), F32), pltpu.SemaphoreType.DMA((4,))],
        out_specs=[HBM, HBM],
        aliases={2: 0},
    )
    return result[None], in_grad[None], weight_grad, bias_grad[0]


def solution(mesh):
    placed = (
        P("rep", "space", None, None),
        P("rep", "space", None, None),
        P(),
        P(),
        P("rep", "space", None),
        P("rep", "space", None),
    )
    return jax.shard_map(
        on_device,
        mesh=mesh,
        in_specs=placed,
        out_specs=(P("rep", "space", None, None), P("rep", "space", None, None), P(), P()),
        check_vma=False,
    )
```

```python
import functools
import math

import jax
import jax.numpy as jnp
from jax import lax
from jax.experimental import pallas as pl
from jax.experimental.pallas import tpu as pltpu
from jax.sharding import PartitionSpec as P

BF, F32 = jnp.bfloat16, jnp.float32
DIRECTIONS = [
    (a, b, c) for a in (-1, 0, 1) for b in (-1, 0, 1) for c in (-1, 0, 1) if (a, b, c) != (0, 0, 0)
]
PLANE = 64
VMEM = pl.BlockSpec(memory_space=pltpu.VMEM)
ANY = pl.BlockSpec(memory_space=pl.ANY)
HBM = pl.BlockSpec(memory_space=pltpu.HBM)
SMEM = pl.BlockSpec(memory_space=pltpu.SMEM)


def to_planes(tiles):
    low = lax.broadcasted_iota(jnp.int32, tiles[0].shape, 1) < PLANE
    turned = [pltpu.roll(tile, PLANE, 1) for tile in tiles]
    first, second = [], []
    for m in range(0, len(tiles), 2):
        first.append(jnp.where(low, tiles[m], turned[m + 1]))
        second.append(jnp.where(low, turned[m], tiles[m + 1]))
    return jnp.concatenate(first, axis=1), jnp.concatenate(second, axis=1)


def from_planes(first, second):
    low = lax.broadcasted_iota(jnp.int32, (first.shape[0], 128), 1) < PLANE
    tiles = []
    for g in range(first.shape[1] // 128):
        one = first[:, 128 * g : 128 * g + 128]
        two = second[:, 128 * g : 128 * g + 128]
        tiles.append(jnp.where(low, one, pltpu.roll(two, PLANE, 1)))
        tiles.append(jnp.where(low, pltpu.roll(one, PLANE, 1), two))
    return tiles


SHIFTS = [(a, b, c) for a in (-1, 0, 1) for b in (-1, 0, 1) for c in (-1, 0, 1)]


def fill_slot_rows(near_ref, rows_ref, bricks):
    lane = lax.broadcasted_iota(jnp.int32, (1, bricks * PLANE), 1)
    brick = lane // PLANE
    for d, shift in enumerate(SHIFTS):
        if shift == (0, 0, 0):
            rows_ref[d : d + 1, :] = brick * PLANE
            continue
        j = DIRECTIONS.index(shift)
        found = jnp.full(lane.shape, -(1 << 20), jnp.int32)
        for n in range(bricks):
            chosen = near_ref[n, j]
            row = jnp.where(chosen >= 0, lax.rem(chosen, bricks) * PLANE, -(1 << 20))
            found = jnp.where(brick == n, row, found)
        rows_ref[d : d + 1, :] = found


def slot_rows(rows_ref, dx):
    rows = {}
    for d, (a, b, c) in enumerate(SHIFTS):
        if a == dx:
            rows[b, c] = rows_ref[d : d + 1, :]
    return rows


def selection(rows, b, c, bricks):
    size = bricks * PLANE
    lane = lax.broadcasted_iota(jnp.int32, (1, size), 1)
    y = ((lane >> 3) & 7) + (b - 1)
    z = (lane & 7) + (c - 1)
    out_y = (y < 0) | (y > 7)
    out_z = (z < 0) | (z > 7)
    base = rows[0, 0]
    if b != 1:
        base = jnp.where(out_y, rows[b - 1, 0], base)
    if c != 1:
        base = jnp.where(out_z, rows[0, c - 1], base)
    if b != 1 and c != 1:
        base = jnp.where(out_y & out_z, rows[b - 1, c - 1], base)
    source = base + (y & 7) * 8 + (z & 7)
    row = lax.broadcasted_iota(jnp.int32, (size, size), 0)
    return jnp.where(row == source, 1.0, 0.0).astype(BF)


def phase(scalar_ref):
    return pl.when(scalar_ref[0] >= 0)


def dot(x, y):
    return lax.dot_general(x, y, (((1,), (0,)), ((), ())), preferred_element_type=F32)


def dot_t(x, y):
    return lax.dot_general(x, y, (((1,), (1,)), ((), ())), preferred_element_type=F32)


def load_faces(core_ref, first_ref, second_ref):
    upward = core_ref[0] == 0
    first, second = first_ref[...].astype(F32), second_ref[...].astype(F32)
    return jnp.where(upward, first, second).astype(BF), jnp.where(upward, second, first).astype(BF)


def stage_kernel(
    core_ref, feats_ref, occ_ref, near_ref, cot_from_ref, weight_from_ref, bias_from_ref,
    first_ref, rows_ref, x_ref, keep_ref, cot_ref, weight_ref, bias_ref, near_held_ref, sems,
):
    pairs = (
        (near_ref, near_held_ref), (occ_ref, keep_ref), (feats_ref, x_ref), (cot_from_ref, cot_ref),
        (weight_from_ref, weight_ref), (bias_from_ref, bias_ref),
    )
    copies = [pltpu.make_async_copy(a, b, sems.at[i]) for i, (a, b) in enumerate(pairs)]
    for copy in copies:
        copy.start()
    bricks, _, voxels = x_ref.shape
    copies[0].wait()
    fill_slot_rows(near_held_ref, rows_ref, bricks)
    copies[1].wait()
    copies[2].wait()
    keep = keep_ref[...].astype(F32)
    faces = []
    for i, start in enumerate((0, voxels - 128)):
        at = slice(start, start + 128)
        tiles = [x_ref[m, :, at].astype(F32) * keep[m : m + 1, at] for m in range(bricks)]
        faces.append(to_planes(tiles)[i])
    first_ref[...] = jnp.where(core_ref[0] == 0, faces[1], faces[0]).astype(BF)
    for copy in copies[3:]:
        copy.wait()


def planes_kernel(core_ref, feats_ref, occ_ref, planes_ref, occ2_ref, second_ref):
    bricks, channels, voxels = feats_ref.shape
    keep = occ_ref[...].astype(F32)
    for t in range(voxels // 128):
        at = slice(128 * t, 128 * t + 128)
        kept = [jnp.broadcast_to(keep[m : m + 1, at], (channels, 128)) for m in range(bricks)]
        first, second = to_planes([feats_ref[m, :, at].astype(F32) * kept[m] for m in range(bricks)])
        planes_ref[2 * t] = first.astype(BF)
        planes_ref[2 * t + 1] = second.astype(BF)
        first, second = to_planes([kept[m][:8] for m in range(bricks)])
        occ2_ref[2 * t] = first
        occ2_ref[2 * t + 1] = second
    low, high = planes_ref[0].astype(F32), planes_ref[planes_ref.shape[0] - 1].astype(F32)
    second_ref[...] = jnp.where(core_ref[0] == 0, low, high).astype(BF)


def ahead_weights(weight_ref, ahead_ref):
    channels = weight_ref.shape[1]
    for r in range(3):
        blocks = [weight_ref[9 * (2 - r) + k].astype(F32) for k in range(9)]
        ahead_ref[channels * r : channels * (r + 1), :] = jnp.concatenate(blocks, axis=1).astype(BF)


def back_weights(weight_ref, back_ref):
    channels = weight_ref.shape[1]
    for r in range(3):
        blocks = [weight_ref[9 * r + 8 - k].astype(F32).T for k in range(9)]
        back_ref[channels * r : channels * (r + 1), :] = jnp.concatenate(blocks, axis=1).astype(BF)


def shifted(flat, moved_ref, rows_ref, bricks, channels):
    rows = slot_rows(rows_ref, 0)
    count = moved_ref.shape[0]
    for b in range(3):
        for c in range(3):
            k = 3 * b + c
            if k == 4:
                part = flat
            else:
                part = dot(flat, selection(rows, b, c, bricks)).astype(BF)
            moved_ref[:, channels * k : channels * (k + 1), :] = part.reshape(
                count, channels, bricks * PLANE
            )


def add_products(core_ref, weight_ref, moved_ref, total_ref):
    channels = weight_ref.shape[0] // 3

    @phase(core_ref)
    def _():
        for x in range(moved_ref.shape[0]):
            at = slice(channels * x, channels * (x + 3))
            total_ref[at, :] += dot(weight_ref[...], moved_ref[x])


def shifted_face(face, rows, bricks):
    parts = []
    for b in range(3):
        for c in range(3):
            parts.append(dot(face, selection(rows, b, c, bricks)).astype(BF))
    return jnp.concatenate(parts, axis=0)


def side_rows(rows_ref, low):
    below, above = slot_rows(rows_ref, -1), slot_rows(rows_ref, 1)
    return {key: jnp.where(low, below[key], above[key]) for key in below}


def inner_kernel(
    core_ref, rows_ref, planes_ref, occ_ref, cot_ref, weight_ref, bias_ref,
    moved_ref, pre_ref, cot2_ref, ahead_ref, total_ref,
):
    bricks, channels, voxels = cot_ref.shape
    flat = planes_ref[...].reshape(planes_ref.shape[0] * channels, bricks * PLANE)
    shifted(flat, moved_ref, rows_ref, bricks, channels)
    keep = occ_ref[...].astype(F32)
    for t in range(voxels // 128):
        at = slice(128 * t, 128 * t + 128)
        kept = [jnp.broadcast_to(keep[m : m + 1, at], (channels, 128)) for m in range(bricks)]
        first, second = to_planes([cot_ref[m, :, at].astype(F32) * kept[m] for m in range(bricks)])
        cot2_ref[2 * t] = first.astype(BF)
        cot2_ref[2 * t + 1] = second.astype(BF)
    ahead_weights(weight_ref, ahead_ref)
    count = planes_ref.shape[0]
    at = (channels, channels)
    same = lax.broadcasted_iota(jnp.int32, at, 0) == lax.broadcasted_iota(jnp.int32, at, 1)
    column = jnp.sum(jnp.where(same, bias_ref[...], 0.0), axis=1, keepdims=True)
    start = jnp.broadcast_to(column, (channels, bricks * PLANE))
    for x in range(count + 2):
        total_ref[channels * x : channels * (x + 1), :] = start
    add_products(core_ref, ahead_ref, moved_ref, total_ref)
    pre_ref[...] = total_ref[channels : channels * (count + 1), :].reshape(pre_ref.shape)


def terms_of(padded_ref, x, start, half, moved):
    channels = moved.shape[0] // 9
    rows = pl.ds(pl.multiple_of(channels * (x + 1) + start, 32), half)
    return dot_t(padded_ref[rows, :], moved)


def activate(pre, masked, cot, keep):
    sig = jax.nn.sigmoid(pre)
    result = (masked + keep * pre * sig).astype(BF)
    return result, (cot * sig * (1.0 + pre * (1.0 - sig))).astype(BF)


def store_terms(terms, copies_ref, start, out_ref):
    half = terms.shape[0]
    unit = half // 3
    full = terms.shape[1] // 128
    for t in range(full):
        out_ref[half * t : half * (t + 1), :] = terms[:, 128 * t : 128 * t + 128].astype(out_ref.dtype)
    last = terms[:, 128 * full :]
    copies = jnp.where(start == 0, copies_ref[...], 0.0)
    one = jnp.concatenate([last[:unit], last[unit : 2 * unit]], axis=1)
    two = jnp.concatenate([last[2 * unit :], copies], axis=1)
    at = half * full
    out_ref[at : at + unit, :] = one.astype(out_ref.dtype)
    out_ref[at + unit : at + 2 * unit, :] = two.astype(out_ref.dtype)


def first_outer_kernel(
    core_ref, own_ref, rows_ref, face_ref, moved_ref, pre_ref, cot2_ref, occ2_ref, weight_ref,
    result_ref, padded_ref, face_moved_ref, partial_ref, bias_ref,
):
    count, channels, lanes = pre_ref.shape
    bricks = lanes // PLANE
    upward = core_ref[0] == 0
    face_moved_ref[...] = shifted_face(face_ref[...], side_rows(rows_ref, upward), bricks)
    at = pl.multiple_of(jnp.where(upward, 2 * channels, 0), channels)
    add = dot(weight_ref[pl.ds(at, channels), :], face_moved_ref[...])
    padded_ref[0 : 2 * channels, :] = jnp.zeros((2 * channels, lanes), BF)
    padded_ref[channels * (count + 2) :, :] = jnp.zeros((2 * channels, lanes), BF)
    bias = jnp.zeros((channels, lanes), F32)
    for x in range(count):
        pre = pre_ref[x]
        if x in (0, count - 1):
            pre = pre + add
        keep = jnp.broadcast_to(occ2_ref[x][0:1], (channels, lanes))
        masked = moved_ref[x, 4 * channels : 5 * channels, :].astype(F32)
        result, grad = activate(pre, masked, cot2_ref[x].astype(F32), keep)
        if x in (0, count - 1):
            there = upward if x == 0 else jnp.logical_not(upward)
            grad = jnp.where(there, grad.astype(F32), 0.0).astype(BF)
        result_ref[x] = result
        padded_ref[channels * (x + 2) : channels * (x + 3), :] = grad
        bias = bias + grad.astype(F32)
    bias_ref[...] = bias
    half = partial_ref.shape[0]
    start = (1 - own_ref[0]) * half
    terms = terms_of(padded_ref, jnp.where(upward, -1, count), start, half, face_moved_ref[...])
    for x in range(count):
        terms = terms + terms_of(padded_ref, x, start, half, moved_ref[x])
    partial_ref[...] = terms


def second_outer_kernel(
    core_ref, own_ref, rows_ref, face_ref, moved_ref, pre_ref, cot2_ref, occ2_ref, weight_ref,
    begun_ref, partial_ref, bias_ref,
    result_ref, padded_ref, face_moved_ref, theirs_ref, copies_ref,
    late_ref,
):
    count, channels, lanes = pre_ref.shape
    bricks = lanes // PLANE
    upward = core_ref[0] == 0
    plane = jnp.where(upward, count - 1, 0)
    inward = jnp.where(upward, -1, 1)
    face_moved_ref[...] = shifted_face(
        face_ref[...], side_rows(rows_ref, jnp.logical_not(upward)), bricks
    )
    at = pl.multiple_of(jnp.where(upward, 0, 2 * channels), channels)
    add = dot(weight_ref[pl.ds(at, channels), :], face_moved_ref[...])
    keep = jnp.broadcast_to(occ2_ref[plane][0:1], (channels, lanes))
    masked = moved_ref[plane, 4 * channels : 5 * channels, :].astype(F32)
    cot = cot2_ref[plane].astype(F32)
    result, grad = activate(pre_ref[plane] + add, masked, cot, keep)
    result_ref[...] = result
    padded_ref[...] = begun_ref[...]
    padded_ref[pl.ds(pl.multiple_of(channels * (plane + 2), channels), channels), :] = grad
    late_ref[...] = jnp.zeros(late_ref.shape, BF)
    late_ref[2 * channels : 3 * channels, :] = grad
    same = lax.broadcasted_iota(jnp.int32, (channels, channels), 0)
    same = same == lax.broadcasted_iota(jnp.int32, (channels, channels), 1)
    bias = jnp.sum(bias_ref[...] + grad.astype(F32), axis=1, keepdims=True)
    row = jnp.sum(jnp.where(same, bias, 0.0), axis=0, keepdims=True)
    copies_ref[...] = row * spread(copies_ref.shape)
    half = partial_ref.shape[0]
    start = (1 - own_ref[0]) * half
    terms = partial_ref[...] + terms_of(late_ref, -inward, start, half, face_moved_ref[...])
    terms = terms + terms_of(late_ref, 0, start, half, moved_ref[plane])
    terms = terms + terms_of(late_ref, inward, start, half, moved_ref[plane + inward])
    store_terms(terms, copies_ref, start, theirs_ref)
    low = padded_ref[2 * channels : 3 * channels, :].astype(F32)
    high = padded_ref[channels * (count + 1) : channels * (count + 2), :].astype(F32)
    face = jnp.where(upward, low, high).astype(BF)
    size = theirs_ref.shape[0] - channels * (lanes // 128)
    for t in range(lanes // 128):
        theirs_ref[size + channels * t : size + channels * (t + 1), :] = face[:, 128 * t : 128 * t + 128]


def own_kernel(
    core_ref, own_ref, padded_ref, moved_ref, first_ref, second_ref, copies_ref, mine_ref
):
    count = moved_ref.shape[0]
    half = 3 * copies_ref.shape[1] // 2
    start = own_ref[0] * half
    upward = core_ref[0] == 0
    terms = terms_of(padded_ref, jnp.where(upward, -1, count), start, half, first_ref[...])
    for x in range(count):
        terms = terms + terms_of(padded_ref, x, start, half, moved_ref[x])
    terms = terms + terms_of(padded_ref, jnp.where(upward, count, -1), start, half, second_ref[...])
    store_terms(terms, copies_ref, start, mine_ref)


def spread(shape):
    return 1.0 + lax.broadcasted_iota(jnp.int32, shape, 0).astype(F32) * (1.0 / shape[0])


def first_sum_kernel(core_ref, mine_ref, other_ref, padded_ref, out_ref, faces_ref):
    size = mine_ref.shape[0]
    out_ref[...] = (mine_ref[...] + other_ref[0:size, :].astype(F32)).astype(BF)
    channels, lanes = faces_ref.shape[0] // 2, faces_ref.shape[1]
    end = padded_ref.shape[0] - 2 * channels
    upward = core_ref[0] == 0
    low = padded_ref[2 * channels : 3 * channels, :].astype(F32)
    high = padded_ref[end - channels : end, :].astype(F32)
    faces_ref[0:channels, :] = jnp.where(upward, high, low).astype(BF)
    for t in range(lanes // 128):
        rows = slice(size + channels * t, size + channels * (t + 1))
        faces_ref[channels:, 128 * t : 128 * t + 128] = other_ref[rows, :]


def sum_kernel(mine_ref, other_ref, *refs):
    out_ref = refs[-1]
    out_ref[...] = (mine_ref[...].astype(F32) + other_ref[...].astype(F32)).astype(out_ref.dtype)


def back_inner_kernel(
    core_ref, rows_ref, padded_ref, result2_ref, late_ref, weight_ref, after_ref,
    result_ref, total_ref, back_ref, moved_ref,
):
    count, channels, lanes = result2_ref.shape
    bricks = lanes // PLANE
    back_weights(weight_ref, back_ref)
    flat = padded_ref[2 * channels : channels * (count + 2), :]
    shifted(flat, moved_ref, rows_ref, bricks, channels)
    total_ref[...] = jnp.zeros(total_ref.shape, F32)
    add_products(core_ref, back_ref, moved_ref, total_ref)
    upward = core_ref[0] == 0
    late = late_ref[...].astype(F32)
    for t in range(count // 2):
        first, second = result2_ref[2 * t].astype(F32), result2_ref[2 * t + 1].astype(F32)
        if t == 0:
            first = jnp.where(upward, first, late)
        if t == count // 2 - 1:
            second = jnp.where(upward, late, second)
        out = from_planes(first, second)
        for m in range(bricks):
            result_ref[m, :, 128 * t : 128 * t + 128] = out[m].astype(BF)


def back_outer_kernel(
    core_ref, rows_ref, first_ref, second_ref, total_ref, cot_ref, occ_ref, weight_ref, after_ref,
    in_grad_ref, done_ref,
):
    bricks, channels, voxels = cot_ref.shape
    count = voxels // PLANE
    done_ref[...] = jnp.zeros(done_ref.shape, F32)
    low, high = load_faces(core_ref, first_ref, second_ref)
    moved_low = shifted_face(low, slot_rows(rows_ref, -1), bricks)
    moved_high = shifted_face(high, slot_rows(rows_ref, 1), bricks)
    add_low = dot(weight_ref[2 * channels : 3 * channels, :], moved_low)
    add_high = dot(weight_ref[0:channels, :], moved_high)
    keep = occ_ref[...].astype(F32)
    for t in range(count // 2):
        at = slice(128 * t, 128 * t + 128)
        first = total_ref[channels * (2 * t + 1) : channels * (2 * t + 2), :]
        second = total_ref[channels * (2 * t + 2) : channels * (2 * t + 3), :]
        if t == 0:
            first = first + add_low
        if t == count // 2 - 1:
            second = second + add_high
        back = from_planes(first, second)
        for m in range(bricks):
            in_grad_ref[m, :, at] = (
                keep[m : m + 1, at] * (cot_ref[m, :, at].astype(F32) + back[m])
            ).astype(BF)


def arrived_bias(scale, source_ref, channels):
    unit = channels // 2
    rows = source_ref.shape[0]
    tile = pltpu.roll(source_ref[rows - unit : rows, :], 128 - channels, 1)[:, :channels]
    return jnp.sum(tile * (scale / (spread(tile.shape) * unit)), axis=0, keepdims=True)


def store_half(scale, mine, source_ref, weight_ref, held_ref, sems):
    half, unit, channels = 3 * held_ref.shape[3] // 2, held_ref.shape[2], held_ref.shape[3]
    copies = []
    for j in range(3):
        for t in range(4):
            rows = slice(half * t + unit * j, half * t + unit * (j + 1))
            tile = source_ref[rows, :] * scale
            held_ref[j, 2 * t] = tile[:, :channels]
            held_ref[j, 2 * t + 1] = pltpu.roll(tile, 128 - channels, 1)[:, :channels]
        at = 4 * half + unit * (j // 2)
        tile = source_ref[at : at + unit, :] * scale
        if j == 1:
            tile = pltpu.roll(tile, 128 - channels, 1)
        held_ref[j, 8] = tile[:, :channels]
        u = 3 * mine + j
        place = weight_ref.at[
            pl.ds(9 * (2 - u // 2), 9), pl.ds(pl.multiple_of(unit * (u % 2), unit), unit), :
        ]
        copies.append(pltpu.make_async_copy(held_ref.at[j], place, sems.at[j]))
        copies[-1].start()
    return copies


def own_half_kernel(scale, own_ref, source_ref, weight_ref, bias_ref, held_ref, sems):
    copies = store_half(scale, own_ref[0], source_ref, weight_ref, held_ref, sems)
    bias_ref[...] = arrived_bias(scale, source_ref, held_ref.shape[3])
    for copy in copies:
        copy.wait()


def other_half_kernel(
    scale, own_ref, source_ref, begun_ref, own_bias_ref,
    weight_ref, bias_ref, held_ref, bias_held_ref, sems,
):
    bias = arrived_bias(scale, source_ref, held_ref.shape[3])
    bias_held_ref[...] = jnp.where(own_ref[0] == 0, own_bias_ref[...], bias)
    copies = [pltpu.make_async_copy(bias_held_ref, bias_ref, sems.at[3])]
    copies[0].start()
    copies += store_half(scale, 1 - own_ref[0], source_ref, weight_ref, held_ref, sems)
    for copy in copies:
        copy.wait()


def call(body, outs, ins, scratch=(), flops=0, out_specs=None, aliases=None):
    shapes = [jax.ShapeDtypeStruct(shape, dtype) for shape, dtype in outs]
    moved = sum(math.prod(s.shape) * s.dtype.itemsize for s in shapes)
    moved += sum(math.prod(x.shape) * x.dtype.itemsize for _, x in ins)
    return pl.pallas_call(
        body,
        out_shape=shapes,
        in_specs=[spec for spec, _ in ins],
        out_specs=out_specs or [VMEM] * len(shapes),
        input_output_aliases=aliases or {},
        scratch_shapes=list(scratch),
        compiler_params=pltpu.CompilerParams(vmem_limit_bytes=32 << 20),
        cost_estimate=pl.CostEstimate(flops=flops, bytes_accessed=moved, transcendentals=0),
    )(*[pltpu.with_memory_space_constraint(x, pltpu.HBM) if s is HBM else x for s, x in ins])


def face_pairs():
    spaces, reps = lax.axis_size("space"), lax.axis_size("rep")
    pairs = []
    for space in range(spaces):
        for rep in range(reps):
            step = 1 if rep % 2 == 1 else -1
            there, to = space + step, rep
            if not 0 <= there < spaces:
                there, to = space, rep ^ 1
            pairs.append((space * reps + rep, there * reps + to))
    return pairs


def on_device(feats, cotangent, weight, bias, neighbours, occupancy):
    x, cot, near, occ = feats[0], cotangent[0], neighbours[0], occupancy[0]
    bricks, channels, voxels = x.shape
    count, lanes = voxels // PLANE, bricks * PLANE
    width = 9 * channels
    plane = ((channels, lanes), BF)
    core = 1 - (lax.axis_index("rep") % 2).astype(jnp.int32)
    cores = core[None]
    first, rows, x, occ, cot, weight, bias = call(
        stage_kernel,
        [
            plane, ((32, lanes), jnp.int32), (x.shape, BF), (occ.shape, jnp.int32), (x.shape, BF),
            (weight.shape, BF), ((1, channels), F32),
        ],
        [
            (SMEM, cores), (HBM, x), (HBM, occ), (HBM, near), (HBM, cot), (HBM, weight),
            (HBM, bias[None]),
        ],
        [pltpu.SMEM(near.shape, jnp.int32), pltpu.SemaphoreType.DMA((6,))],
    )
    axes = ("space", "rep")
    pairs = face_pairs()
    first = lax.ppermute(first, axes, pairs)
    planes, occ2, second = call(
        planes_kernel,
        [((count, channels, lanes), BF), ((count, 8, lanes), F32), plane],
        [(SMEM, cores), (VMEM, x), (VMEM, occ)],
    )
    second = lax.ppermute(second, axes, [(j, i) for i, j in pairs])
    moved, pre, cot2, ahead = call(
        inner_kernel,
        [
            ((count, width, lanes), BF),
            ((count, channels, lanes), F32),
            ((count, channels, lanes), BF),
            ((3 * channels, width), BF),
        ],
        [
            (SMEM, cores), (VMEM, rows), (VMEM, planes), (VMEM, occ), (VMEM, cot), (VMEM, weight),
            (VMEM, bias),
        ],
        [pltpu.VMEM((channels * (count + 2), lanes), F32)],
        flops=2 * 27 * channels * channels * bricks * voxels,
    )
    devices = lax.axis_size("space") * lax.axis_size("rep")
    me = lax.axis_index("space") * lax.axis_size("rep") + lax.axis_index("rep")
    own = (lax.population_count(me.astype(jnp.int32)) & 1)[None]
    size = 3 * channels // 2 * (width // 128) + channels
    field = [(VMEM, moved), (VMEM, pre), (VMEM, cot2), (VMEM, occ2), (VMEM, ahead)]
    result2, begun, moved_first, partial, bias_part = call(
        first_outer_kernel,
        [
            ((count, channels, lanes), BF),
            ((channels * (count + 4), lanes), BF),
            ((width, lanes), BF),
            ((3 * channels // 2, width), F32),
            ((channels, lanes), F32),
        ],
        [(SMEM, cores), (SMEM, own), (VMEM, rows), (VMEM, first)] + field,
        flops=14 * channels * channels * bricks * voxels,
    )
    late, padded, moved_second, theirs, copies = call(
        second_outer_kernel,
        [
            plane,
            ((channels * (count + 4), lanes), BF),
            ((width, lanes), BF),
            ((size + channels * lanes // 128, 128), BF),
            ((channels // 2, channels), F32),
        ],
        [(SMEM, cores), (SMEM, own), (VMEM, rows), (VMEM, second)]
        + field
        + [(VMEM, begun), (VMEM, partial), (VMEM, bias_part)],
        [pltpu.VMEM((5 * channels, lanes), BF)],
        flops=14 * channels * channels * bricks * voxels,
    )
    partner = [(i, i ^ 1) for i in range(devices)]
    other = lax.ppermute(theirs, axes, partner)
    (mine,) = call(
        own_kernel,
        [((size, 128), F32)],
        [
            (SMEM, cores), (SMEM, own), (VMEM, padded), (VMEM, moved), (VMEM, moved_first),
            (VMEM, moved_second), (VMEM, copies),
        ],
        flops=27 * channels * channels * bricks * voxels,
    )
    sent = ((size, 128), BF)
    mine, faces = call(
        first_sum_kernel,
        [sent, ((2 * channels, lanes), BF)],
        [(SMEM, cores), (VMEM, mine), (VMEM, other), (VMEM, padded)],
    )
    bits = [1 << i for i in range(1, (devices).bit_length() - 1)]
    order = bits[1:2] + bits[-1:] + bits[:1] + bits[2:-1]
    order = bits[:1] + bits[-1:] + bits[1:-1]
    rounds = list(zip(order, order[1:2] + order[:1] + order[:1:-1]))
    for i, steps in enumerate(rounds):
        joined = [(j, j ^ 1 ^ steps[j.bit_count() % 2]) for j in range(devices)]
        other = lax.ppermute(mine, axes, joined)
        held = []
        if i == 0:
            faces = lax.ppermute(faces, axes, pairs)
            result, total, back = call(
                back_inner_kernel,
                [
                    ((bricks, channels, voxels), BF),
                    ((channels * (count + 2), lanes), F32),
                    ((3 * channels, width), BF),
                ],
                [
                    (SMEM, cores), (VMEM, rows), (VMEM, padded), (VMEM, result2), (VMEM, late),
                    (VMEM, weight), (ANY, mine),
                ],
                [pltpu.VMEM((count, width, lanes), BF)],
                flops=2 * 27 * channels * channels * bricks * voxels,
            )
            held = [total]
        if i == 2:
            first, second = faces[:channels], lax.ppermute(faces[channels:], axes, partner)
            held = [second]
        if i == 3:
            in_grad, done = call(
                back_outer_kernel,
                [((bricks, channels, voxels), BF), ((8, 128), F32)],
                [
                    (SMEM, cores), (VMEM, rows), (VMEM, first), (VMEM, second), (VMEM, total),
                    (VMEM, cot), (VMEM, occ), (VMEM, back), (ANY, mine),
                ],
                flops=2 * 6 * channels * channels * bricks * voxels,
            )
            held = [done]
        last = i == len(rounds) - 1
        (mine,) = call(
            sum_kernel,
            [(sent[0], F32 if last else BF)],
            [(VMEM, mine), (VMEM, other)] + [(ANY, h) for h in held],
        )
    other = lax.ppermute(mine, axes, partner)
    normaliser = 1.0 / math.sqrt(
        feats.shape[0] * lax.axis_size("rep") * bricks * lax.axis_size("space") * voxels
    )
    held = pltpu.VMEM((3, 9, channels // 2, channels), F32)
    outs = [(weight.shape, F32), ((1, channels), F32)]
    weight_grad, bias_grad = call(
        functools.partial(own_half_kernel, normaliser),
        outs,
        [(SMEM, own), (VMEM, mine)],
        [held, pltpu.SemaphoreType.DMA((3,))],
        out_specs=[HBM, VMEM],
    )
    weight_grad, bias_grad = call(
        functools.partial(other_half_kernel, normaliser),
        outs,
        [(SMEM, own), (VMEM, other), (ANY, weight_grad), (VMEM, bias_grad)],
        [held, pltpu.VMEM((1, channels), F32), pltpu.SemaphoreType.DMA((4,))],
        out_specs=[HBM, HBM],
        aliases={2: 0},
    )
    return result[None], in_grad[None], weight_grad, bias_grad[0]


def solution(mesh):
    placed = (
        P("rep", "space", None, None),
        P("rep", "space", None, None),
        P(),
        P(),
        P("rep", "space", None),
        P("rep", "space", None),
    )
    return jax.shard_map(
        on_device,
        mesh=mesh,
        in_specs=placed,
        out_specs=(P("rep", "space", None, None), P("rep", "space", None, None), P(), P()),
        check_vma=False,
    )
```
